512 devices in a mesh: tm: 128 (over y, z, core), head: 4 (over x).
Axes of the slice: x: 4, y: 8, z: 8, core: 2. Of those that a mesh axis runs over, the one named last changes fastest.
Arguments:
- video_keys: bfloat16 [16384, 4096], P('tm', 'head'), may hold values from -6 to 6
- video_values: bfloat16 [16384, 4096], P('tm', 'head'), may hold values from -12 to 12
- text_queries: bfloat16 [8192, 4096], P('tm', 'head'), may hold values from -64 to 64
- text_keys: bfloat16 [8192, 4096], P('tm', 'head'), may hold values from -7 to 7
- text_values: bfloat16 [8192, 4096], P('tm', 'head'), may hold values from -6 to 6
- boundaries: int32 [128], P('tm'), may hold values from 1 to 16384, as said below
- gate_logit: float32 [32], P('head'), may hold values from -3 to 3
- out_weight: bfloat16 [4096, 4096], P('head', 'tm'), may hold values from -0.09375 to 0.09375
Outputs:
- layer_out: bfloat16 [8192, 4096], P('tm', 'head')
The draws below stay inside these ranges and needn't reach their ends.
Inputs may be any that keep to these rules, and one draw needn't show every extreme that they name: `boundaries`: the bound of a block of text rows held by index t of tm lies in t * 128 + 1 to (t + 1) * 128, and the bounds never fall.
All inputs are finite; a program needn't handle non-finite values.
Results may differ from the reference program's by a relative error of at most 0.0052.
Values may be sent and summed in bfloat16 or wider, within the bound.
A program may use at most 192 MiB of HBM per device.

```python
import jax
import jax.numpy as jnp
from jax import lax

D = 4096
H = 32
DH = 128
VID_DEV = 128
TEXT_DEV = 64
GROUP = 64
VIDEO = 16384
TEXT = 8192
N_TM = 128


def shared_text(key):
    return jax.random.truncated_normal(key, -6.0, 6.0, (TEXT, H * DH), jnp.float32)


def video_shared(key):
    first, second = jax.random.split(key)
    level = jax.random.truncated_normal(first, -4.0, 4.0, (VIDEO, H * DH), jnp.float32)
    marked = jax.random.randint(second, (VIDEO, H * DH), 0, 16, jnp.int32) == 0
    return (level, marked)


def draw_video_keys(key, part):
    level, marked = video_shared(key)
    keys = jnp.where(marked, 3.0 + 0.6 * level, -3.0 + 0.6 * level)
    return keys.astype(jnp.bfloat16)


def draw_text_keys(key, part):
    base = shared_text(key)
    keys = base
    return keys.astype(jnp.bfloat16)


def draw_text_queries(key, part):
    key = jax.random.fold_in(key, 23)
    fresh = jax.random.truncated_normal(key, -6.0, 6.0, (TEXT, H * DH), jnp.float32)
    queries = fresh
    return queries.astype(jnp.bfloat16)


def draw_video_values(key, part):
    level, marked = video_shared(key)
    key = jax.random.fold_in(key, 37)
    first, second = jax.random.split(key)
    shards = VIDEO // VID_DEV
    offset = jax.random.uniform(first, (shards, 1, H * DH), jnp.float32, -2.0, 2.0)
    noise = jax.random.truncated_normal(second, -3.0, 3.0, (shards, VID_DEV, H * DH), jnp.float32)
    values = (offset + noise).reshape(VIDEO, H * DH) + 7.0 * marked.astype(jnp.float32)
    return values.astype(jnp.bfloat16)


def draw_boundaries(key, part):
    key = jax.random.fold_in(key, 53)
    blocks = TEXT_DEV // GROUP
    span = VID_DEV // blocks
    count = TEXT // GROUP
    index = jnp.arange(count, dtype=jnp.int32)
    shard_part = index // blocks
    within = index % blocks
    back = jax.random.randint(key, (count,), 0, span, jnp.int32)
    return shard_part * VID_DEV + (within + 1) * span - back


def levels(key, shape, cuts, least, largest):
    level = 1.0
    for dim, shards_of in cuts:
        draws = jax.random.uniform(jax.random.fold_in(jax.random.fold_in(key, 6), dim), (shards_of,), jnp.float32, least / len(cuts), largest / len(cuts))
        level = level * jnp.repeat(jnp.exp(draws), shape[dim] // shards_of).reshape((-1,) + (1,) * (len(shape) - 1 - dim))
    return level


def normal_values(own_key, extent, scale, limit, cuts=(), held_as=jnp.bfloat16):
    level = levels(own_key, extent, cuts, -0.22, 0.18) if cuts else 1.0
    values = jax.random.normal(own_key, extent, jnp.float32) * scale * level
    return jnp.minimum(jnp.maximum(values, -limit), limit).astype(held_as)


def setup_inputs(seed: int = 0) -> dict:
    seeds = jax.random.split(jax.random.key(seed), 9)
    return {
        "video_keys": draw_video_keys(jax.random.fold_in(seeds[8], 71), 0),
        "video_values": draw_video_values(jax.random.fold_in(seeds[8], 71), 0),
        "text_queries": draw_text_queries(jax.random.fold_in(seeds[8], 71), 0),
        "text_keys": draw_text_keys(jax.random.fold_in(seeds[8], 71), 0),
        "text_values": normal_values(seeds[4], (TEXT, H * DH), 1.0, 6.0, ((0, 128), (1, 4))),
        "boundaries": draw_boundaries(jax.random.fold_in(seeds[8], 71), 0),
        "gate_logit": jnp.clip(jax.random.uniform(seeds[6], (H,), jnp.float32, -3.0, 3.0) * levels(seeds[6], (H,), ((0, 4),), -0.4, 0.0), -3.0, 3.0),
        "out_weight": normal_values(seeds[7], (H * DH, D), (H * DH) ** -0.5, 0.09375, ((0, 4), (1, 128))),
    }


def elu_one(values):
    return jnp.where(values > 0, values + 1.0, jnp.exp(jnp.minimum(values, 0.0)))

def reference(video_keys, video_values, text_queries, text_keys, text_values, boundaries, gate_logit, out_weight):
    largest_value = lax.Precision.HIGHEST
    blocks = TEXT_DEV // GROUP
    key_feat = elu_one(video_keys.astype(jnp.float32)).astype(jnp.bfloat16)
    key_feat = key_feat.reshape(N_TM, VID_DEV, H, DH)
    vals = video_values.reshape(N_TM, VID_DEV, H, DH)

    def shard_state(pair):
        keys_f = pair[0].astype(jnp.float32)
        vals_f = pair[1].astype(jnp.float32)
        memory_state = jnp.einsum('jhd,jhe->hde', keys_f, vals_f, precision=largest_value)
        return (memory_state, lax.optimization_barrier(jnp.sum(keys_f, axis=0)))
    states, norms = lax.map(shard_state, (key_feat, vals))
    prior = jnp.concatenate([jnp.zeros((1, H, DH, DH), jnp.float32), jnp.cumsum(states, axis=0)[:-1]], axis=0)
    prior_z = jnp.concatenate([jnp.zeros((1, H, DH), jnp.float32), jnp.cumsum(norms, axis=0)[:-1]], axis=0)
    gate = jax.nn.sigmoid(gate_logit.astype(jnp.float32))[None, :, None]
    queries = text_queries.reshape(N_TM, TEXT_DEV, H, DH)
    keys_t = text_keys.reshape(N_TM, TEXT_DEV, H, DH)
    vals_t = text_values.reshape(N_TM, TEXT_DEV, H, DH)
    bounds = boundaries.reshape(N_TM, blocks)
    shard_ids = jnp.arange(N_TM, dtype=jnp.int32)

    def one_shard(entry_list):
        shard_part, feature_rows, video_value_rows, prior_state, prior_norm, query_rows, key_transposed, value_transposed, limit_value = entry_list
        position = shard_part * VID_DEV + jnp.arange(VID_DEV, dtype=jnp.int32)
        attend_mask = (position[None, :] < limit_value[:, None]).astype(jnp.float32)
        feature_rows_flat = feature_rows.astype(jnp.float32)
        part = jnp.einsum('gp,pvt,pvi->gvti', attend_mask, feature_rows_flat, video_value_rows.astype(jnp.float32), precision=largest_value)
        part_z = jnp.einsum('cj,jhd->chd', attend_mask, feature_rows_flat, precision=largest_value)
        memory_state = prior_state[None] + part
        norm = prior_norm[None] + part_z
        query_feat = lax.optimization_barrier(elu_one(query_rows.astype(jnp.float32)).astype(jnp.bfloat16)).astype(jnp.float32)
        query_feat = query_feat.reshape(blocks, GROUP, H, DH)
        numer = jnp.einsum('crhd,chde->crhe', query_feat, memory_state, precision=largest_value)
        denom = jnp.einsum('crhd,chd->crh', query_feat, norm, precision=largest_value)
        retrieved = (numer / denom[..., None]).reshape(TEXT_DEV, H, DH)
        scores = jnp.einsum('rhd,shd->hrs', query_rows.astype(jnp.float32), key_transposed.astype(jnp.float32)) / jnp.sqrt(jnp.float32(DH))
        rows = jnp.arange(TEXT_DEV, dtype=jnp.int32)
        causal = rows[None, :] <= rows[:, None]
        scores = jnp.where(causal[None], scores, -jnp.inf)
        top = lax.optimization_barrier(jnp.max(scores, axis=-1, keepdims=True))
        expo = jnp.exp(scores - top)
        probs = (expo / lax.optimization_barrier(jnp.sum(expo, axis=-1, keepdims=True))).astype(jnp.bfloat16)
        local_out = jnp.einsum('hrs,shd->rhd', probs.astype(jnp.float32), value_transposed.astype(jnp.float32))
        mixed = gate * retrieved + (1.0 - gate) * local_out
        return mixed.reshape(TEXT_DEV, H * DH).astype(jnp.bfloat16)
    mixed = lax.map(one_shard, (shard_ids, key_feat, vals, prior, prior_z, queries, keys_t, vals_t, bounds))
    mixed = mixed.reshape(TEXT, H * DH)
    return jnp.dot(mixed, out_weight, preferred_element_type=jnp.float32).astype(jnp.bfloat16)
```

```python
import functools

import jax
import jax.numpy as jnp
from jax import lax
from jax.experimental import pallas as pl
from jax.experimental.pallas import tpu as pltpu
from jax.sharding import PartitionSpec as P

MESH = pl.DeviceIdType.MESH
F32 = jnp.float32
BF16 = jnp.bfloat16
NORM_ROWS = 16
NN = (((1,), (0,)), ((), ()))
NT = (((1,), (1,)), ((), ()))
TN = (((0,), (0,)), ((), ()))


def dot(a, b, dims):
    return lax.dot_general(a, b, dims, preferred_element_type=F32)


def elu_one(values):
    return jnp.where(values > 0, values + 1.0, jnp.exp(jnp.minimum(values, 0.0)))


def split(value):
    high = value.astype(BF16)
    return high, (value - high.astype(F32)).astype(BF16)


def kernel(
    ny,
    nz,
    nx,
    bound_ref,
    gate_ref,
    vk_ref,
    vv_ref,
    q_ref,
    tk_ref,
    tv_ref,
    w_ref,
    out_ref,
    w_all,
    kf,
    qf,
    sbuf,
    abuf,
    rbuf,
    tbuf,
    tsend,
    pbuf,
    pfx,
    numer_l,
    denom_l,
    local_o,
    mixed,
    part_send,
    part_own,
    part_recv,
    done_own,
    done_other,
    copy_sem,
    w1_send,
    w1_recv,
    w2_send,
    w2_recv,
    a_send,
    a_recv,
    t_send,
    t_recv,
    p_send,
    p_recv,
    m_send,
    m_recv,
    x_send,
    x_recv,
    d_send,
    d_recv,
):
    tm = lax.axis_index("tm")
    x = lax.axis_index("head")
    c = lax.rem(tm, 2)
    chip = tm // 2
    z = lax.rem(chip, nz)
    y = chip // nz
    row_n = 2 * nz
    m = lax.rem(tm, row_n)
    row0 = y * row_n

    vlen, width = vk_ref.shape
    rows = q_ref.shape[0]
    hdim = 128
    heads = width // hdim
    per_head = row_n // heads
    srows = hdim // per_head
    wc = w_ref.shape[0]
    wh = wc // 2

    def dev(t, xx):
        return {"tm": t, "head": xx}

    def in_row(step):
        return lax.rem(m + step, row_n)

    def y_dev(yy):
        return (yy * nz + z) * 2 + c

    def z_dev(zz):
        return (y * nz + zz) * 2 + c

    barrier = pltpu.get_barrier_semaphore()
    for step in range(1, row_n):
        pl.semaphore_signal(barrier, inc=1, device_id=dev(row0 + in_row(step), x), device_id_type=MESH)
    for step in range(1, ny):
        pl.semaphore_signal(barrier, inc=1, device_id=dev(y_dev(lax.rem(y + step, ny)), x), device_id_type=MESH)
    for step in range(1, nx):
        pl.semaphore_signal(barrier, inc=1, device_id=dev(tm, lax.rem(x + step, nx)), device_id_type=MESH)
    own_w = pltpu.make_async_copy(w_ref, w_all.at[y, z], copy_sem)
    own_w.start()

    feat = elu_one(vk_ref[...].astype(F32)).astype(BF16)
    kf[...] = feat
    norm = dot(jnp.ones((NORM_ROWS, vlen), BF16), kf[...], NN).astype(BF16)
    for h in range(heads):
        cols = slice(h * hdim, (h + 1) * hdim)
        state = dot(kf[:, cols], vv_ref[:, cols], TN).astype(BF16)
        for k in range(per_head):
            sbuf[h * per_head + k, 0:srows] = state[k * srows : (k + 1) * srows]
            sbuf[h * per_head + k, srows : srows + NORM_ROWS] = norm[:, cols]
    abuf[m] = sbuf[m]

    pl.semaphore_wait(barrier, (row_n - 1) + (ny - 1) + (nx - 1))

    for step in range(1, row_n):
        to = in_row(step)
        pltpu.make_async_remote_copy(
            sbuf.at[to], abuf.at[m], a_send, a_recv, device_id=dev(row0 + to, x), device_id_type=MESH
        ).start()

    for step in range(1, nz):
        zz = lax.rem(z + step, nz)
        pltpu.make_async_remote_copy(
            w_ref.at[0:wh], w_all.at[y, z, 0:wh], w1_send.at[0], w1_recv.at[0],
            device_id=dev(z_dev(zz), x), device_id_type=MESH,
        ).start()
    for step in range(1, ny):
        yy = lax.rem(y + step, ny)
        pltpu.make_async_remote_copy(
            w_ref.at[wh:wc], w_all.at[y, z, wh:wc], w1_send.at[1], w1_recv.at[1],
            device_id=dev(y_dev(yy), x), device_id_type=MESH,
        ).start()

    def wait_bytes(ref, sem):
        pltpu.make_async_copy(ref, ref, sem).wait()

    def bundle(half, index, q):
        if half == 0:
            return w_all.at[index, q * (nz // 2) : (q + 1) * (nz // 2), 0:wh]
        return w_all.at[q * (ny // 2) : (q + 1) * (ny // 2), index, wh:wc]

    laps = {}

    def lap_copy(half, way, s, q):
        n, me = (ny, y) if half == 0 else (nz, z)
        block = lax.rem(me + n - s, n) if way == 0 else lax.rem(me + s, n)
        to = lax.rem(me + 1, n) if way == 0 else lax.rem(me + n - 1, n)
        device = y_dev(to) if half == 0 else z_dev(to)
        return pltpu.make_async_remote_copy(
            bundle(half, block, q), bundle(half, block, q),
            w2_send.at[half, way, s, q], w2_recv.at[half, way, s, q],
            device_id=dev(device, x), device_id_type=MESH,
        )

    def lap_keys(s, q):
        keys = []
        for half in range(2):
            n = ny if half == 0 else nz
            for way in range(2):
                if s < n // 2 and (s < n // 2 - 1 or q == way):
                    keys.append((half, way, s, q))
        return keys

    def lap(s):
        for q in range(2):
            for key in lap_keys(s, q):
                if s > 0:
                    half, way, _, _ = key
                    laps[(half, way, s - 1, q)].wait_recv()
                copy = lap_copy(*key)
                copy.start()
                laps[key] = copy

    steps = max(ny, nz) // 2

    qf[...] = elu_one(q_ref[...].astype(F32)).astype(BF16)
    position = tm * vlen + lax.broadcasted_iota(jnp.int32, (rows, vlen), 1)
    seen = position < bound_ref[0]
    causal = lax.broadcasted_iota(jnp.int32, (rows, rows), 1) <= lax.broadcasted_iota(
        jnp.int32, (rows, rows), 0
    )

    def own_part(h):
        cols = slice(h * hdim, (h + 1) * hdim)
        weight = jnp.where(seen, dot(qf[:, cols], kf[:, cols], NT), 0.0)
        high, low = split(weight)
        values = vv_ref[:, cols]
        numer_l[:, cols] = dot(high, values, NN) + dot(low, values, NN)
        denom_l[h] = jnp.broadcast_to(jnp.sum(weight, axis=1, keepdims=True), (rows, hdim))
        scores = dot(q_ref[:, cols], tk_ref[:, cols], NT) * (float(hdim) ** -0.5)
        scores = jnp.where(causal, scores, -jnp.inf)
        expo = jnp.exp(scores - jnp.max(scores, axis=1, keepdims=True))
        probs = (expo / jnp.sum(expo, axis=1, keepdims=True)).astype(BF16)
        local_o[:, cols] = dot(probs, tv_ref[:, cols], NN)

    for h in range(heads // 2):
        own_part(h)

    wait_bytes(abuf.at[0 : row_n - 1], a_recv)
    total = jnp.zeros((srows + NORM_ROWS, hdim), F32)
    for k in range(row_n):
        rbuf[k] = total
        total = total + abuf[k].astype(F32)
    tsend[...] = total.astype(BF16)
    tbuf[y] = tsend[...]
    for step in range(1, ny):
        yy = lax.rem(y + step, ny)
        pltpu.make_async_remote_copy(
            tsend, tbuf.at[y], t_send, t_recv, device_id=dev(y_dev(yy), x), device_id_type=MESH
        ).start()

    own_w.wait()
    wait_bytes(w_all.at[0, 0 : nz - 1, 0:wh], w1_recv.at[0])
    wait_bytes(w_all.at[0 : ny - 1, 0, wh:wc], w1_recv.at[1])
    lap(0)

    wait_bytes(tbuf.at[0 : ny - 1], t_recv)
    base = jnp.zeros((srows + NORM_ROWS, hdim), F32)
    for k in range(ny):
        base = base + jnp.where(k < y, tbuf[k].astype(F32), 0.0)
    for k in range(row_n):
        pbuf[k] = (base + rbuf[k]).astype(BF16)
    pfx[m] = pbuf[m]
    for step in range(1, row_n):
        to = in_row(step)
        pltpu.make_async_remote_copy(
            pbuf.at[to], pfx.at[m], p_send, p_recv, device_id=dev(row0 + to, x), device_id_type=MESH
        ).start()

    for h in range(heads // 2, heads):
        own_part(h)

    if steps > 1:
        lap(1)

    wait_bytes(pfx.at[0 : row_n - 1], p_recv)
    for h in range(heads):
        cols = slice(h * hdim, (h + 1) * hdim)
        query = qf[:, cols]
        numer = numer_l[:, cols]
        for k in range(per_head):
            state = pfx[h * per_head + k, 0:srows]
            numer = numer + dot(query[:, k * srows : (k + 1) * srows], state, NN)
        denom = dot(query, pfx[h * per_head, srows : srows + NORM_ROWS], NT)
        denom = denom[:, 0:1] + denom_l[h]
        gate = 1.0 / (1.0 + jnp.exp(-jnp.full((8, hdim), gate_ref[h], F32)))[0:1]
        mixed[c, :, cols] = (gate * (numer / denom) + (1.0 - gate) * local_o[:, cols]).astype(BF16)

    mix_copy = pltpu.make_async_remote_copy(
        mixed.at[c], mixed.at[c], m_send, m_recv, device_id=dev(tm + 1 - 2 * c, x), device_id_type=MESH
    )
    mix_copy.start()

    for s in range(2, steps):
        lap(s)
    for key in list(laps):
        half, way, s, q = key
        n = ny if half == 0 else nz
        if s == n // 2 - 1 or (s == n // 2 - 2 and q != way):
            laps[key].wait_recv()

    mix_copy.wait_recv()
    both = mixed[...].reshape(2 * rows, width)
    ypx = ny // nx
    pcols = nz * wc

    def partial(xx, yy):
        block = w_all[xx * ypx + yy].reshape(pcols, width)
        return dot(both, block, NT)

    for step in range(1, nx):
        xx = lax.rem(x + step, nx)
        for yy in range(ypx):
            part_send[step - 1, :, yy * pcols : (yy + 1) * pcols] = partial(xx, yy).astype(BF16)
        pltpu.make_async_remote_copy(
            part_send.at[step - 1], part_recv.at[step - 1], x_send.at[step - 1], x_recv.at[step - 1],
            device_id=dev(tm, xx), device_id_type=MESH,
        ).start()
    for yy in range(ypx):
        part_own[:, yy * pcols : (yy + 1) * pcols] = partial(x, yy)

    acc = part_own[...]
    for step in range(1, nx):
        wait_bytes(part_recv.at[step - 1], x_recv.at[step - 1])
        acc = acc + part_recv[step - 1].astype(F32)
    done_own[...] = acc.astype(BF16).reshape(2, rows, ypx * pcols)
    done_copy = pltpu.make_async_remote_copy(
        done_own.at[1 - c], done_other, d_send, d_recv, device_id=dev(tm + 1 - 2 * c, x), device_id_type=MESH
    )
    done_copy.start()

    src = lax.broadcasted_iota(jnp.int32, (hdim, hdim), 0)
    dst = lax.broadcasted_iota(jnp.int32, (hdim, hdim), 1)
    low = lax.rem(dst, 2 * wc)
    place = (dst // (2 * wc)) * wc + lax.rem(low, wc)
    owner = low // wc

    def spread(e, odd):
        hit = jnp.logical_and(src == place + odd * (hdim // 2), owner == e)
        return jnp.where(hit, 1.0, 0.0).astype(BF16)

    nblocks = 2 * ypx * pcols // hdim
    mine = [spread(c, odd) for odd in range(2)]
    theirs = [spread(1 - c, odd) for odd in range(2)]
    done_copy.wait_recv()
    for b in range(nblocks):
        from_cols = slice((b // 2) * hdim, (b // 2 + 1) * hdim)
        value = dot(done_own[c, :, from_cols], mine[b % 2], NN) + dot(done_other[:, from_cols], theirs[b % 2], NN)
        out_ref[:, b * hdim : (b + 1) * hdim] = value.astype(BF16)

    wait_bytes(sbuf.at[0 : row_n - 1], a_send)
    wait_bytes(w_all.at[0, 0 : nz - 1, 0:wh], w1_send.at[0])
    wait_bytes(w_all.at[0 : ny - 1, 0, wh:wc], w1_send.at[1])
    wait_bytes(tbuf.at[0 : ny - 1], t_send)
    wait_bytes(pbuf.at[0 : row_n - 1], p_send)
    for copy in laps.values():
        copy.wait_send()
    mix_copy.wait_send()
    for step in range(1, nx):
        wait_bytes(part_send.at[step - 1], x_send.at[step - 1])
    done_copy.wait_send()


def local(grid, vk, vv, q, tk, tv, bounds, gate, w):
    ny, nz, nx = grid
    vlen, width = vk.shape
    rows = q.shape[0]
    heads = gate.shape[0]
    hdim = width // heads
    row_n = 2 * nz
    srows = heads * hdim // row_n
    wt = w.T
    wc = wt.shape[0]
    pcols = (ny // nx) * nz * wc
    steps = max(ny, nz) // 2
    vmem = pl.BlockSpec(memory_space=pltpu.VMEM)
    smem = pl.BlockSpec(memory_space=pltpu.SMEM)
    dma = pltpu.SemaphoreType.DMA
    slices = (row_n, srows + NORM_ROWS, hdim)
    return pl.pallas_call(
        functools.partial(kernel, ny, nz, nx),
        out_shape=jax.ShapeDtypeStruct((rows, 2 * pcols), BF16),
        in_specs=[smem, smem, vmem, vmem, vmem, vmem, vmem, vmem],
        out_specs=vmem,
        scratch_shapes=[
            pltpu.VMEM((ny, nz, wc, width), BF16),
            pltpu.VMEM((vlen, width), BF16),
            pltpu.VMEM((rows, width), BF16),
            pltpu.VMEM(slices, BF16),
            pltpu.VMEM(slices, BF16),
            pltpu.VMEM(slices, F32),
            pltpu.VMEM((ny, srows + NORM_ROWS, hdim), BF16),
            pltpu.VMEM((srows + NORM_ROWS, hdim), BF16),
            pltpu.VMEM(slices, BF16),
            pltpu.VMEM(slices, BF16),
            pltpu.VMEM((rows, width), F32),
            pltpu.VMEM((heads, rows, hdim), F32),
            pltpu.VMEM((rows, width), F32),
            pltpu.VMEM((2, rows, width), BF16),
            pltpu.VMEM((max(nx - 1, 1), 2 * rows, pcols), BF16),
            pltpu.VMEM((2 * rows, pcols), F32),
            pltpu.VMEM((max(nx - 1, 1), 2 * rows, pcols), BF16),
            pltpu.VMEM((2, rows, pcols), BF16),
            pltpu.VMEM((rows, pcols), BF16),
            dma,
            dma((2,)),
            dma((2,)),
            dma((2, 2, steps, 2)),
            dma((2, 2, steps, 2)),
            dma, dma, dma, dma, dma, dma, dma, dma,
            dma((max(nx - 1, 1),)),
            dma((max(nx - 1, 1),)),
            dma, dma,
        ],
        compiler_params=pltpu.CompilerParams(
            collective_id=0, has_side_effects=True, vmem_limit_bytes=40 * 1024 * 1024
        ),
    )(bounds, gate, vk, vv, q, tk, tv, wt)


def grid_of(mesh):
    nx = mesh.shape["head"]
    return 8, mesh.shape["tm"] // 16, nx


def solution(mesh):
    specs = (
        P("tm", "head"),
        P("tm", "head"),
        P("tm", "head"),
        P("tm", "head"),
        P("tm", "head"),
        P("tm"),
        P("head"),
        P("head", "tm"),
    )
    return jax.shard_map(
        functools.partial(local, grid_of(mesh)),
        mesh=mesh,
        in_specs=specs,
        out_specs=P("tm", "head"),
        check_vma=False,
    )
```

```python
import functools

import jax
import jax.numpy as jnp
from jax import lax
from jax.experimental import pallas as pl
from jax.experimental.pallas import tpu as pltpu
from jax.sharding import PartitionSpec as P

MESH = pl.DeviceIdType.MESH
F32 = jnp.float32
BF16 = jnp.bfloat16
HDIM = 128
NORM_ROWS = 16
NN = (((1,), (0,)), ((), ()))
NT = (((1,), (1,)), ((), ()))
TN = (((0,), (0,)), ((), ()))


def dot(a, b, dims):
    return lax.dot_general(a, b, dims, preferred_element_type=F32)


def elu_one(values):
    return jnp.where(values > 0, values + 1.0, jnp.exp(jnp.minimum(values, 0.0)))


def split(value):
    high = value.astype(BF16)
    return high, (value - high.astype(F32)).astype(BF16)


def wait_bytes(ref, sem):
    pltpu.make_async_copy(ref, ref, sem).wait()


def kernel(
    ny,
    nz,
    nx,
    bound_ref,
    gate_ref,
    vk_ref,
    vv_ref,
    q_ref,
    tk_ref,
    tv_ref,
    w_ref,
    out_ref,
    w_all,
    kin,
    vin,
    qin,
    tkin,
    tvin,
    bin_,
    kf,
    qf,
    sbuf,
    abuf,
    rbuf,
    tbuf,
    tsend,
    pbuf,
    pfx,
    numer_l,
    denom_l,
    local_o,
    mixed,
    part_send,
    part_own,
    part_recv,
    dsend,
    fin,
    in_sem,
    w_sem,
    c_send,
    c_recv,
    w1_send,
    w1_recv,
    w2_send,
    w2_recv,
    a_send,
    a_recv,
    t_send,
    t_recv,
    p_send,
    p_recv,
    m_send,
    m_recv,
    x_send,
    x_recv,
    d_send,
    d_recv,
):
    tm = lax.axis_index("tm")
    x = lax.axis_index("head")
    c = lax.rem(tm, 2)
    chip = tm // 2
    z = lax.rem(chip, nz)
    y = chip // nz

    vlen, width = vk_ref.shape
    rows = q_ref.shape[0]
    half_w = width // 2
    heads = half_w // HDIM
    per_head = nz // heads
    srows = HDIM // per_head
    wc = w_ref.shape[0]
    wh = wc // 2

    def dev(t, xx):
        return {"tm": t, "head": xx}

    def y_dev(yy):
        return dev((yy * nz + z) * 2 + c, x)

    def z_dev(zz):
        return dev((y * nz + zz) * 2 + c, x)

    def x_dev(xx):
        return dev(tm, xx)

    twin = dev(tm + 1 - 2 * c, x)

    def ahead(me, step, n):
        return lax.rem(me + step, n)

    def send(src, dst, send_sem, recv_sem, device):
        copy = pltpu.make_async_remote_copy(
            src, dst, send_sem, recv_sem, device_id=device, device_id_type=MESH
        )
        copy.start()
        return copy

    mine = pl.ds(pl.multiple_of(c * half_w, HDIM), half_w)
    other = pl.ds(pl.multiple_of((1 - c) * half_w, HDIM), half_w)
    inputs = ((vk_ref, kin), (vv_ref, vin), (q_ref, qin), (tk_ref, tkin), (tv_ref, tvin))
    loads = [
        pltpu.make_async_copy(src.at[:, mine], dst.at[c], in_sem.at[i])
        for i, (src, dst) in enumerate(inputs)
    ]
    for load in loads:
        load.start()
    own_w = pltpu.make_async_copy(w_ref, w_all.at[y, z], w_sem)
    own_w.start()

    barrier = pltpu.get_barrier_semaphore()

    def greet(device):
        pl.semaphore_signal(barrier, inc=1, device_id=device, device_id_type=MESH)

    greet(twin)
    for step in range(1, nz):
        greet(z_dev(ahead(z, step, nz)))
    for step in range(1, ny):
        greet(y_dev(ahead(y, step, ny)))
    for step in range(1, nx):
        greet(x_dev(ahead(x, step, nx)))
    bin_[c] = jnp.full((8, HDIM), bound_ref[0], jnp.int32)
    pl.semaphore_wait(barrier, 1 + (nz - 1) + (ny - 1) + (nx - 1))

    swaps = [
        send(src.at[:, other], dst.at[c], c_send.at[i], c_recv.at[i], twin)
        for i, (src, dst) in enumerate(inputs)
    ]
    swaps.append(send(bin_.at[c], bin_.at[c], c_send.at[5], c_recv.at[5], twin))

    for step in range(1, nz):
        send(w_ref.at[0:wh], w_all.at[y, z, 0:wh], w1_send.at[0], w1_recv.at[0], z_dev(ahead(z, step, nz)))
    for step in range(1, ny):
        send(w_ref.at[wh:wc], w_all.at[y, z, wh:wc], w1_send.at[1], w1_recv.at[1], y_dev(ahead(y, step, ny)))

    loads[0].wait()
    kf[c] = elu_one(kin[c].astype(F32)).astype(BF16)
    loads[1].wait()
    swaps[0].wait_recv()
    kf[1 - c] = elu_one(kin[1 - c].astype(F32)).astype(BF16)
    swaps[1].wait_recv()
    ones = jnp.ones((NORM_ROWS, 2 * vlen), BF16)
    for h in range(heads):
        cols = slice(h * HDIM, (h + 1) * HDIM)
        feat = kf[:, :, cols].reshape(2 * vlen, HDIM)
        state = dot(feat, vin[:, :, cols].reshape(2 * vlen, HDIM), TN).astype(BF16)
        norm = dot(ones, feat, NN).astype(BF16)
        for k in range(per_head):
            sbuf[h * per_head + k, 0:srows] = state[k * srows : (k + 1) * srows]
            sbuf[h * per_head + k, srows : srows + NORM_ROWS] = norm
    abuf[z] = sbuf[z]
    for step in range(1, nz):
        to = ahead(z, step, nz)
        send(sbuf.at[to], abuf.at[z], a_send, a_recv, z_dev(to))

    def bundle(half, index, q):
        if half == 0:
            return w_all.at[index, q * (nz // 2) : (q + 1) * (nz // 2), 0:wh]
        return w_all.at[q * (ny // 2) : (q + 1) * (ny // 2), index, wh:wc]

    laps = {}
    waited = set()

    def lap_len(half):
        return (ny if half == 0 else nz) // 2

    def arrived(key):
        if key in laps and key not in waited:
            waited.add(key)
            laps[key].wait_recv()

    def lap(s, q):
        for half in range(2):
            for way in range(2):
                n, me = (ny, y) if half == 0 else (nz, z)
                if s >= n // 2 or (s == n // 2 - 1 and q != way):
                    continue
                arrived((half, way, s - 1, q))
                block = ahead(me, n - s, n) if way == 0 else ahead(me, s, n)
                to = ahead(me, 1, n) if way == 0 else ahead(me, n - 1, n)
                part = bundle(half, block, q)
                laps[(half, way, s, q)] = send(
                    part, part, w2_send.at[half, way, s, q], w2_recv.at[half, way, s, q],
                    y_dev(to) if half == 0 else z_dev(to),
                )

    for i in range(2, 5):
        loads[i].wait()
        swaps[i].wait_recv()
    swaps[5].wait_recv()
    bounds = jnp.concatenate(
        [jnp.broadcast_to(bin_[0, 0:1, :], (rows, HDIM)), jnp.broadcast_to(bin_[1, 0:1, :], (rows, HDIM))]
    )
    row_ids = lax.broadcasted_iota(jnp.int32, (2 * rows, HDIM), 0)
    col_ids = lax.broadcasted_iota(jnp.int32, (2 * rows, HDIM), 1)

    def own_part(h):
        cols = slice(h * HDIM, (h + 1) * HDIM)
        query = qin[:, :, cols].reshape(2 * rows, HDIM)
        q_feat = elu_one(query.astype(F32)).astype(BF16)
        qf[h] = q_feat
        numer = jnp.zeros((2 * rows, HDIM), F32)
        denom = jnp.zeros((2 * rows, 1), F32)
        for e in range(2):
            weight = dot(q_feat, kf[e, :, cols], NT)
            weight = jnp.where(col_ids + (chip * 2 + e) * vlen < bounds, weight, 0.0)
            high, low = split(weight)
            values = vin[e, :, cols]
            numer = numer + dot(high, values, NN) + dot(low, values, NN)
            denom = denom + jnp.sum(weight, axis=1, keepdims=True)
        numer_l[h] = numer
        denom_l[h] = jnp.broadcast_to(denom, (2 * rows, HDIM))
        scores = dot(query, tkin[:, :, cols].reshape(2 * rows, HDIM), NT) * (float(HDIM) ** -0.5)
        causal = jnp.logical_and(col_ids <= row_ids, col_ids // rows == row_ids // rows)
        scores = jnp.where(causal, scores, -jnp.inf)
        expo = jnp.exp(scores - jnp.max(scores, axis=1, keepdims=True))
        probs = (expo / jnp.sum(expo, axis=1, keepdims=True)).astype(BF16)
        local_o[h] = dot(probs, tvin[:, :, cols].reshape(2 * rows, HDIM), NN)

    for h in range(heads // 2):
        own_part(h)

    own_w.wait()
    wait_bytes(w_all.at[0, 0 : nz - 1, 0:wh], w1_recv.at[0])
    wait_bytes(w_all.at[0 : ny - 1, 0, wh:wc], w1_recv.at[1])
    lap(0, 0)
    lap(0, 1)

    for h in range(heads // 2, heads):
        own_part(h)

    wait_bytes(abuf.at[0 : nz - 1], a_recv)
    total = jnp.zeros((srows + NORM_ROWS, HDIM), F32)
    for k in range(nz):
        rbuf[k] = total
        total = total + abuf[k].astype(F32)
    tsend[...] = total.astype(BF16)
    tbuf[y] = tsend[...]
    for step in range(1, ny):
        send(tsend, tbuf.at[y], t_send, t_recv, y_dev(ahead(y, step, ny)))

    lap(1, 0)

    wait_bytes(tbuf.at[0 : ny - 1], t_recv)
    base = jnp.zeros((srows + NORM_ROWS, HDIM), F32)
    for k in range(ny):
        base = base + jnp.where(k < y, tbuf[k].astype(F32), 0.0)
    for k in range(nz):
        pbuf[k] = (base + rbuf[k]).astype(BF16)
    pfx[z] = pbuf[z]
    for step in range(1, nz):
        to = ahead(z, step, nz)
        send(pbuf.at[to], pfx.at[z], p_send, p_recv, z_dev(to))

    lap(1, 1)
    lap(2, 0)

    wait_bytes(pfx.at[0 : nz - 1], p_recv)
    for h in range(heads):
        query = qf[h]
        first = h * per_head
        state = pfx[first : first + per_head, 0:srows].reshape(HDIM, HDIM)
        numer = numer_l[h] + dot(query, state, NN)
        denom = dot(query, pfx[first, srows : srows + NORM_ROWS], NT)[:, 0:1] + denom_l[h]
        gate = 1.0 / (1.0 + jnp.exp(-jnp.full((8, HDIM), gate_ref[c * heads + h], F32)))[0:1]
        mixed[c * heads + h] = (gate * (numer / denom) + (1.0 - gate) * local_o[h]).astype(BF16)
    own_mix = mixed.at[pl.ds(c * heads, heads)]
    mix_copy = send(own_mix, own_mix, m_send, m_recv, twin)

    lap(2, 1)
    lap(3, 0)
    lap(3, 1)

    ypx = ny // nx
    pcols = ypx * nz * wh
    mix_copy.wait_recv()

    def partial(xx, half):
        both = jnp.concatenate([mixed[h] for h in range(2 * heads)], axis=1)
        block = w_all[pl.ds(xx * ypx, ypx), :, half * wh : (half + 1) * wh]
        return dot(both, block.reshape(pcols, width), NT)

    def project(xx, half):
        value = partial(xx, half)
        slot = lax.rem(x - xx + nx, nx)

        @pl.when(slot == 0)
        def _():
            part_own[half] = value

        if nx > 1:

            @pl.when(slot > 0)
            def _():
                part_send[slot - 1, half] = value.astype(BF16)
                send(
                    part_send.at[slot - 1, half], part_recv.at[slot - 1, half],
                    x_send.at[slot - 1, half], x_recv.at[slot - 1, half], x_dev(xx),
                )

    group = y // ypx
    order = [0] + [r for k in range(1, nx // 2) for r in (k, nx - k)] + ([nx // 2] if nx > 1 else [])
    for key in list(laps):
        if key[0] == 0 and key[2] < lap_len(0) - 1:
            arrived(key)
    for r in order[:-1]:
        project(ahead(group, r, nx), 0)
    for key in list(laps):
        if key[0] == 0:
            arrived(key)
    project(ahead(group, order[-1], nx), 0)
    for key in list(laps):
        arrived(key)
    for step in list(range(1, nx)) + [0]:
        project(ahead(x, step, nx), 1)

    for half in range(2):
        acc = part_own[half]
        for s in range(nx - 1):
            wait_bytes(part_recv.at[s, half], x_recv.at[s, half])
            acc = acc + part_recv[s, half].astype(F32)
        acc = acc.astype(BF16)
        dsend[0, half] = acc[0:rows]
        dsend[1, half] = acc[rows : 2 * rows]
    done_copy = send(dsend.at[1 - c], fin.at[c], d_send, d_recv, twin)
    fin[c] = dsend[c]
    done_copy.wait_recv()

    lane = lax.broadcasted_iota(jnp.int32, (rows, HDIM), 1)
    runs = HDIM // wh
    for b in range(4 * pcols // HDIM):
        value = jnp.zeros((rows, HDIM), F32)
        for k in range(runs):
            run = b * runs + k
            e, half, pos = (run // 2) % 2, run % 2, (run // 4) * wh
            piece = fin[e, half, :, pos // HDIM * HDIM : (pos // HDIM + 1) * HDIM].astype(F32)
            shift = (k * wh - pos) % HDIM
            if shift:
                piece = pltpu.roll(piece, shift, 1)
            value = jnp.where(lane // wh == k, piece, value)
        out_ref[:, b * HDIM : (b + 1) * HDIM] = value.astype(BF16)

    for copy in swaps:
        copy.wait_send()
    wait_bytes(w_all.at[0, 0 : nz - 1, 0:wh], w1_send.at[0])
    wait_bytes(w_all.at[0 : ny - 1, 0, wh:wc], w1_send.at[1])
    wait_bytes(sbuf.at[0 : nz - 1], a_send)
    wait_bytes(tbuf.at[0 : ny - 1], t_send)
    wait_bytes(pbuf.at[0 : nz - 1], p_send)
    for copy in laps.values():
        copy.wait_send()
    mix_copy.wait_send()
    for s in range(nx - 1):
        for half in range(2):
            wait_bytes(part_send.at[s, half], x_send.at[s, half])
    done_copy.wait_send()


def local(grid, vk, vv, q, tk, tv, bounds, gate, w):
    ny, nz, nx = grid
    vlen, width = vk.shape
    rows = q.shape[0]
    half_w = width // 2
    heads = half_w // HDIM
    srows = half_w // nz
    wt = w.T
    wc = wt.shape[0]
    pcols = (ny // nx) * nz * wc // 2
    steps = max(ny, nz) // 2
    peers = max(nx - 1, 1)
    hbm = pl.BlockSpec(memory_space=pltpu.HBM)
    smem = pl.BlockSpec(memory_space=pltpu.SMEM)
    dma = pltpu.SemaphoreType.DMA
    slices = (nz, srows + NORM_ROWS, HDIM)
    per_head = (heads, 2 * rows, HDIM)
    return pl.pallas_call(
        functools.partial(kernel, ny, nz, nx),
        out_shape=jax.ShapeDtypeStruct((rows, 4 * pcols), BF16),
        in_specs=[smem, smem] + [hbm] * 6,
        out_specs=pl.BlockSpec(memory_space=pltpu.VMEM),
        scratch_shapes=[
            pltpu.VMEM((ny, nz, wc, width), BF16),
            pltpu.VMEM((2, vlen, half_w), BF16),
            pltpu.VMEM((2, vlen, half_w), BF16),
            pltpu.VMEM((2, rows, half_w), BF16),
            pltpu.VMEM((2, rows, half_w), BF16),
            pltpu.VMEM((2, rows, half_w), BF16),
            pltpu.VMEM((2, 8, HDIM), jnp.int32),
            pltpu.VMEM((2, vlen, half_w), BF16),
            pltpu.VMEM(per_head, BF16),
            pltpu.VMEM(slices, BF16),
            pltpu.VMEM(slices, BF16),
            pltpu.VMEM(slices, F32),
            pltpu.VMEM((ny, srows + NORM_ROWS, HDIM), BF16),
            pltpu.VMEM((srows + NORM_ROWS, HDIM), BF16),
            pltpu.VMEM(slices, BF16),
            pltpu.VMEM(slices, BF16),
            pltpu.VMEM(per_head, F32),
            pltpu.VMEM(per_head, F32),
            pltpu.VMEM(per_head, F32),
            pltpu.VMEM((2 * heads, 2 * rows, HDIM), BF16),
            pltpu.VMEM((peers, 2, 2 * rows, pcols), BF16),
            pltpu.VMEM((2, 2 * rows, pcols), F32),
            pltpu.VMEM((peers, 2, 2 * rows, pcols), BF16),
            pltpu.VMEM((2, 2, rows, pcols), BF16),
            pltpu.VMEM((2, 2, rows, pcols), BF16),
            dma((5,)),
            dma,
            dma((6,)),
            dma((6,)),
            dma((2,)),
            dma((2,)),
            dma((2, 2, steps, 2)),
            dma((2, 2, steps, 2)),
            dma, dma, dma, dma, dma, dma, dma, dma,
            dma((peers, 2)),
            dma((peers, 2)),
            dma, dma,
        ],
        compiler_params=pltpu.CompilerParams(
            collective_id=0, has_side_effects=True, vmem_limit_bytes=60 * 1024 * 1024
        ),
    )(bounds, gate, vk, vv, q, tk, tv, wt)


def solution(mesh):
    nx = mesh.shape["head"]
    specs = (
        P("tm", "head"),
        P("tm", "head"),
        P("tm", "head"),
        P("tm", "head"),
        P("tm", "head"),
        P("tm"),
        P("head"),
        P("head", "tm"),
    )
    return jax.shard_map(
        functools.partial(local, (8, mesh.shape["tm"] // 16, nx)),
        mesh=mesh,
        in_specs=specs,
        out_specs=P("tm", "head"),
        check_vma=False,
    )
```

```python
import functools

import jax
import jax.numpy as jnp
from jax import lax
from jax.experimental import pallas as pl
from jax.experimental.pallas import tpu as pltpu
from jax.sharding import PartitionSpec as P

MESH = pl.DeviceIdType.MESH
F32 = jnp.float32
BF16 = jnp.bfloat16
HDIM = 128
NORM_ROWS = 16
NN = (((1,), (0,)), ((), ()))
NT = (((1,), (1,)), ((), ()))
TN = (((0,), (0,)), ((), ()))


def dot(a, b, dims):
    return lax.dot_general(a, b, dims, preferred_element_type=F32)


def elu_one(values):
    return jnp.where(values > 0, values + 1.0, jnp.exp(jnp.minimum(values, 0.0)))


def split(value):
    high = value.astype(BF16)
    return high, (value - high.astype(F32)).astype(BF16)


def wait_bytes(ref, sem):
    pltpu.make_async_copy(ref, ref, sem).wait()


def kernel(
    ny,
    nz,
    nx,
    bound_ref,
    gate_ref,
    vk_ref,
    vv_ref,
    q_ref,
    tk_ref,
    tv_ref,
    w_ref,
    out_ref,
    w_all,
    kin,
    vin,
    qin,
    tkin,
    tvin,
    bin_,
    kf,
    qf,
    sbuf,
    abuf,
    rbuf,
    tbuf,
    tsend,
    pbuf,
    pfx,
    numer_l,
    denom_l,
    local_o,
    mixed,
    part_send,
    part_own,
    part_recv,
    dsend,
    fin,
    in_sem,
    w_sem,
    c_send,
    c_recv,
    w1_send,
    w1_recv,
    w2_send,
    w2_recv,
    a_send,
    a_recv,
    t_send,
    t_recv,
    p_send,
    p_recv,
    m_send,
    m_recv,
    x_send,
    x_recv,
    d_send,
    d_recv,
):
    tm = lax.axis_index("tm")
    x = lax.axis_index("head")
    c = lax.rem(tm, 2)
    chip = tm // 2
    z = lax.rem(chip, nz)
    y = chip // nz

    vlen, width = vk_ref.shape
    rows = q_ref.shape[0]
    half_w = width // 2
    heads = half_w // HDIM
    per_head = nz // heads
    srows = HDIM // per_head
    wc = w_ref.shape[0]
    wh = wc // 2

    def dev(t, xx):
        return {"tm": t, "head": xx}

    def y_dev(yy):
        return dev((yy * nz + z) * 2 + c, x)

    def z_dev(zz):
        return dev((y * nz + zz) * 2 + c, x)

    def x_dev(xx):
        return dev(tm, xx)

    twin = dev(tm + 1 - 2 * c, x)

    def ahead(me, step, n):
        return lax.rem(me + step, n)

    def send(src, dst, send_sem, recv_sem, device):
        copy = pltpu.make_async_remote_copy(
            src, dst, send_sem, recv_sem, device_id=device, device_id_type=MESH
        )
        copy.start()
        return copy

    mine = pl.ds(pl.multiple_of(c * half_w, HDIM), half_w)
    other = pl.ds(pl.multiple_of((1 - c) * half_w, HDIM), half_w)
    inputs = ((vk_ref, kin), (vv_ref, vin), (q_ref, qin), (tk_ref, tkin), (tv_ref, tvin))
    loads = [
        pltpu.make_async_copy(src.at[:, mine], dst.at[c], in_sem.at[i])
        for i, (src, dst) in enumerate(inputs)
    ]
    for load in loads:
        load.start()
    own_w = pltpu.make_async_copy(w_ref, w_all.at[y, z], w_sem)
    own_w.start()

    barrier = pltpu.get_barrier_semaphore()

    def greet(device):
        pl.semaphore_signal(barrier, inc=1, device_id=device, device_id_type=MESH)

    greet(twin)
    for step in range(1, nz):
        greet(z_dev(ahead(z, step, nz)))
    for step in range(1, ny):
        greet(y_dev(ahead(y, step, ny)))
    for step in range(1, nx):
        greet(x_dev(ahead(x, step, nx)))
    bin_[c] = jnp.full((8, HDIM), bound_ref[0], jnp.int32)
    loads[0].wait()
    kf[c] = elu_one(kin[c].astype(F32)).astype(BF16)
    pl.semaphore_wait(barrier, 1 + (nz - 1) + (ny - 1) + (nx - 1))

    swaps = [
        send(src.at[:, other], dst.at[c], c_send.at[i], c_recv.at[i], twin)
        for i, (src, dst) in enumerate(inputs)
    ]
    swaps.append(send(bin_.at[c], bin_.at[c], c_send.at[5], c_recv.at[5], twin))

    for step in range(1, nz):
        send(w_ref.at[0:wh], w_all.at[y, z, 0:wh], w1_send.at[0], w1_recv.at[0], z_dev(ahead(z, step, nz)))
    for step in range(1, ny):
        send(w_ref.at[wh:wc], w_all.at[y, z, wh:wc], w1_send.at[1], w1_recv.at[1], y_dev(ahead(y, step, ny)))

    loads[1].wait()
    swaps[0].wait_recv()
    kf[1 - c] = elu_one(kin[1 - c].astype(F32)).astype(BF16)
    swaps[1].wait_recv()
    ones = jnp.ones((NORM_ROWS, 2 * vlen), BF16)
    for h in range(heads):
        cols = slice(h * HDIM, (h + 1) * HDIM)
        feat = kf[:, :, cols].reshape(2 * vlen, HDIM)
        state = dot(feat, vin[:, :, cols].reshape(2 * vlen, HDIM), TN).astype(BF16)
        norm = dot(ones, feat, NN).astype(BF16)
        for k in range(per_head):
            sbuf[h * per_head + k, 0:srows] = state[k * srows : (k + 1) * srows]
            sbuf[h * per_head + k, srows : srows + NORM_ROWS] = norm
    abuf[z] = sbuf[z]
    for step in range(1, nz):
        to = ahead(z, step, nz)
        send(sbuf.at[to], abuf.at[z], a_send, a_recv, z_dev(to))

    def bundle(half, index, q):
        if half == 0:
            return w_all.at[index, q * (nz // 2) : (q + 1) * (nz // 2), 0:wh]
        return w_all.at[q * (ny // 2) : (q + 1) * (ny // 2), index, wh:wc]

    laps = {}
    waited = set()

    def lap_len(half):
        return (ny if half == 0 else nz) // 2

    def arrived(key):
        if key in laps and key not in waited:
            waited.add(key)
            laps[key].wait_recv()

    def lap(s, q):
        for half in range(2):
            for way in range(2):
                n, me = (ny, y) if half == 0 else (nz, z)
                if s >= n // 2 or (s == n // 2 - 1 and q != way):
                    continue
                arrived((half, way, s - 1, q))
                block = ahead(me, n - s, n) if way == 0 else ahead(me, s, n)
                to = ahead(me, 1, n) if way == 0 else ahead(me, n - 1, n)
                part = bundle(half, block, q)
                laps[(half, way, s, q)] = send(
                    part, part, w2_send.at[half, way, s, q], w2_recv.at[half, way, s, q],
                    y_dev(to) if half == 0 else z_dev(to),
                )

    for i in range(2, 5):
        loads[i].wait()
        swaps[i].wait_recv()
    swaps[5].wait_recv()
    bounds = jnp.concatenate(
        [jnp.broadcast_to(bin_[0, 0:1, :], (rows, HDIM)), jnp.broadcast_to(bin_[1, 0:1, :], (rows, HDIM))]
    )
    row_ids = lax.broadcasted_iota(jnp.int32, (2 * rows, HDIM), 0)
    col_ids = lax.broadcasted_iota(jnp.int32, (2 * rows, HDIM), 1)

    def own_part(h):
        cols = slice(h * HDIM, (h + 1) * HDIM)
        query = qin[:, :, cols].reshape(2 * rows, HDIM)
        q_feat = elu_one(query.astype(F32)).astype(BF16)
        qf[h] = q_feat
        numer = jnp.zeros((2 * rows, HDIM), F32)
        denom = jnp.zeros((2 * rows, 1), F32)
        for e in range(2):
            weight = dot(q_feat, kf[e, :, cols], NT)
            weight = jnp.where(col_ids + (chip * 2 + e) * vlen < bounds, weight, 0.0)
            high, low = split(weight)
            values = vin[e, :, cols]
            numer = numer + dot(high, values, NN) + dot(low, values, NN)
            denom = denom + jnp.sum(weight, axis=1, keepdims=True)
        numer_l[h] = numer
        denom_l[h] = jnp.broadcast_to(denom, (2 * rows, HDIM))
        scores = dot(query, tkin[:, :, cols].reshape(2 * rows, HDIM), NT) * (float(HDIM) ** -0.5)
        causal = jnp.logical_and(col_ids <= row_ids, col_ids // rows == row_ids // rows)
        scores = jnp.where(causal, scores, -jnp.inf)
        expo = jnp.exp(scores - jnp.max(scores, axis=1, keepdims=True))
        probs = (expo / jnp.sum(expo, axis=1, keepdims=True)).astype(BF16)
        local_o[h] = dot(probs, tvin[:, :, cols].reshape(2 * rows, HDIM), NN)

    for h in range(heads // 2):
        own_part(h)

    own_w.wait()
    wait_bytes(w_all.at[0, 0 : nz - 1, 0:wh], w1_recv.at[0])
    wait_bytes(w_all.at[0 : ny - 1, 0, wh:wc], w1_recv.at[1])
    lap(0, 0)
    lap(0, 1)

    for h in range(heads // 2, heads):
        own_part(h)

    wait_bytes(abuf.at[0 : nz - 1], a_recv)
    total = jnp.zeros((srows + NORM_ROWS, HDIM), F32)
    for k in range(nz):
        rbuf[k] = total
        total = total + abuf[k].astype(F32)
    tsend[...] = total.astype(BF16)
    tbuf[y] = tsend[...]
    for step in range(1, ny):
        send(tsend, tbuf.at[y], t_send, t_recv, y_dev(ahead(y, step, ny)))

    lap(1, 0)
    lap(1, 1)

    wait_bytes(tbuf.at[0 : ny - 1], t_recv)
    base = jnp.zeros((srows + NORM_ROWS, HDIM), F32)
    for k in range(ny):
        base = base + jnp.where(k < y, tbuf[k].astype(F32), 0.0)
    for k in range(nz):
        pbuf[k] = (base + rbuf[k]).astype(BF16)
    pfx[z] = pbuf[z]
    for step in range(1, nz):
        to = ahead(z, step, nz)
        send(pbuf.at[to], pfx.at[z], p_send, p_recv, z_dev(to))

    lap(2, 0)
    lap(2, 1)

    wait_bytes(pfx.at[0 : nz - 1], p_recv)

    def retrieve(h):
        query = qf[h]
        first = h * per_head
        state = pfx[first : first + per_head, 0:srows].reshape(HDIM, HDIM)
        numer = numer_l[h] + dot(query, state, NN)
        denom = dot(query, pfx[first, srows : srows + NORM_ROWS], NT)[:, 0:1] + denom_l[h]
        gate = 1.0 / (1.0 + jnp.exp(-jnp.full((8, HDIM), gate_ref[c * heads + h], F32)))[0:1]
        mixed[c * heads + h] = (gate * (numer / denom) + (1.0 - gate) * local_o[h]).astype(BF16)

    for h in range(heads // 2):
        retrieve(h)
    lap(3, 0)
    lap(3, 1)
    for h in range(heads // 2, heads):
        retrieve(h)
    own_mix = mixed.at[pl.ds(c * heads, heads)]
    mix_copy = send(own_mix, own_mix, m_send, m_recv, twin)

    ypx = ny // nx
    group_n = nz // 2
    pieces = part_own.shape[0]
    a_pieces = pieces - 2
    mix_copy.wait_recv()

    def both():
        return jnp.concatenate([mixed[h] for h in range(2 * heads)], axis=1)

    def deliver(xx, first, values, sem):
        slot = lax.rem(x - xx + nx, nx)
        span = pl.ds(first, len(values))

        @pl.when(slot == 0)
        def _():
            for i, value in enumerate(values):
                part_own[first + i] = value

        if nx > 1:

            @pl.when(slot > 0)
            def _():
                for i, value in enumerate(values):
                    part_send[slot - 1, first + i] = value.astype(BF16)
                send(
                    part_send.at[slot - 1, span], part_recv.at[slot - 1, span],
                    x_send.at[slot - 1, sem], x_recv.at[slot - 1, sem], x_dev(xx),
                )

    def project_a(xx):
        block = w_all[pl.ds(xx * ypx, ypx), :, 0:wh].reshape(ypx * nz * wh, width)
        value = dot(both(), block, NT)
        deliver(xx, 0, [value[:, i * HDIM : (i + 1) * HDIM] for i in range(a_pieces)], 0)

    def z_of(place):
        return lax.rem(z + place - 1 + nz, nz)

    def project_b(xxs, g):
        block = jnp.concatenate(
            [
                w_all[pl.ds(xx * ypx, ypx), z_of(g * group_n + k), wh:wc].reshape(ypx * wh, width)
                for xx in xxs
                for k in range(group_n)
            ]
        )
        value = dot(both(), block, NT)
        for i, xx in enumerate(xxs):
            deliver(xx, a_pieces + g, [value[:, i * HDIM : (i + 1) * HDIM]], 1 + g)

    def all_arrived(half, last):
        for key in list(laps):
            if key[0] == half and key[2] <= last:
                arrived(key)

    steps_x = list(range(1, nx)) + [0]
    pairs = [[ahead(x, r, nx) for r in steps_x[i : i + 2]] for i in range(0, nx, 2)]
    group = y // ypx
    order = [0] + [r for k in range(1, nx // 2) for r in (k, nx - k)] + ([nx // 2] if nx > 1 else [])
    all_arrived(1, 1)
    for xxs in pairs:
        project_b(xxs, 0)
    all_arrived(0, lap_len(0) - 2)
    for r in order[:-1]:
        project_a(ahead(group, r, nx))
    all_arrived(1, lap_len(1))
    for xxs in pairs:
        project_b(xxs, 1)
    all_arrived(0, lap_len(0))
    project_a(ahead(group, order[-1], nx))

    sems = [list(range(a_pieces)), [a_pieces], [a_pieces + 1]]
    for sem, group_pieces in ((1, sems[1]), (2, sems[2]), (0, sems[0])):
        span = slice(group_pieces[0], group_pieces[-1] + 1)
        for s in range(nx - 1):
            wait_bytes(part_recv.at[s, span], x_recv.at[s, sem])
        for i in group_pieces:
            acc = part_own[i]
            for s in range(nx - 1):
                acc = acc + part_recv[s, i].astype(F32)
            acc = acc.astype(BF16)
            dsend[0, i] = acc[0:rows]
            dsend[1, i] = acc[rows : 2 * rows]
    done_copy = send(dsend.at[1 - c], fin.at[c], d_send, d_recv, twin)
    fin[c] = dsend[c]
    done_copy.wait_recv()

    lane = lax.broadcasted_iota(jnp.int32, (rows, HDIM), 1)
    runs = HDIM // wh
    for b in range(2 * pieces):
        value = jnp.zeros((rows, HDIM), F32)
        for k in range(runs):
            run = b * runs + k
            shard, e, half = run // 4, (run // 2) % 2, run % 2
            yy, zz = shard // nz, shard % nz
            if half == 0:
                pos = shard * wh
                piece = fin[e, pos // HDIM].astype(F32)
                shift = (k * wh - pos) % HDIM
            else:
                place = lax.rem(zz - z + 1 + nz, nz)
                pos = lax.rem(place, group_n) * (ypx * wh) + yy * wh
                piece = fin[e, a_pieces + place // group_n].astype(F32)
                shift = lax.rem(k * wh - pos + HDIM, HDIM)
            piece = pltpu.roll(piece, shift, 1)
            value = jnp.where(lane // wh == k, piece, value)
        out_ref[:, b * HDIM : (b + 1) * HDIM] = value.astype(BF16)

    for copy in swaps:
        copy.wait_send()
    wait_bytes(w_all.at[0, 0 : nz - 1, 0:wh], w1_send.at[0])
    wait_bytes(w_all.at[0 : ny - 1, 0, wh:wc], w1_send.at[1])
    wait_bytes(sbuf.at[0 : nz - 1], a_send)
    wait_bytes(tbuf.at[0 : ny - 1], t_send)
    wait_bytes(pbuf.at[0 : nz - 1], p_send)
    for copy in laps.values():
        copy.wait_send()
    mix_copy.wait_send()
    for s in range(nx - 1):
        wait_bytes(part_send.at[s, 0:a_pieces], x_send.at[s, 0])
        wait_bytes(part_send.at[s, a_pieces], x_send.at[s, 1])
        wait_bytes(part_send.at[s, a_pieces + 1], x_send.at[s, 2])
    done_copy.wait_send()


def local(grid, vk, vv, q, tk, tv, bounds, gate, w):
    ny, nz, nx = grid
    vlen, width = vk.shape
    rows = q.shape[0]
    half_w = width // 2
    heads = half_w // HDIM
    srows = half_w // nz
    wt = w.T
    wc = wt.shape[0]
    out_w = (ny // nx) * nz * wc * 2
    pieces = out_w // 2 // HDIM
    assert pieces % 2 == 0 and nz * (ny // nx) * wc // 4 == HDIM
    steps = max(ny, nz) // 2
    peers = max(nx - 1, 1)
    hbm = pl.BlockSpec(memory_space=pltpu.HBM)
    smem = pl.BlockSpec(memory_space=pltpu.SMEM)
    dma = pltpu.SemaphoreType.DMA
    slices = (nz, srows + NORM_ROWS, HDIM)
    per_head = (heads, 2 * rows, HDIM)
    return pl.pallas_call(
        functools.partial(kernel, ny, nz, nx),
        out_shape=jax.ShapeDtypeStruct((rows, out_w), BF16),
        in_specs=[smem, smem] + [hbm] * 6,
        out_specs=pl.BlockSpec(memory_space=pltpu.VMEM),
        scratch_shapes=[
            pltpu.VMEM((ny, nz, wc, width), BF16),
            pltpu.VMEM((2, vlen, half_w), BF16),
            pltpu.VMEM((2, vlen, half_w), BF16),
            pltpu.VMEM((2, rows, half_w), BF16),
            pltpu.VMEM((2, rows, half_w), BF16),
            pltpu.VMEM((2, rows, half_w), BF16),
            pltpu.VMEM((2, 8, HDIM), jnp.int32),
            pltpu.VMEM((2, vlen, half_w), BF16),
            pltpu.VMEM(per_head, BF16),
            pltpu.VMEM(slices, BF16),
            pltpu.VMEM(slices, BF16),
            pltpu.VMEM(slices, F32),
            pltpu.VMEM((ny, srows + NORM_ROWS, HDIM), BF16),
            pltpu.VMEM((srows + NORM_ROWS, HDIM), BF16),
            pltpu.VMEM(slices, BF16),
            pltpu.VMEM(slices, BF16),
            pltpu.VMEM(per_head, F32),
            pltpu.VMEM(per_head, F32),
            pltpu.VMEM(per_head, F32),
            pltpu.VMEM((2 * heads, 2 * rows, HDIM), BF16),
            pltpu.VMEM((peers, pieces, 2 * rows, HDIM), BF16),
            pltpu.VMEM((pieces, 2 * rows, HDIM), F32),
            pltpu.VMEM((peers, pieces, 2 * rows, HDIM), BF16),
            pltpu.VMEM((2, pieces, rows, HDIM), BF16),
            pltpu.VMEM((2, pieces, rows, HDIM), BF16),
            dma((5,)),
            dma,
            dma((6,)),
            dma((6,)),
            dma((2,)),
            dma((2,)),
            dma((2, 2, steps, 2)),
            dma((2, 2, steps, 2)),
            dma, dma, dma, dma, dma, dma, dma, dma,
            dma((peers, 3)),
            dma((peers, 3)),
            dma, dma,
        ],
        compiler_params=pltpu.CompilerParams(
            collective_id=0, has_side_effects=True, vmem_limit_bytes=60 * 1024 * 1024
        ),
    )(bounds, gate, vk, vv, q, tk, tv, wt)


def solution(mesh):
    nx = mesh.shape["head"]
    specs = (
        P("tm", "head"),
        P("tm", "head"),
        P("tm", "head"),
        P("tm", "head"),
        P("tm", "head"),
        P("tm"),
        P("head"),
        P("head", "tm"),
    )
    return jax.shard_map(
        functools.partial(local, (8, mesh.shape["tm"] // 16, nx)),
        mesh=mesh,
        in_specs=specs,
        out_specs=P("tm", "head"),
        check_vma=False,
    )
```

```python
import functools

import jax
import jax.numpy as jnp
from jax import lax
from jax.experimental import pallas as pl
from jax.experimental.pallas import tpu as pltpu
from jax.sharding import PartitionSpec as P

MESH = pl.DeviceIdType.MESH
F32 = jnp.float32
BF16 = jnp.bfloat16
HDIM = 128
NORM_ROWS = 16
NN = (((1,), (0,)), ((), ()))
NT = (((1,), (1,)), ((), ()))
TN = (((0,), (0,)), ((), ()))


def dot(a, b, dims):
    return lax.dot_general(a, b, dims, preferred_element_type=F32)


def elu_one(values):
    return jnp.where(values > 0, values + 1.0, jnp.exp(jnp.minimum(values, 0.0)))


def split(value):
    high = value.astype(BF16)
    return high, (value - high.astype(F32)).astype(BF16)


def wait_bytes(ref, sem):
    pltpu.make_async_copy(ref, ref, sem).wait()


def kernel(
    ny,
    nz,
    nx,
    gy,
    gz,
    bound_ref,
    gate_ref,
    vk_ref,
    vv_ref,
    q_ref,
    tk_ref,
    tv_ref,
    w_ref,
    out_ref,
    w_all,
    kin,
    vin,
    qin,
    tkin,
    tvin,
    bin_,
    kf,
    qf,
    sbuf,
    abuf,
    rbuf,
    tbuf,
    tsend,
    base,
    pbuf,
    pfx,
    numer_l,
    denom_l,
    local_o,
    mixed,
    far_send,
    far_recv,
    dir_send,
    dir_recv,
    sum_own,
    sum_fwd,
    fwd_send,
    fwd_recv,
    dsend,
    fin,
    in_sem,
    w_sem,
    c_send,
    c_recv,
    w1_send,
    w1_recv,
    w2_send,
    w2_recv,
    a_send,
    a_recv,
    t_send,
    t_recv,
    p_send,
    p_recv,
    g_send,
    g_recv,
    m_send,
    m_recv,
    x_send,
    x_recv,
    d_send,
    d_recv,
):
    tm = lax.axis_index("tm")
    x = lax.axis_index("head")
    c = lax.rem(tm, 2)
    chip = tm // 2
    z = lax.rem(chip, nz)
    y = chip // nz

    vlen, width = vk_ref.shape
    rows = q_ref.shape[0]
    half_w = width // 2
    heads = half_w // HDIM
    per_head = nz // heads
    srows = HDIM // per_head
    wc = w_ref.shape[0]
    wh = wc // 2
    my, mz = ny // gy, nz // gz
    py, pz = lax.rem(y, gy), lax.rem(z, gz)
    yc, zc = y // gy, z // gz
    own_class = py * gz + pz
    offsets = [(dy, dz) for dy in range(gy) for dz in range(gz)]
    offsets.sort(key=lambda o: (o[0] + o[1], o[1]))

    def dev(t, xx):
        return {"tm": t, "head": xx}

    def y_dev(yy):
        return dev((yy * nz + z) * 2 + c, x)

    def z_dev(zz):
        return dev((y * nz + zz) * 2 + c, x)

    def x_dev(xx):
        return dev(tm, xx)

    def group_dev(dy, dz, core):
        yy = yc * gy + lax.rem(py + dy, gy)
        zz = zc * gz + lax.rem(pz + dz, gz)
        return dev((yy * nz + zz) * 2 + core, x)

    def class_of(dy, dz):
        return lax.rem(py + dy, gy) * gz + lax.rem(pz + dz, gz)

    twin = dev(tm + 1 - 2 * c, x)

    def ahead(me, step, n):
        return lax.rem(me + step, n)

    def send(src, dst, send_sem, recv_sem, device):
        copy = pltpu.make_async_remote_copy(
            src, dst, send_sem, recv_sem, device_id=device, device_id_type=MESH
        )
        copy.start()
        return copy

    mine = pl.ds(pl.multiple_of(c * half_w, HDIM), half_w)
    other = pl.ds(pl.multiple_of((1 - c) * half_w, HDIM), half_w)
    inputs = ((vk_ref, kin), (vv_ref, vin), (q_ref, qin), (tk_ref, tkin), (tv_ref, tvin))
    loads = [
        pltpu.make_async_copy(src.at[:, mine], dst.at[c], in_sem.at[i])
        for i, (src, dst) in enumerate(inputs)
    ]
    for load in loads:
        load.start()
    own_w = pltpu.make_async_copy(w_ref, w_all.at[yc, zc], w_sem)
    own_w.start()

    barrier = pltpu.get_barrier_semaphore()

    def greet(device):
        pl.semaphore_signal(barrier, inc=1, device_id=device, device_id_type=MESH)

    greet(twin)
    for step in range(1, nz):
        greet(z_dev(ahead(z, step, nz)))
    for step in range(1, ny):
        greet(y_dev(ahead(y, step, ny)))
    x_steps = [1, nx - 1] if nx > 2 else list(range(1, nx))
    for step in x_steps:
        greet(x_dev(ahead(x, step, nx)))
    greeted = 1 + (nz - 1) + (ny - 1) + len(x_steps)
    for dy, dz in offsets[1:]:
        greet(group_dev(dy, dz, 1 - c))
        greeted += 1
        if dy and dz:
            greet(group_dev(dy, dz, c))
            greeted += 1
    bin_[c] = jnp.full((8, HDIM), bound_ref[0], jnp.int32)
    loads[0].wait()
    kf[c] = elu_one(kin[c].astype(F32)).astype(BF16)
    pl.semaphore_wait(barrier, greeted)

    swaps = [
        send(src.at[:, other], dst.at[c], c_send.at[i], c_recv.at[i], twin)
        for i, (src, dst) in enumerate(inputs)
    ]
    swaps.append(send(bin_.at[c], bin_.at[c], c_send.at[5], c_recv.at[5], twin))

    def y_class(k):
        return y_dev(k * gy + py)

    def z_class(k):
        return z_dev(k * gz + pz)

    for step in range(1, mz):
        send(w_ref.at[0:wh], w_all.at[yc, zc, 0:wh], w1_send.at[0], w1_recv.at[0], z_class(ahead(zc, step, mz)))
    for step in range(1, my):
        send(w_ref.at[wh:wc], w_all.at[yc, zc, wh:wc], w1_send.at[1], w1_recv.at[1], y_class(ahead(yc, step, my)))

    loads[1].wait()
    swaps[0].wait_recv()
    kf[1 - c] = elu_one(kin[1 - c].astype(F32)).astype(BF16)
    swaps[1].wait_recv()
    ones = jnp.ones((NORM_ROWS, 2 * vlen), BF16)
    norm_row = lax.broadcasted_iota(jnp.int32, (NORM_ROWS, HDIM), 0)
    norms = jnp.zeros((NORM_ROWS, HDIM), F32)
    for h in range(heads):
        cols = slice(h * HDIM, (h + 1) * HDIM)
        feat = kf[:, :, cols].reshape(2 * vlen, HDIM)
        state = dot(feat, vin[:, :, cols].reshape(2 * vlen, HDIM), TN).astype(BF16)
        norms = jnp.where(norm_row == h, dot(ones, feat, NN), norms)
        for k in range(per_head):
            sbuf[h * per_head + k, 0:srows] = state[k * srows : (k + 1) * srows]
    for k in range(nz):
        sbuf[k, srows : srows + NORM_ROWS] = norms.astype(BF16)
    abuf[z] = sbuf[z]
    for step in range(1, nz):
        to = ahead(z, step, nz)
        send(sbuf.at[to], abuf.at[z], a_send, a_recv, z_dev(to))

    def bundle(half, index, q):
        if half == 0:
            return w_all.at[index, q * (mz // 2) : (q + 1) * (mz // 2), 0:wh]
        return w_all.at[q * (my // 2) : (q + 1) * (my // 2), index, wh:wc]

    laps = {}
    waited = set()

    def arrived(key):
        if key in laps and key not in waited:
            waited.add(key)
            laps[key].wait_recv()

    def lap(s, q):
        for half in range(2):
            for way in range(2):
                n, me = (my, yc) if half == 0 else (mz, zc)
                if s >= n // 2 or (s == n // 2 - 1 and q != way):
                    continue
                arrived((half, way, s - 1, q))
                block = ahead(me, n - s, n) if way == 0 else ahead(me, s, n)
                to = ahead(me, 1, n) if way == 0 else ahead(me, n - 1, n)
                part = bundle(half, block, q)
                laps[(half, way, s, q)] = send(
                    part, part, w2_send.at[half, way, s, q], w2_recv.at[half, way, s, q],
                    y_class(to) if half == 0 else z_class(to),
                )

    for i in range(2, 5):
        loads[i].wait()
        swaps[i].wait_recv()
    swaps[5].wait_recv()
    bounds = jnp.concatenate(
        [jnp.broadcast_to(bin_[0, 0:1, :], (rows, HDIM)), jnp.broadcast_to(bin_[1, 0:1, :], (rows, HDIM))]
    )
    row_ids = lax.broadcasted_iota(jnp.int32, (2 * rows, HDIM), 0)
    col_ids = lax.broadcasted_iota(jnp.int32, (2 * rows, HDIM), 1)

    def own_part(h):
        cols = slice(h * HDIM, (h + 1) * HDIM)
        query = qin[:, :, cols].reshape(2 * rows, HDIM)
        q_feat = elu_one(query.astype(F32)).astype(BF16)
        qf[h] = q_feat
        numer = jnp.zeros((2 * rows, HDIM), F32)
        denom = jnp.zeros((2 * rows, 1), F32)
        for e in range(2):
            weight = dot(q_feat, kf[e, :, cols], NT)
            weight = jnp.where(col_ids + (chip * 2 + e) * vlen < bounds, weight, 0.0)
            high, low = split(weight)
            values = vin[e, :, cols]
            numer = numer + dot(high, values, NN) + dot(low, values, NN)
            denom = denom + jnp.sum(weight, axis=1, keepdims=True)
        numer_l[h] = numer
        denom_l[h] = jnp.broadcast_to(denom, (2 * rows, HDIM))
        scores = dot(query, tkin[:, :, cols].reshape(2 * rows, HDIM), NT) * (float(HDIM) ** -0.5)
        causal = jnp.logical_and(col_ids <= row_ids, col_ids // rows == row_ids // rows)
        scores = jnp.where(causal, scores, -jnp.inf)
        expo = jnp.exp(scores - jnp.max(scores, axis=1, keepdims=True))
        probs = (expo / jnp.sum(expo, axis=1, keepdims=True)).astype(BF16)
        local_o[h] = dot(probs, tvin[:, :, cols].reshape(2 * rows, HDIM), NN)

    for h in range(heads):
        own_part(h)

    wait_bytes(abuf.at[0 : nz - 1], a_recv)
    total = jnp.zeros((srows + NORM_ROWS, HDIM), F32)
    for k in range(nz):
        rbuf[k] = total
        total = total + abuf[k].astype(F32)
    tsend[...] = total.astype(BF16)
    for step in range(1, ny):

        @pl.when(y + step < ny)
        def _():
            send(tsend, tbuf.at[y], t_send.at[step], t_recv.at[y], y_dev(y + step))

    own_w.wait()
    if mz > 1:
        wait_bytes(w_all.at[0, 0 : mz - 1, 0:wh], w1_recv.at[0])
    if my > 1:
        wait_bytes(w_all.at[0 : my - 1, 0, wh:wc], w1_recv.at[1])
    steps = max(my, mz) // 2
    if steps:
        lap(0, 0)
        lap(0, 1)

    base[...] = jnp.zeros_like(base)
    for k in range(ny - 1):

        @pl.when(k < y)
        def _():
            wait_bytes(tbuf.at[k], t_recv.at[k])
            base[...] += tbuf[k].astype(F32)

    for k in range(nz):
        pbuf[k] = (base[0:srows] + rbuf[k, 0:srows]).astype(BF16)
    pfx[z] = pbuf[z]
    for step in range(1, nz):
        to = ahead(z, step, nz)
        send(pbuf.at[to], pfx.at[z], p_send, p_recv, z_dev(to))
    norm_high, norm_low = split(base[srows : srows + NORM_ROWS] + rbuf[z, srows : srows + NORM_ROWS])

    for s in range(1, steps):
        lap(s, 0)
        lap(s, 1)

    wait_bytes(pfx.at[0 : nz - 1], p_recv)
    for h in range(heads):
        query = qf[h]
        first = h * per_head
        state = pfx[first : first + per_head].reshape(HDIM, HDIM)
        numer = numer_l[h] + dot(query, state, NN)
        denom = (dot(query, norm_high, NT) + dot(query, norm_low, NT))[:, h : h + 1] + denom_l[h]
        gate = 1.0 / (1.0 + jnp.exp(-jnp.full((8, HDIM), gate_ref[c * heads + h], F32)))[0:1]
        value = gate * (numer / denom) + (1.0 - gate) * local_o[h]
        mixed[own_class, c * heads + h] = value.astype(BF16)

    def mixed_half(cls):
        return mixed.at[cls, pl.ds(c * heads, heads)]

    group_copies, twin_copies = [None], []
    for r, (dy, dz) in enumerate(offsets):
        part = mixed_half(own_class)
        if r == 0:
            twin_copies.append(send(part, part, m_send.at[0], m_recv.at[0], twin))
        else:
            group_copies.append(send(part, part, g_send.at[r], g_recv.at[r], group_dev(dy, dz, c)))
    for key in list(laps):
        arrived(key)

    yx = my // nx

    def project(cls, xxs):
        both = jnp.concatenate([mixed[cls, h] for h in range(2 * heads)], axis=1)
        block = jnp.concatenate([w_all[pl.ds(xx * yx, yx)].reshape(yx * mz * wc, width) for xx in xxs])
        value = dot(both, block, NT)
        return [value[:, i * HDIM : (i + 1) * HDIM] for i in range(len(xxs))]

    far_copies, dir_copies, fwd_copies = [], [], []

    def forward(r):
        to = ahead(x, 1 if r % 2 == 0 else nx - 1, nx)
        far_copies[r].wait_recv()
        fwd_send[r] = (sum_fwd[r] + far_recv[r].astype(F32)).astype(BF16)
        fwd_copies.append(send(fwd_send.at[r], fwd_recv.at[r], x_send.at[r, 2], x_recv.at[r, 2], x_dev(to)))

    for r, (dy, dz) in enumerate(offsets):
        cls = class_of(dy, dz)
        twin_copies[r].wait_recv()
        if r + 1 < len(offsets):
            group_copies[r + 1].wait_recv()
            part = mixed_half(class_of(*offsets[r + 1]))
            twin_copies.append(send(part, part, m_send.at[r + 1], m_recv.at[r + 1], twin))
        if nx == 4:
            near, away = (1, 3) if r % 2 == 0 else (3, 1)
            far, direct = project(cls, [ahead(x, 2, nx), ahead(x, away, nx)])
            far_send[r] = far.astype(BF16)
            far_copies.append(
                send(far_send.at[r], far_recv.at[r], x_send.at[r, 0], x_recv.at[r, 0], x_dev(ahead(x, near, nx)))
            )
            dir_send[r] = direct.astype(BF16)
            dir_copies.append(
                send(dir_send.at[r], dir_recv.at[r], x_send.at[r, 1], x_recv.at[r, 1], x_dev(ahead(x, away, nx)))
            )
            sum_fwd[r], sum_own[r] = project(cls, [ahead(x, near, nx), x])
            if r > 0:
                forward(r - 1)
        elif nx == 2:
            direct, sum_own[r] = project(cls, [1 - x, x])
            dir_send[r] = direct.astype(BF16)
            dir_copies.append(
                send(dir_send.at[r], dir_recv.at[r], x_send.at[r, 1], x_recv.at[r, 1], x_dev(1 - x))
            )
        else:
            (sum_own[r],) = project(cls, [x])
    if nx == 4:
        forward(len(offsets) - 1)

    done_copies = []
    for r, (dy, dz) in enumerate(offsets):
        total = sum_own[r]
        for copies, landed in ((dir_copies, dir_recv), (fwd_copies, fwd_recv)):
            if copies:
                copies[r].wait_recv()
                total = total + landed[r].astype(F32)
        total = total.astype(BF16)
        for e in range(2):
            dsend[r, e] = total[e * rows : (e + 1) * rows]
        place = fin.at[own_class * 2 + c]
        if r == 0:
            fin[own_class * 2 + c] = dsend[0, c]
            done_copies.append(send(dsend.at[0, 1 - c], place, d_send, d_recv, twin))
        else:
            for e in range(2):
                done_copies.append(send(dsend.at[r, e], place, d_send, d_recv, group_dev(dy, dz, e)))
    wait_bytes(fin.at[0 : len(done_copies)], d_recv)

    lane = lax.broadcasted_iota(jnp.int32, (rows, HDIM), 1)
    runs = HDIM // wc
    for b in range(out_ref.shape[1] // HDIM):
        value = jnp.zeros((rows, HDIM), F32)
        for k in range(runs):
            shard, e = divmod(b * runs + k, 2)
            yl, zz = divmod(shard, nz)
            pos = ((yl // gy) * mz + zz // gz) * wc
            piece = fin[((yl % gy) * gz + zz % gz) * 2 + e].astype(F32)
            shift = (k * wc - pos) % HDIM
            if shift:
                piece = pltpu.roll(piece, shift, 1)
            value = jnp.where(lane // wc == k, piece, value)
        out_ref[:, b * HDIM : (b + 1) * HDIM] = value.astype(BF16)

    for copy in swaps:
        copy.wait_send()
    if mz > 1:
        wait_bytes(w_all.at[0, 0 : mz - 1, 0:wh], w1_send.at[0])
    if my > 1:
        wait_bytes(w_all.at[0 : my - 1, 0, wh:wc], w1_send.at[1])
    wait_bytes(sbuf.at[0 : nz - 1], a_send)
    for step in range(1, ny):

        @pl.when(y + step < ny)
        def _():
            wait_bytes(tsend, t_send.at[step])

    wait_bytes(pbuf.at[0 : nz - 1], p_send)
    for copies in (laps.values(), twin_copies, group_copies[1:], far_copies, dir_copies, fwd_copies):
        for copy in copies:
            copy.wait_send()
    wait_bytes(fin.at[0 : len(done_copies)], d_send)


def local(grid, vk, vv, q, tk, tv, bounds, gate, w):
    ny, nz, nx, gy, gz = grid
    vlen, width = vk.shape
    rows = q.shape[0]
    half_w = width // 2
    heads = half_w // HDIM
    srows = half_w // nz
    wt = w.T
    wc = wt.shape[0]
    my, mz = ny // gy, nz // gz
    n = gy * gz
    assert (my // nx) * mz * wc == HDIM
    steps = max(my, mz, 2) // 2
    hbm = pl.BlockSpec(memory_space=pltpu.HBM)
    smem = pl.BlockSpec(memory_space=pltpu.SMEM)
    dma = pltpu.SemaphoreType.DMA
    slices = (nz, srows + NORM_ROWS, HDIM)
    states = (nz, srows, HDIM)
    per_head = (heads, 2 * rows, HDIM)
    blocks = (n, 2 * rows, HDIM)
    return pl.pallas_call(
        functools.partial(kernel, ny, nz, nx, gy, gz),
        out_shape=jax.ShapeDtypeStruct((rows, 2 * n * HDIM), BF16),
        in_specs=[smem, smem] + [hbm] * 6,
        out_specs=pl.BlockSpec(memory_space=pltpu.VMEM),
        scratch_shapes=[
            pltpu.VMEM((my, mz, wc, width), BF16),
            pltpu.VMEM((2, vlen, half_w), BF16),
            pltpu.VMEM((2, vlen, half_w), BF16),
            pltpu.VMEM((2, rows, half_w), BF16),
            pltpu.VMEM((2, rows, half_w), BF16),
            pltpu.VMEM((2, rows, half_w), BF16),
            pltpu.VMEM((2, 8, HDIM), jnp.int32),
            pltpu.VMEM((2, vlen, half_w), BF16),
            pltpu.VMEM(per_head, BF16),
            pltpu.VMEM(slices, BF16),
            pltpu.VMEM(slices, BF16),
            pltpu.VMEM(slices, F32),
            pltpu.VMEM((ny, srows + NORM_ROWS, HDIM), BF16),
            pltpu.VMEM((srows + NORM_ROWS, HDIM), BF16),
            pltpu.VMEM((srows + NORM_ROWS, HDIM), F32),
            pltpu.VMEM(states, BF16),
            pltpu.VMEM(states, BF16),
            pltpu.VMEM(per_head, F32),
            pltpu.VMEM(per_head, F32),
            pltpu.VMEM(per_head, F32),
            pltpu.VMEM((n, 2 * heads, 2 * rows, HDIM), BF16),
            pltpu.VMEM(blocks, BF16),
            pltpu.VMEM(blocks, BF16),
            pltpu.VMEM(blocks, BF16),
            pltpu.VMEM(blocks, BF16),
            pltpu.VMEM(blocks, F32),
            pltpu.VMEM(blocks, F32),
            pltpu.VMEM(blocks, BF16),
            pltpu.VMEM(blocks, BF16),
            pltpu.VMEM((n, 2, rows, HDIM), BF16),
            pltpu.VMEM((2 * n, rows, HDIM), BF16),
            dma((5,)),
            dma,
            dma((6,)),
            dma((6,)),
            dma((2,)),
            dma((2,)),
            dma((2, 2, steps, 2)),
            dma((2, 2, steps, 2)),
            dma,
            dma,
            dma((ny,)),
            dma((ny,)),
            dma,
            dma,
            dma((n,)),
            dma((n,)),
            dma((n,)),
            dma((n,)),
            dma((n, 3)),
            dma((n, 3)),
            dma,
            dma,
        ],
        compiler_params=pltpu.CompilerParams(
            collective_id=0, has_side_effects=True, vmem_limit_bytes=60 * 1024 * 1024
        ),
    )(bounds, gate, vk, vv, q, tk, tv, wt)


def solution(mesh):
    nx = mesh.shape["head"]
    specs = (
        P("tm", "head"),
        P("tm", "head"),
        P("tm", "head"),
        P("tm", "head"),
        P("tm", "head"),
        P("tm"),
        P("head"),
        P("head", "tm"),
    )
    return jax.shard_map(
        functools.partial(local, (8, mesh.shape["tm"] // 16, nx, 2, 2)),
        mesh=mesh,
        in_specs=specs,
        out_specs=P("tm", "head"),
        check_vma=False,
    )
```

```python
import functools

import jax
import jax.numpy as jnp
from jax import lax
from jax.experimental import pallas as pl
from jax.experimental.pallas import tpu as pltpu
from jax.sharding import PartitionSpec as P

MESH = pl.DeviceIdType.MESH
F32 = jnp.float32
BF16 = jnp.bfloat16
HDIM = 128
NORM_ROWS = 16
NN = (((1,), (0,)), ((), ()))
NT = (((1,), (1,)), ((), ()))
TN = (((0,), (0,)), ((), ()))


def dot(a, b, dims):
    return lax.dot_general(a, b, dims, preferred_element_type=F32)


def elu_one(values):
    return jnp.where(values > 0, values + 1.0, jnp.exp(jnp.minimum(values, 0.0)))


def split(value):
    high = value.astype(BF16)
    return high, (value - high.astype(F32)).astype(BF16)


def wait_bytes(ref, sem):
    pltpu.make_async_copy(ref, ref, sem).wait()


def kernel(
    ny,
    nz,
    nx,
    gy,
    gz,
    bound_ref,
    gate_ref,
    vk_ref,
    vv_ref,
    q_ref,
    tk_ref,
    tv_ref,
    w_ref,
    out_ref,
    w_all,
    kin,
    vown,
    vin,
    qin,
    tkin,
    tvin,
    bin_,
    kf,
    qf,
    s_send,
    s_recv,
    s_own,
    n_send,
    n_recv,
    n_own,
    sbuf,
    abuf,
    rbuf,
    tbuf,
    tsend,
    base,
    pbuf,
    pfx,
    numer_l,
    denom_l,
    local_o,
    mixed,
    far_send,
    far_recv,
    dir_send,
    dir_recv,
    sum_own,
    sum_fwd,
    fwd_send,
    fwd_recv,
    dsend,
    fin,
    in_sem,
    s_sem,
    w_sem,
    c_send,
    c_recv,
    w1_send,
    w1_recv,
    w2_send,
    w2_recv,
    a_send,
    a_recv,
    t_send,
    t_recv,
    p_send,
    p_recv,
    g_send,
    g_recv,
    m_send,
    m_recv,
    x_send,
    x_recv,
    d_send,
    d_recv,
):
    tm = lax.axis_index("tm")
    x = lax.axis_index("head")
    c = lax.rem(tm, 2)
    chip = tm // 2
    z = lax.rem(chip, nz)
    y = chip // nz

    vlen, width = vk_ref.shape
    rows = q_ref.shape[0]
    half_w = width // 2
    heads = half_w // HDIM
    per_head = nz // heads
    srows = HDIM // per_head
    wc = w_ref.shape[0]
    wh = wc // 2
    my, mz = ny // gy, nz // gz
    py, pz = lax.rem(y, gy), lax.rem(z, gz)
    yc, zc = y // gy, z // gz
    own_class = py * gz + pz
    offsets = [(dy, dz) for dy in range(gy) for dz in range(gz)]
    offsets.sort(key=lambda o: (o[0] + o[1], o[1]))

    def dev(t, xx):
        return {"tm": t, "head": xx}

    def y_dev(yy):
        return dev((yy * nz + z) * 2 + c, x)

    def z_dev(zz):
        return dev((y * nz + zz) * 2 + c, x)

    def x_dev(xx):
        return dev(tm, xx)

    def group_dev(dy, dz, core):
        yy = yc * gy + lax.rem(py + dy, gy)
        zz = zc * gz + lax.rem(pz + dz, gz)
        return dev((yy * nz + zz) * 2 + core, x)

    def class_of(dy, dz):
        return lax.rem(py + dy, gy) * gz + lax.rem(pz + dz, gz)

    twin = dev(tm + 1 - 2 * c, x)

    def ahead(me, step, n):
        return lax.rem(me + step, n)

    def send(src, dst, send_sem, recv_sem, device):
        copy = pltpu.make_async_remote_copy(
            src, dst, send_sem, recv_sem, device_id=device, device_id_type=MESH
        )
        copy.start()
        return copy

    mine = pl.ds(pl.multiple_of(c * half_w, HDIM), half_w)
    other = pl.ds(pl.multiple_of((1 - c) * half_w, HDIM), half_w)
    inputs = ((vk_ref, kin), (vv_ref, vin), (q_ref, qin), (tk_ref, tkin), (tv_ref, tvin))
    loads = [
        pltpu.make_async_copy(vk_ref, kin, in_sem.at[0]),
        pltpu.make_async_copy(vv_ref, vown, in_sem.at[1]),
        pltpu.make_async_copy(vv_ref.at[:, mine], vin.at[c], in_sem.at[5]),
    ] + [
        pltpu.make_async_copy(src.at[:, mine], dst.at[c], in_sem.at[i + 2])
        for i, (src, dst) in enumerate(inputs[2:])
    ]
    for load in loads:
        load.start()
    own_w = pltpu.make_async_copy(w_ref, w_all.at[yc, zc], w_sem)
    own_w.start()

    def far_first(n):
        return sorted(range(1, n), key=lambda step: -min(step, n - step))

    barrier = pltpu.get_barrier_semaphore()

    def greet(device):
        pl.semaphore_signal(barrier, inc=1, device_id=device, device_id_type=MESH)

    for step in far_first(nz):
        greet(z_dev(ahead(z, step, nz)))
    for step in far_first(ny):
        greet(y_dev(ahead(y, step, ny)))
    x_steps = [1, nx - 1] if nx > 2 else list(range(1, nx))
    for step in x_steps:
        greet(x_dev(ahead(x, step, nx)))
    greeted = 1 + (nz - 1) + (ny - 1) + len(x_steps)
    for dy, dz in offsets[1:]:
        greet(group_dev(dy, dz, 1 - c))
        greeted += 1
        if dy and dz:
            greet(group_dev(dy, dz, c))
            greeted += 1
    greet(twin)
    bin_[c] = jnp.full((8, HDIM), bound_ref[0], jnp.int32)

    loads[0].wait()
    kin[...] = elu_one(kin[...].astype(F32)).astype(BF16)
    loads[1].wait()
    ones = jnp.ones((NORM_ROWS, vlen), BF16)
    norm_row = lax.broadcasted_iota(jnp.int32, (NORM_ROWS, HDIM), 0)

    def own_state(core):
        norms = jnp.zeros((NORM_ROWS, HDIM), F32)
        states = []
        for h in range(heads):
            cols = pl.ds(pl.multiple_of(core * half_w + h * HDIM, HDIM), HDIM)
            feat = kin[:, cols]
            states.append(dot(feat, vown[:, cols], TN))
            norms = jnp.where(norm_row == h, dot(ones, feat, NN), norms)
        return states, norms

    states, norms = own_state(1 - c)
    for h in range(heads):
        for k in range(per_head):
            s_send[h * per_head + k] = states[h][k * srows : (k + 1) * srows].astype(BF16)
    n_send[...] = norms.astype(BF16)
    states, norms = own_state(c)
    for h in range(heads):
        for k in range(per_head):
            s_own[h * per_head + k] = states[h][k * srows : (k + 1) * srows]
    n_own[...] = norms
    kf[c] = kin[:, mine]
    pl.semaphore_wait(barrier, greeted)

    state_copy = send(s_send, s_recv, s_sem.at[0], s_sem.at[1], twin)
    norm_copy = send(n_send, n_recv, s_sem.at[2], s_sem.at[3], twin)
    state_copy.wait_recv()
    norm_copy.wait_recv()
    norms = (n_own[...] + n_recv[...].astype(F32)).astype(BF16)
    for k in range(nz):
        sbuf[k, 0:srows] = (s_own[k] + s_recv[k].astype(F32)).astype(BF16)
        sbuf[k, srows : srows + NORM_ROWS] = norms
    for step in far_first(nz):
        to = ahead(z, step, nz)
        send(sbuf.at[to], abuf.at[z], a_send, a_recv, z_dev(to))
    abuf[z] = sbuf[z]

    swaps = [send(kin.at[:, other], kf.at[c], c_send.at[0], c_recv.at[0], twin)]
    swaps += [
        send(src.at[:, other], dst.at[c], c_send.at[i + 1], c_recv.at[i + 1], twin)
        for i, (src, dst) in enumerate(inputs[1:])
    ]
    swaps.append(send(bin_.at[c], bin_.at[c], c_send.at[5], c_recv.at[5], twin))

    def y_class(k):
        return y_dev(k * gy + py)

    def z_class(k):
        return z_dev(k * gz + pz)

    for step in far_first(mz):
        send(w_ref.at[0:wh], w_all.at[yc, zc, 0:wh], w1_send.at[0], w1_recv.at[0], z_class(ahead(zc, step, mz)))
    for step in far_first(my):
        send(w_ref.at[wh:wc], w_all.at[yc, zc, wh:wc], w1_send.at[1], w1_recv.at[1], y_class(ahead(yc, step, my)))

    def bundle(half, index, q):
        if half == 0:
            return w_all.at[index, q * (mz // 2) : (q + 1) * (mz // 2), 0:wh]
        return w_all.at[q * (my // 2) : (q + 1) * (my // 2), index, wh:wc]

    laps = {}
    waited = set()

    def arrived(key):
        if key in laps and key not in waited:
            waited.add(key)
            laps[key].wait_recv()

    def lap(s, q):
        for half in range(2):
            for way in range(2):
                n, me = (my, yc) if half == 0 else (mz, zc)
                if s >= n // 2 or (s == n // 2 - 1 and q != way):
                    continue
                arrived((half, way, s - 1, q))
                block = ahead(me, n - s, n) if way == 0 else ahead(me, s, n)
                to = ahead(me, 1, n) if way == 0 else ahead(me, n - 1, n)
                part = bundle(half, block, q)
                laps[(half, way, s, q)] = send(
                    part, part, w2_send.at[half, way, s, q], w2_recv.at[half, way, s, q],
                    y_class(to) if half == 0 else z_class(to),
                )

    for load in loads[2:]:
        load.wait()
    for swap in swaps:
        swap.wait_recv()
    bounds = jnp.concatenate(
        [jnp.broadcast_to(bin_[0, 0:1, :], (rows, HDIM)), jnp.broadcast_to(bin_[1, 0:1, :], (rows, HDIM))]
    )
    row_ids = lax.broadcasted_iota(jnp.int32, (2 * rows, HDIM), 0)
    col_ids = lax.broadcasted_iota(jnp.int32, (2 * rows, HDIM), 1)

    def own_part(h):
        cols = slice(h * HDIM, (h + 1) * HDIM)
        query = qin[:, :, cols].reshape(2 * rows, HDIM)
        q_feat = elu_one(query.astype(F32)).astype(BF16)
        qf[h] = q_feat
        numer = jnp.zeros((2 * rows, HDIM), F32)
        denom = jnp.zeros((2 * rows, 1), F32)
        for e in range(2):
            weight = dot(q_feat, kf[e, :, cols], NT)
            weight = jnp.where(col_ids + (chip * 2 + e) * vlen < bounds, weight, 0.0)
            high, low = split(weight)
            values = vin[e, :, cols]
            numer = numer + dot(high, values, NN) + dot(low, values, NN)
            denom = denom + jnp.sum(weight, axis=1, keepdims=True)
        numer_l[h] = numer
        denom_l[h] = jnp.broadcast_to(denom, (2 * rows, HDIM))
        scores = dot(query, tkin[:, :, cols].reshape(2 * rows, HDIM), NT) * (float(HDIM) ** -0.5)
        causal = jnp.logical_and(col_ids <= row_ids, col_ids // rows == row_ids // rows)
        scores = jnp.where(causal, scores, -jnp.inf)
        expo = jnp.exp(scores - jnp.max(scores, axis=1, keepdims=True))
        probs = (expo / jnp.sum(expo, axis=1, keepdims=True)).astype(BF16)
        local_o[h] = dot(probs, tvin[:, :, cols].reshape(2 * rows, HDIM), NN)

    own_part(0)

    wait_bytes(abuf.at[0 : nz - 1], a_recv)
    total = jnp.zeros((srows + NORM_ROWS, HDIM), F32)
    for k in range(nz):
        rbuf[k] = total
        total = total + abuf[k].astype(F32)
    tsend[...] = total.astype(BF16)
    for step in range(1, ny):

        @pl.when(y + step < ny)
        def _():
            send(tsend, tbuf.at[y], t_send.at[step], t_recv.at[y], y_dev(y + step))

    for h in range(1, max(1, heads - 1)):
        own_part(h)

    base[...] = jnp.zeros_like(base)
    for k in range(ny - 1):

        @pl.when(k < y)
        def _():
            wait_bytes(tbuf.at[k], t_recv.at[k])
            base[...] += tbuf[k].astype(F32)

    for k in range(nz):
        pbuf[k] = (base[0:srows] + rbuf[k, 0:srows]).astype(BF16)
    pfx[z] = pbuf[z]
    for step in far_first(nz):
        to = ahead(z, step, nz)
        send(pbuf.at[to], pfx.at[z], p_send, p_recv, z_dev(to))
    norm_high, norm_low = split(base[srows : srows + NORM_ROWS] + rbuf[z, srows : srows + NORM_ROWS])

    own_w.wait()
    if mz > 1:
        wait_bytes(w_all.at[0, 0 : mz - 1, 0:wh], w1_recv.at[0])
    if my > 1:
        wait_bytes(w_all.at[0 : my - 1, 0, wh:wc], w1_recv.at[1])
    steps = max(my, mz) // 2
    if steps:
        lap(0, 0)
        lap(0, 1)

    for h in range(max(1, heads - 1), heads):
        own_part(h)

    wait_bytes(pfx.at[0 : nz - 1], p_recv)

    def retrieve(h):
        query = qf[h]
        first = h * per_head
        state = pfx[first : first + per_head].reshape(HDIM, HDIM)
        numer = numer_l[h] + dot(query, state, NN)
        denom = (dot(query, norm_high, NT) + dot(query, norm_low, NT))[:, h : h + 1] + denom_l[h]
        gate = 1.0 / (1.0 + jnp.exp(-jnp.full((8, HDIM), gate_ref[c * heads + h], F32)))[0:1]
        value = gate * (numer / denom) + (1.0 - gate) * local_o[h]
        mixed[own_class, c * heads + h] = value.astype(BF16)

    split_n = 2 if heads > 1 else 1

    def mixed_part(cls, i):
        return mixed.at[cls, pl.ds(c * heads + i * (heads // split_n), heads // split_n)]

    group_copies, twin_copies = {}, {}
    for i in range(split_n):
        for h in range(i * heads // split_n, (i + 1) * heads // split_n):
            retrieve(h)
        part = mixed_part(own_class, i)
        for r, (dy, dz) in reversed(list(enumerate(offsets))):
            if r == 0:
                twin_copies[r, i] = send(part, part, m_send.at[r, i], m_recv.at[r, i], twin)
            else:
                group_copies[r, i] = send(part, part, g_send.at[r, i], g_recv.at[r, i], group_dev(dy, dz, c))
    for s in range(1, steps):
        lap(s, 0)
        lap(s, 1)

    state_copy.wait_send()
    norm_copy.wait_send()
    for copy in swaps:
        copy.wait_send()
    if mz > 1:
        wait_bytes(w_all.at[0, 0 : mz - 1, 0:wh], w1_send.at[0])
    if my > 1:
        wait_bytes(w_all.at[0 : my - 1, 0, wh:wc], w1_send.at[1])
    wait_bytes(sbuf.at[0 : nz - 1], a_send)
    for step in range(1, ny):

        @pl.when(y + step < ny)
        def _():
            wait_bytes(tsend, t_send.at[step])

    wait_bytes(pbuf.at[0 : nz - 1], p_send)
    for key in list(laps):
        arrived(key)
    for copy in laps.values():
        copy.wait_send()

    yx = my // nx

    def project(cls, xxs):
        both = jnp.concatenate([mixed[cls, h] for h in range(2 * heads)], axis=1)
        block = jnp.concatenate([w_all[pl.ds(xx * yx, yx)].reshape(yx * mz * wc, width) for xx in xxs])
        value = dot(both, block, NT)
        return [value[:, i * HDIM : (i + 1) * HDIM] for i in range(len(xxs))]

    far_copies, dir_copies, fwd_copies = [], [], []

    def forward(r):
        to = ahead(x, 1 if r % 2 == 0 else nx - 1, nx)
        far_copies[r].wait_recv()
        fwd_send[r] = (sum_fwd[r] + far_recv[r].astype(F32)).astype(BF16)
        fwd_copies.append(send(fwd_send.at[r], fwd_recv.at[r], x_send.at[r, 2], x_recv.at[r, 2], x_dev(to)))

    def hand_over(r):
        for i in range(split_n):
            group_copies[r, i].wait_recv()
            part = mixed_part(class_of(*offsets[r]), i)
            twin_copies[r, i] = send(part, part, m_send.at[r, i], m_recv.at[r, i], twin)

    for r, (dy, dz) in enumerate(offsets):
        cls = class_of(dy, dz)
        for i in range(split_n):
            twin_copies[r, i].wait_recv()
        if nx == 4:
            near, away = (1, 3) if r % 2 == 0 else (3, 1)
            far, direct = project(cls, [ahead(x, 2, nx), ahead(x, away, nx)])
            far_send[r] = far.astype(BF16)
            far_copies.append(
                send(far_send.at[r], far_recv.at[r], x_send.at[r, 0], x_recv.at[r, 0], x_dev(ahead(x, near, nx)))
            )
            dir_send[r] = direct.astype(BF16)
            dir_copies.append(
                send(dir_send.at[r], dir_recv.at[r], x_send.at[r, 1], x_recv.at[r, 1], x_dev(ahead(x, away, nx)))
            )
            sum_fwd[r], sum_own[r] = project(cls, [ahead(x, near, nx), x])
            if r > 0:
                forward(r - 1)
        elif nx == 2:
            direct, sum_own[r] = project(cls, [1 - x, x])
            dir_send[r] = direct.astype(BF16)
            dir_copies.append(
                send(dir_send.at[r], dir_recv.at[r], x_send.at[r, 1], x_recv.at[r, 1], x_dev(1 - x))
            )
        else:
            (sum_own[r],) = project(cls, [x])
        for later in {0: (1, 2), 1: (3,)}.get(r, ()):
            if later < len(offsets):
                hand_over(later)
    if nx == 4:
        forward(len(offsets) - 1)

    done_copies = []
    for r, (dy, dz) in enumerate(offsets):
        total = sum_own[r]
        for copies, landed in ((dir_copies, dir_recv), (fwd_copies, fwd_recv)):
            if copies:
                copies[r].wait_recv()
                total = total + landed[r].astype(F32)
        total = total.astype(BF16)
        for e in range(2):
            dsend[r, e] = total[e * rows : (e + 1) * rows]
        place = fin.at[own_class * 2 + c]
        if r == 0:
            fin[own_class * 2 + c] = dsend[0, c]
            done_copies.append(send(dsend.at[0, 1 - c], place, d_send, d_recv, twin))
        else:
            for e in range(2):
                done_copies.append(send(dsend.at[r, e], place, d_send, d_recv, group_dev(dy, dz, e)))
    wait_bytes(fin.at[0 : len(done_copies)], d_recv)

    lane = lax.broadcasted_iota(jnp.int32, (rows, HDIM), 1)
    runs = HDIM // wc
    for b in range(out_ref.shape[1] // HDIM):
        value = jnp.zeros((rows, HDIM), F32)
        for k in range(runs):
            shard, e = divmod(b * runs + k, 2)
            yl, zz = divmod(shard, nz)
            pos = ((yl // gy) * mz + zz // gz) * wc
            piece = fin[((yl % gy) * gz + zz % gz) * 2 + e].astype(F32)
            shift = (k * wc - pos) % HDIM
            if shift:
                piece = pltpu.roll(piece, shift, 1)
            value = jnp.where(lane // wc == k, piece, value)
        out_ref[:, b * HDIM : (b + 1) * HDIM] = value.astype(BF16)

    for copies in (twin_copies.values(), group_copies.values(), far_copies, dir_copies, fwd_copies):
        for copy in copies:
            copy.wait_send()
    wait_bytes(fin.at[0 : len(done_copies)], d_send)


def local(grid, vk, vv, q, tk, tv, bounds, gate, w):
    ny, nz, nx, gy, gz = grid
    vlen, width = vk.shape
    rows = q.shape[0]
    half_w = width // 2
    heads = half_w // HDIM
    srows = half_w // nz
    wt = w.T
    wc = wt.shape[0]
    my, mz = ny // gy, nz // gz
    n = gy * gz
    assert (my // nx) * mz * wc == HDIM
    steps = max(my, mz, 2) // 2
    hbm = pl.BlockSpec(memory_space=pltpu.HBM)
    smem = pl.BlockSpec(memory_space=pltpu.SMEM)
    dma = pltpu.SemaphoreType.DMA
    slices = (nz, srows + NORM_ROWS, HDIM)
    states = (nz, srows, HDIM)
    per_head = (heads, 2 * rows, HDIM)
    blocks = (n, 2 * rows, HDIM)
    return pl.pallas_call(
        functools.partial(kernel, ny, nz, nx, gy, gz),
        out_shape=jax.ShapeDtypeStruct((rows, 2 * n * HDIM), BF16),
        in_specs=[smem, smem] + [hbm] * 6,
        out_specs=pl.BlockSpec(memory_space=pltpu.VMEM),
        scratch_shapes=[
            pltpu.VMEM((my, mz, wc, width), BF16),
            pltpu.VMEM((vlen, width), BF16),
            pltpu.VMEM((vlen, width), BF16),
            pltpu.VMEM((2, vlen, half_w), BF16),
            pltpu.VMEM((2, rows, half_w), BF16),
            pltpu.VMEM((2, rows, half_w), BF16),
            pltpu.VMEM((2, rows, half_w), BF16),
            pltpu.VMEM((2, 8, HDIM), jnp.int32),
            pltpu.VMEM((2, vlen, half_w), BF16),
            pltpu.VMEM(per_head, BF16),
            pltpu.VMEM(states, BF16),
            pltpu.VMEM(states, BF16),
            pltpu.VMEM(states, F32),
            pltpu.VMEM((NORM_ROWS, HDIM), BF16),
            pltpu.VMEM((NORM_ROWS, HDIM), BF16),
            pltpu.VMEM((NORM_ROWS, HDIM), F32),
            pltpu.VMEM(slices, BF16),
            pltpu.VMEM(slices, BF16),
            pltpu.VMEM(slices, F32),
            pltpu.VMEM((ny, srows + NORM_ROWS, HDIM), BF16),
            pltpu.VMEM((srows + NORM_ROWS, HDIM), BF16),
            pltpu.VMEM((srows + NORM_ROWS, HDIM), F32),
            pltpu.VMEM(states, BF16),
            pltpu.VMEM(states, BF16),
            pltpu.VMEM(per_head, F32),
            pltpu.VMEM(per_head, F32),
            pltpu.VMEM(per_head, F32),
            pltpu.VMEM((n, 2 * heads, 2 * rows, HDIM), BF16),
            pltpu.VMEM(blocks, BF16),
            pltpu.VMEM(blocks, BF16),
            pltpu.VMEM(blocks, BF16),
            pltpu.VMEM(blocks, BF16),
            pltpu.VMEM(blocks, F32),
            pltpu.VMEM(blocks, F32),
            pltpu.VMEM(blocks, BF16),
            pltpu.VMEM(blocks, BF16),
            pltpu.VMEM((n, 2, rows, HDIM), BF16),
            pltpu.VMEM((2 * n, rows, HDIM), BF16),
            dma((6,)),
            dma((4,)),
            dma,
            dma((6,)),
            dma((6,)),
            dma((2,)),
            dma((2,)),
            dma((2, 2, steps, 2)),
            dma((2, 2, steps, 2)),
            dma,
            dma,
            dma((ny,)),
            dma((ny,)),
            dma,
            dma,
            dma((n, 2)),
            dma((n, 2)),
            dma((n, 2)),
            dma((n, 2)),
            dma((n, 3)),
            dma((n, 3)),
            dma,
            dma,
        ],
        compiler_params=pltpu.CompilerParams(
            collective_id=0, has_side_effects=True, vmem_limit_bytes=60 * 1024 * 1024
        ),
    )(bounds, gate, vk, vv, q, tk, tv, wt)


def solution(mesh):
    nx = mesh.shape["head"]
    specs = (
        P("tm", "head"),
        P("tm", "head"),
        P("tm", "head"),
        P("tm", "head"),
        P("tm", "head"),
        P("tm"),
        P("head"),
        P("head", "tm"),
    )
    return jax.shard_map(
        functools.partial(local, (8, mesh.shape["tm"] // 16, nx, 2, 2)),
        mesh=mesh,
        in_specs=specs,
        out_specs=P("tm", "head"),
        check_vma=False,
    )
```

```python
import functools

import jax
import jax.numpy as jnp
from jax import lax
from jax.experimental import pallas as pl
from jax.experimental.pallas import tpu as pltpu
from jax.sharding import PartitionSpec as P

MESH = pl.DeviceIdType.MESH
F32 = jnp.float32
BF16 = jnp.bfloat16
HDIM = 128
NORM_ROWS = 16
NN = (((1,), (0,)), ((), ()))
NT = (((1,), (1,)), ((), ()))
TN = (((0,), (0,)), ((), ()))


def dot(a, b, dims):
    return lax.dot_general(a, b, dims, preferred_element_type=F32)


def elu_one(values):
    return jnp.where(values > 0, values + 1.0, jnp.exp(jnp.minimum(values, 0.0)))


def split(value):
    high = value.astype(BF16)
    return high, (value - high.astype(F32)).astype(BF16)


def wait_bytes(ref, sem):
    pltpu.make_async_copy(ref, ref, sem).wait()


def kernel(
    ny,
    nz,
    nx,
    gy,
    gz,
    bound_ref,
    gate_ref,
    vk_ref,
    vv_ref,
    q_ref,
    tk_ref,
    tv_ref,
    w_ref,
    out_ref,
    w_all,
    kin,
    vown,
    vin,
    qin,
    tkin,
    tvin,
    bin_,
    kf,
    qf,
    s_send,
    s_recv,
    s_own,
    n_send,
    n_recv,
    n_own,
    sbuf,
    abuf,
    rbuf,
    tbuf,
    tsend,
    base,
    pbuf,
    pfx,
    numer_l,
    denom_l,
    local_o,
    mixed,
    far_send,
    far_recv,
    dir_send,
    dir_recv,
    sum_own,
    sum_fwd,
    fwd_send,
    fwd_recv,
    dsend,
    fin,
    in_sem,
    s_sem,
    w_sem,
    c_send,
    c_recv,
    w1_send,
    w1_recv,
    w2_send,
    w2_recv,
    a_send,
    a_recv,
    t_send,
    t_recv,
    p_send,
    p_recv,
    g_send,
    g_recv,
    m_send,
    m_recv,
    x_send,
    x_recv,
    d_send,
    d_recv,
):
    tm = lax.axis_index("tm")
    x = lax.axis_index("head")
    c = lax.rem(tm, 2)
    chip = tm // 2
    z = lax.rem(chip, nz)
    y = chip // nz

    vlen, width = vk_ref.shape
    rows = q_ref.shape[0]
    half_w = width // 2
    heads = half_w // HDIM
    per_head = nz // heads
    srows = HDIM // per_head
    wc = w_ref.shape[0]
    wh = wc // 2
    my, mz = ny // gy, nz // gz
    py, pz = lax.rem(y, gy), lax.rem(z, gz)
    yc, zc = y // gy, z // gz
    own_class = py * gz + pz
    offsets = [(dy, dz) for dy in range(gy) for dz in range(gz)]
    offsets.sort(key=lambda o: (o[0] + o[1], o[1]))

    def dev(t, xx):
        return {"tm": t, "head": xx}

    def y_dev(yy):
        return dev((yy * nz + z) * 2 + c, x)

    def z_dev(zz):
        return dev((y * nz + zz) * 2 + c, x)

    def x_dev(xx):
        return dev(tm, xx)

    def group_dev(dy, dz, core):
        yy = yc * gy + lax.rem(py + dy, gy)
        zz = zc * gz + lax.rem(pz + dz, gz)
        return dev((yy * nz + zz) * 2 + core, x)

    def class_of(dy, dz):
        return lax.rem(py + dy, gy) * gz + lax.rem(pz + dz, gz)

    twin = dev(tm + 1 - 2 * c, x)

    def ahead(me, step, n):
        return lax.rem(me + step, n)

    def send(src, dst, send_sem, recv_sem, device):
        copy = pltpu.make_async_remote_copy(
            src, dst, send_sem, recv_sem, device_id=device, device_id_type=MESH
        )
        copy.start()
        return copy

    mine = pl.ds(pl.multiple_of(c * half_w, HDIM), half_w)
    other = pl.ds(pl.multiple_of((1 - c) * half_w, HDIM), half_w)
    inputs = ((vk_ref, kin), (vv_ref, vin), (q_ref, qin), (tk_ref, tkin), (tv_ref, tvin))
    loads = [
        pltpu.make_async_copy(vk_ref, kin, in_sem.at[0]),
        pltpu.make_async_copy(vv_ref, vown, in_sem.at[1]),
        pltpu.make_async_copy(vv_ref.at[:, mine], vin.at[c], in_sem.at[5]),
    ] + [
        pltpu.make_async_copy(src.at[:, mine], dst.at[c], in_sem.at[i + 2])
        for i, (src, dst) in enumerate(inputs[2:])
    ]
    for load in loads:
        load.start()
    own_w = pltpu.make_async_copy(w_ref, w_all.at[yc, zc], w_sem)
    own_w.start()

    def far_first(n):
        return sorted(range(1, n), key=lambda step: -min(step, n - step))

    barrier = pltpu.get_barrier_semaphore()

    def greet(device):
        pl.semaphore_signal(barrier, inc=1, device_id=device, device_id_type=MESH)

    for step in far_first(nz):
        greet(z_dev(ahead(z, step, nz)))
    for step in far_first(ny):
        greet(y_dev(ahead(y, step, ny)))
    x_steps = [1, nx - 1] if nx > 2 else list(range(1, nx))
    for step in x_steps:
        greet(x_dev(ahead(x, step, nx)))
    greeted = 1 + (nz - 1) + (ny - 1) + len(x_steps)
    for dy, dz in offsets[1:]:
        greet(group_dev(dy, dz, 1 - c))
        greeted += 1
        if dy and dz:
            greet(group_dev(dy, dz, c))
            greeted += 1
    greet(twin)
    bin_[c] = jnp.full((8, HDIM), bound_ref[0], jnp.int32)

    loads[0].wait()
    kin[...] = elu_one(kin[...].astype(F32)).astype(BF16)
    loads[1].wait()
    ones = jnp.ones((NORM_ROWS, vlen), BF16)
    norm_row = lax.broadcasted_iota(jnp.int32, (NORM_ROWS, HDIM), 0)

    def own_state(core):
        norms = jnp.zeros((NORM_ROWS, HDIM), F32)
        states = []
        for h in range(heads):
            cols = pl.ds(pl.multiple_of(core * half_w + h * HDIM, HDIM), HDIM)
            feat = kin[:, cols]
            states.append(dot(feat, vown[:, cols], TN))
            norms = jnp.where(norm_row == h, dot(ones, feat, NN), norms)
        return states, norms

    states, norms = own_state(1 - c)
    for h in range(heads):
        for k in range(per_head):
            s_send[h * per_head + k] = states[h][k * srows : (k + 1) * srows].astype(BF16)
    n_send[...] = norms.astype(BF16)
    states, norms = own_state(c)
    for h in range(heads):
        for k in range(per_head):
            s_own[h * per_head + k] = states[h][k * srows : (k + 1) * srows]
    n_own[...] = norms
    kf[c] = kin[:, mine]
    pl.semaphore_wait(barrier, greeted)

    state_copy = send(s_send, s_recv, s_sem.at[0], s_sem.at[1], twin)
    norm_copy = send(n_send, n_recv, s_sem.at[2], s_sem.at[3], twin)
    def y_class(k):
        return y_dev(k * gy + py)

    def z_class(k):
        return z_dev(k * gz + pz)

    for step in far_first(mz):
        send(w_ref.at[0:wh], w_all.at[yc, zc, 0:wh], w1_send.at[0], w1_recv.at[0], z_class(ahead(zc, step, mz)))
    for step in far_first(my):
        send(w_ref.at[wh:wc], w_all.at[yc, zc, wh:wc], w1_send.at[1], w1_recv.at[1], y_class(ahead(yc, step, my)))

    state_copy.wait_recv()
    norm_copy.wait_recv()
    norms = (n_own[...] + n_recv[...].astype(F32)).astype(BF16)
    for k in range(nz):
        sbuf[k, 0:srows] = (s_own[k] + s_recv[k].astype(F32)).astype(BF16)
        sbuf[k, srows : srows + NORM_ROWS] = norms
    for step in far_first(nz):
        to = ahead(z, step, nz)
        send(sbuf.at[to], abuf.at[z], a_send, a_recv, z_dev(to))
    abuf[z] = sbuf[z]

    swaps = [send(kin.at[:, other], kf.at[c], c_send.at[0], c_recv.at[0], twin)]
    swaps += [
        send(src.at[:, other], dst.at[c], c_send.at[i + 1], c_recv.at[i + 1], twin)
        for i, (src, dst) in enumerate(inputs[1:])
    ]
    swaps.append(send(bin_.at[c], bin_.at[c], c_send.at[5], c_recv.at[5], twin))

    def bundle(half, index, q):
        if half == 0:
            return w_all.at[index, q * (mz // 2) : (q + 1) * (mz // 2), 0:wh]
        return w_all.at[q * (my // 2) : (q + 1) * (my // 2), index, wh:wc]

    laps = {}
    waited = set()

    def arrived(key):
        if key in laps and key not in waited:
            waited.add(key)
            laps[key].wait_recv()

    def lap(s, q):
        for half in range(2):
            for way in range(2):
                n, me = (my, yc) if half == 0 else (mz, zc)
                if s >= n // 2 or (s == n // 2 - 1 and q != way):
                    continue
                arrived((half, way, s - 1, q))
                block = ahead(me, n - s, n) if way == 0 else ahead(me, s, n)
                to = ahead(me, 1, n) if way == 0 else ahead(me, n - 1, n)
                part = bundle(half, block, q)
                laps[(half, way, s, q)] = send(
                    part, part, w2_send.at[half, way, s, q], w2_recv.at[half, way, s, q],
                    y_class(to) if half == 0 else z_class(to),
                )

    for load in loads[2:]:
        load.wait()
    for swap in swaps:
        swap.wait_recv()
    bounds = jnp.concatenate(
        [jnp.broadcast_to(bin_[0, 0:1, :], (rows, HDIM)), jnp.broadcast_to(bin_[1, 0:1, :], (rows, HDIM))]
    )
    row_ids = lax.broadcasted_iota(jnp.int32, (2 * rows, HDIM), 0)
    col_ids = lax.broadcasted_iota(jnp.int32, (2 * rows, HDIM), 1)

    def own_part(h):
        cols = slice(h * HDIM, (h + 1) * HDIM)
        query = qin[:, :, cols].reshape(2 * rows, HDIM)
        q_feat = elu_one(query.astype(F32)).astype(BF16)
        qf[h] = q_feat
        numer = jnp.zeros((2 * rows, HDIM), F32)
        denom = jnp.zeros((2 * rows, 1), F32)
        for e in range(2):
            weight = dot(q_feat, kf[e, :, cols], NT)
            weight = jnp.where(col_ids + (chip * 2 + e) * vlen < bounds, weight, 0.0)
            high, low = split(weight)
            values = vin[e, :, cols]
            numer = numer + dot(high, values, NN) + dot(low, values, NN)
            denom = denom + jnp.sum(weight, axis=1, keepdims=True)
        numer_l[h] = numer
        denom_l[h] = jnp.broadcast_to(denom, (2 * rows, HDIM))
        scores = dot(query, tkin[:, :, cols].reshape(2 * rows, HDIM), NT) * (float(HDIM) ** -0.5)
        causal = jnp.logical_and(col_ids <= row_ids, col_ids // rows == row_ids // rows)
        scores = jnp.where(causal, scores, -jnp.inf)
        expo = jnp.exp(scores - jnp.max(scores, axis=1, keepdims=True))
        probs = (expo / jnp.sum(expo, axis=1, keepdims=True)).astype(BF16)
        local_o[h] = dot(probs, tvin[:, :, cols].reshape(2 * rows, HDIM), NN)

    own_part(0)

    wait_bytes(abuf.at[0 : nz - 1], a_recv)
    total = jnp.zeros((srows + NORM_ROWS, HDIM), F32)
    for k in range(nz):
        rbuf[k] = total
        total = total + abuf[k].astype(F32)
    tsend[...] = total.astype(BF16)
    for step in range(1, ny):

        @pl.when(y + step < ny)
        def _():
            send(tsend, tbuf.at[y], t_send.at[step], t_recv.at[y], y_dev(y + step))

    own_w.wait()
    if mz > 1:
        wait_bytes(w_all.at[0, 0 : mz - 1, 0:wh], w1_recv.at[0])
    if my > 1:
        wait_bytes(w_all.at[0 : my - 1, 0, wh:wc], w1_recv.at[1])
    steps = max(my, mz) // 2
    if steps:
        lap(0, 0)
        lap(0, 1)

    for h in range(1, max(1, heads - 1)):
        own_part(h)

    base[...] = jnp.zeros_like(base)
    for k in range(ny - 1):

        @pl.when(k < y)
        def _():
            wait_bytes(tbuf.at[k], t_recv.at[k])
            base[...] += tbuf[k].astype(F32)

    for k in range(nz):
        pbuf[k] = (base[0:srows] + rbuf[k, 0:srows]).astype(BF16)
    pfx[z] = pbuf[z]
    for step in far_first(nz):
        to = ahead(z, step, nz)
        send(pbuf.at[to], pfx.at[z], p_send, p_recv, z_dev(to))
    norm_high, norm_low = split(base[srows : srows + NORM_ROWS] + rbuf[z, srows : srows + NORM_ROWS])

    for h in range(max(1, heads - 1), heads):
        own_part(h)

    wait_bytes(pfx.at[0 : nz - 1], p_recv)
    for s in range(1, steps):
        lap(s, 0)
        lap(s, 1)

    def retrieve(h):
        query = qf[h]
        first = h * per_head
        state = pfx[first : first + per_head].reshape(HDIM, HDIM)
        numer = numer_l[h] + dot(query, state, NN)
        denom = (dot(query, norm_high, NT) + dot(query, norm_low, NT))[:, h : h + 1] + denom_l[h]
        gate = 1.0 / (1.0 + jnp.exp(-jnp.full((8, HDIM), gate_ref[c * heads + h], F32)))[0:1]
        value = gate * (numer / denom) + (1.0 - gate) * local_o[h]
        mixed[own_class, c * heads + h] = value.astype(BF16)

    split_n = 2 if heads > 1 else 1

    def mixed_part(cls, i):
        return mixed.at[cls, pl.ds(c * heads + i * (heads // split_n), heads // split_n)]

    group_copies, twin_copies = {}, {}
    for i in range(split_n):
        for h in range(i * heads // split_n, (i + 1) * heads // split_n):
            retrieve(h)
        part = mixed_part(own_class, i)
        for r, (dy, dz) in reversed(list(enumerate(offsets))):
            if r == 0:
                twin_copies[r, i] = send(part, part, m_send.at[r, i], m_recv.at[r, i], twin)
            else:
                group_copies[r, i] = send(part, part, g_send.at[r, i], g_recv.at[r, i], group_dev(dy, dz, c))
    state_copy.wait_send()
    norm_copy.wait_send()
    for copy in swaps:
        copy.wait_send()
    if mz > 1:
        wait_bytes(w_all.at[0, 0 : mz - 1, 0:wh], w1_send.at[0])
    if my > 1:
        wait_bytes(w_all.at[0 : my - 1, 0, wh:wc], w1_send.at[1])
    wait_bytes(sbuf.at[0 : nz - 1], a_send)
    for step in range(1, ny):

        @pl.when(y + step < ny)
        def _():
            wait_bytes(tsend, t_send.at[step])

    wait_bytes(pbuf.at[0 : nz - 1], p_send)
    for key in list(laps):
        arrived(key)
    for copy in laps.values():
        copy.wait_send()

    yx = my // nx

    def project(cls, xxs):
        both = jnp.concatenate([mixed[cls, h] for h in range(2 * heads)], axis=1)
        block = jnp.concatenate([w_all[pl.ds(xx * yx, yx)].reshape(yx * mz * wc, width) for xx in xxs])
        value = dot(both, block, NT)
        return [value[:, i * HDIM : (i + 1) * HDIM] for i in range(len(xxs))]

    far_copies, dir_copies, fwd_copies = [], [], []

    def forward(r):
        to = ahead(x, 1 if r % 2 == 0 else nx - 1, nx)
        far_copies[r].wait_recv()
        fwd_send[r] = (sum_fwd[r] + far_recv[r].astype(F32)).astype(BF16)
        fwd_copies.append(send(fwd_send.at[r], fwd_recv.at[r], x_send.at[r, 2], x_recv.at[r, 2], x_dev(to)))

    def hand_over(r):
        for i in range(split_n):
            group_copies[r, i].wait_recv()
            part = mixed_part(class_of(*offsets[r]), i)
            twin_copies[r, i] = send(part, part, m_send.at[r, i], m_recv.at[r, i], twin)

    for r, (dy, dz) in enumerate(offsets):
        cls = class_of(dy, dz)
        for i in range(split_n):
            twin_copies[r, i].wait_recv()
        if nx == 4:
            near, away = (1, 3) if r % 2 == 0 else (3, 1)
            far, direct = project(cls, [ahead(x, 2, nx), ahead(x, away, nx)])
            far_send[r] = far.astype(BF16)
            far_copies.append(
                send(far_send.at[r], far_recv.at[r], x_send.at[r, 0], x_recv.at[r, 0], x_dev(ahead(x, near, nx)))
            )
            dir_send[r] = direct.astype(BF16)
            dir_copies.append(
                send(dir_send.at[r], dir_recv.at[r], x_send.at[r, 1], x_recv.at[r, 1], x_dev(ahead(x, away, nx)))
            )
            sum_fwd[r], sum_own[r] = project(cls, [ahead(x, near, nx), x])
            if r > 0:
                forward(r - 1)
        elif nx == 2:
            direct, sum_own[r] = project(cls, [1 - x, x])
            dir_send[r] = direct.astype(BF16)
            dir_copies.append(
                send(dir_send.at[r], dir_recv.at[r], x_send.at[r, 1], x_recv.at[r, 1], x_dev(1 - x))
            )
        else:
            (sum_own[r],) = project(cls, [x])
        for later in {0: (1, 2), 1: (3,)}.get(r, ()):
            if later < len(offsets):
                hand_over(later)
    if nx == 4:
        forward(len(offsets) - 1)

    done_copies = []
    for r, (dy, dz) in enumerate(offsets):
        total = sum_own[r]
        for copies, landed in ((dir_copies, dir_recv), (fwd_copies, fwd_recv)):
            if copies:
                copies[r].wait_recv()
                total = total + landed[r].astype(F32)
        total = total.astype(BF16)
        for e in range(2):
            dsend[r, e] = total[e * rows : (e + 1) * rows]
        place = fin.at[own_class * 2 + c]
        if r == 0:
            fin[own_class * 2 + c] = dsend[0, c]
            done_copies.append(send(dsend.at[0, 1 - c], place, d_send, d_recv, twin))
        else:
            for e in range(2):
                done_copies.append(send(dsend.at[r, e], place, d_send, d_recv, group_dev(dy, dz, e)))
    wait_bytes(fin.at[0 : len(done_copies)], d_recv)

    lane = lax.broadcasted_iota(jnp.int32, (rows, HDIM), 1)
    runs = HDIM // wc
    for b in range(out_ref.shape[1] // HDIM):
        value = jnp.zeros((rows, HDIM), F32)
        for k in range(runs):
            shard, e = divmod(b * runs + k, 2)
            yl, zz = divmod(shard, nz)
            pos = ((yl // gy) * mz + zz // gz) * wc
            piece = fin[((yl % gy) * gz + zz % gz) * 2 + e].astype(F32)
            shift = (k * wc - pos) % HDIM
            if shift:
                piece = pltpu.roll(piece, shift, 1)
            value = jnp.where(lane // wc == k, piece, value)
        out_ref[:, b * HDIM : (b + 1) * HDIM] = value.astype(BF16)

    for copies in (twin_copies.values(), group_copies.values(), far_copies, dir_copies, fwd_copies):
        for copy in copies:
            copy.wait_send()
    wait_bytes(fin.at[0 : len(done_copies)], d_send)


def local(grid, vk, vv, q, tk, tv, bounds, gate, w):
    ny, nz, nx, gy, gz = grid
    vlen, width = vk.shape
    rows = q.shape[0]
    half_w = width // 2
    heads = half_w // HDIM
    srows = half_w // nz
    wt = w.T
    wc = wt.shape[0]
    my, mz = ny // gy, nz // gz
    n = gy * gz
    assert (my // nx) * mz * wc == HDIM
    steps = max(my, mz, 2) // 2
    hbm = pl.BlockSpec(memory_space=pltpu.HBM)
    smem = pl.BlockSpec(memory_space=pltpu.SMEM)
    dma = pltpu.SemaphoreType.DMA
    slices = (nz, srows + NORM_ROWS, HDIM)
    states = (nz, srows, HDIM)
    per_head = (heads, 2 * rows, HDIM)
    blocks = (n, 2 * rows, HDIM)
    return pl.pallas_call(
        functools.partial(kernel, ny, nz, nx, gy, gz),
        out_shape=jax.ShapeDtypeStruct((rows, 2 * n * HDIM), BF16),
        in_specs=[smem, smem] + [hbm] * 6,
        out_specs=pl.BlockSpec(memory_space=pltpu.VMEM),
        scratch_shapes=[
            pltpu.VMEM((my, mz, wc, width), BF16),
            pltpu.VMEM((vlen, width), BF16),
            pltpu.VMEM((vlen, width), BF16),
            pltpu.VMEM((2, vlen, half_w), BF16),
            pltpu.VMEM((2, rows, half_w), BF16),
            pltpu.VMEM((2, rows, half_w), BF16),
            pltpu.VMEM((2, rows, half_w), BF16),
            pltpu.VMEM((2, 8, HDIM), jnp.int32),
            pltpu.VMEM((2, vlen, half_w), BF16),
            pltpu.VMEM(per_head, BF16),
            pltpu.VMEM(states, BF16),
            pltpu.VMEM(states, BF16),
            pltpu.VMEM(states, F32),
            pltpu.VMEM((NORM_ROWS, HDIM), BF16),
            pltpu.VMEM((NORM_ROWS, HDIM), BF16),
            pltpu.VMEM((NORM_ROWS, HDIM), F32),
            pltpu.VMEM(slices, BF16),
            pltpu.VMEM(slices, BF16),
            pltpu.VMEM(slices, F32),
            pltpu.VMEM((ny, srows + NORM_ROWS, HDIM), BF16),
            pltpu.VMEM((srows + NORM_ROWS, HDIM), BF16),
            pltpu.VMEM((srows + NORM_ROWS, HDIM), F32),
            pltpu.VMEM(states, BF16),
            pltpu.VMEM(states, BF16),
            pltpu.VMEM(per_head, F32),
            pltpu.VMEM(per_head, F32),
            pltpu.VMEM(per_head, F32),
            pltpu.VMEM((n, 2 * heads, 2 * rows, HDIM), BF16),
            pltpu.VMEM(blocks, BF16),
            pltpu.VMEM(blocks, BF16),
            pltpu.VMEM(blocks, BF16),
            pltpu.VMEM(blocks, BF16),
            pltpu.VMEM(blocks, F32),
            pltpu.VMEM(blocks, F32),
            pltpu.VMEM(blocks, BF16),
            pltpu.VMEM(blocks, BF16),
            pltpu.VMEM((n, 2, rows, HDIM), BF16),
            pltpu.VMEM((2 * n, rows, HDIM), BF16),
            dma((6,)),
            dma((4,)),
            dma,
            dma((6,)),
            dma((6,)),
            dma((2,)),
            dma((2,)),
            dma((2, 2, steps, 2)),
            dma((2, 2, steps, 2)),
            dma,
            dma,
            dma((ny,)),
            dma((ny,)),
            dma,
            dma,
            dma((n, 2)),
            dma((n, 2)),
            dma((n, 2)),
            dma((n, 2)),
            dma((n, 3)),
            dma((n, 3)),
            dma,
            dma,
        ],
        compiler_params=pltpu.CompilerParams(
            collective_id=0, has_side_effects=True, vmem_limit_bytes=60 * 1024 * 1024
        ),
    )(bounds, gate, vk, vv, q, tk, tv, wt)


def solution(mesh):
    nx = mesh.shape["head"]
    specs = (
        P("tm", "head"),
        P("tm", "head"),
        P("tm", "head"),
        P("tm", "head"),
        P("tm", "head"),
        P("tm"),
        P("head"),
        P("head", "tm"),
    )
    return jax.shard_map(
        functools.partial(local, (8, mesh.shape["tm"] // 16, nx, 2, 2)),
        mesh=mesh,
        in_specs=specs,
        out_specs=P("tm", "head"),
        check_vma=False,
    )
```

```python
import functools

import jax
import jax.numpy as jnp
from jax import lax
from jax.experimental import pallas as pl
from jax.experimental.pallas import tpu as pltpu
from jax.sharding import PartitionSpec as P

MESH = pl.DeviceIdType.MESH
F32 = jnp.float32
BF16 = jnp.bfloat16
HDIM = 128
NORM_ROWS = 16
NN = (((1,), (0,)), ((), ()))
NT = (((1,), (1,)), ((), ()))
TN = (((0,), (0,)), ((), ()))


def dot(a, b, dims):
    return lax.dot_general(a, b, dims, preferred_element_type=F32)


def elu_one(values):
    return jnp.where(values > 0, values + 1.0, jnp.exp(jnp.minimum(values, 0.0)))


def split(value):
    high = value.astype(BF16)
    return high, (value - high.astype(F32)).astype(BF16)


def wait_bytes(ref, sem):
    pltpu.make_async_copy(ref, ref, sem).wait()


def kernel(
    ny,
    nz,
    nx,
    gy,
    gz,
    bound_ref,
    gate_ref,
    vk_ref,
    vv_ref,
    q_ref,
    tk_ref,
    tv_ref,
    w_ref,
    out_ref,
    w_all,
    kin,
    vown,
    vin,
    qin,
    tkin,
    tvin,
    bin_,
    kf,
    qf,
    s_send,
    s_recv,
    s_own,
    n_send,
    n_recv,
    n_own,
    sbuf,
    abuf,
    rbuf,
    tbuf,
    tsend,
    base,
    pbuf,
    pfx,
    numer_l,
    denom_l,
    local_o,
    mixed,
    far_send,
    far_recv,
    dir_send,
    dir_recv,
    sum_own,
    sum_fwd,
    fwd_send,
    fwd_recv,
    dsend,
    fin,
    in_sem,
    s_sem,
    w_sem,
    c_send,
    c_recv,
    w1_send,
    w1_recv,
    w2_send,
    w2_recv,
    a_send,
    a_recv,
    t_send,
    t_recv,
    p_send,
    p_recv,
    g_send,
    g_recv,
    m_send,
    m_recv,
    x_send,
    x_recv,
    d_send,
    d_recv,
):
    tm = lax.axis_index("tm")
    x = lax.axis_index("head")
    c = lax.rem(tm, 2)
    chip = tm // 2
    z = lax.rem(chip, nz)
    y = chip // nz

    vlen, width = vk_ref.shape
    rows = q_ref.shape[0]
    half_w = width // 2
    heads = half_w // HDIM
    per_head = nz // heads
    srows = HDIM // per_head
    wc = w_ref.shape[0]
    wk = width * 5 // 8 // HDIM * HDIM
    my, mz = ny // gy, nz // gz
    py, pz = lax.rem(y, gy), lax.rem(z, gz)
    yc, zc = y // gy, z // gz
    own_class = py * gz + pz
    offsets = [(dy, dz) for dy in range(gy) for dz in range(gz)]
    offsets.sort(key=lambda o: (o[0] + o[1], o[1]))

    def dev(t, xx):
        return {"tm": t, "head": xx}

    def y_dev(yy):
        return dev((yy * nz + z) * 2 + c, x)

    def z_dev(zz):
        return dev((y * nz + zz) * 2 + c, x)

    def x_dev(xx):
        return dev(tm, xx)

    def group_dev(dy, dz, core):
        yy = yc * gy + lax.rem(py + dy, gy)
        zz = zc * gz + lax.rem(pz + dz, gz)
        return dev((yy * nz + zz) * 2 + core, x)

    def class_of(dy, dz):
        return lax.rem(py + dy, gy) * gz + lax.rem(pz + dz, gz)

    twin = dev(tm + 1 - 2 * c, x)

    def ahead(me, step, n):
        return lax.rem(me + step, n)

    def send(src, dst, send_sem, recv_sem, device):
        copy = pltpu.make_async_remote_copy(
            src, dst, send_sem, recv_sem, device_id=device, device_id_type=MESH
        )
        copy.start()
        return copy

    mine = pl.ds(pl.multiple_of(c * half_w, HDIM), half_w)
    other = pl.ds(pl.multiple_of((1 - c) * half_w, HDIM), half_w)
    inputs = ((vk_ref, kin), (vv_ref, vin), (q_ref, qin), (tk_ref, tkin), (tv_ref, tvin))
    loads = [
        pltpu.make_async_copy(vk_ref, kin, in_sem.at[0]),
        pltpu.make_async_copy(vv_ref, vown, in_sem.at[1]),
        pltpu.make_async_copy(vv_ref.at[:, mine], vin.at[c], in_sem.at[5]),
    ] + [
        pltpu.make_async_copy(src.at[:, mine], dst.at[c], in_sem.at[i + 2])
        for i, (src, dst) in enumerate(inputs[2:])
    ]
    for load in loads:
        load.start()
    own_w = pltpu.make_async_copy(w_ref, w_all.at[yc, zc], w_sem)
    own_w.start()

    def far_first(n):
        return sorted(range(1, n), key=lambda step: -min(step, n - step))

    barrier = pltpu.get_barrier_semaphore()

    def greet(device):
        pl.semaphore_signal(barrier, inc=1, device_id=device, device_id_type=MESH)

    for step in far_first(nz):
        greet(z_dev(ahead(z, step, nz)))
    for step in far_first(ny):
        greet(y_dev(ahead(y, step, ny)))
    x_steps = [1, nx - 1] if nx > 2 else list(range(1, nx))
    for step in x_steps:
        greet(x_dev(ahead(x, step, nx)))
    greeted = 1 + (nz - 1) + (ny - 1) + len(x_steps)
    for dy, dz in offsets[1:]:
        greet(group_dev(dy, dz, 1 - c))
        greeted += 1
        if dy and dz:
            greet(group_dev(dy, dz, c))
            greeted += 1
    greet(twin)
    bin_[c] = jnp.full((8, HDIM), bound_ref[0], jnp.int32)

    loads[0].wait()
    kin[...] = elu_one(kin[...].astype(F32)).astype(BF16)
    loads[1].wait()
    ones = jnp.ones((NORM_ROWS, vlen), BF16)
    norm_row = lax.broadcasted_iota(jnp.int32, (NORM_ROWS, HDIM), 0)

    def own_state(core):
        norms = jnp.zeros((NORM_ROWS, HDIM), F32)
        states = []
        for h in range(heads):
            cols = pl.ds(pl.multiple_of(core * half_w + h * HDIM, HDIM), HDIM)
            feat = kin[:, cols]
            states.append(dot(feat, vown[:, cols], TN))
            norms = jnp.where(norm_row == h, dot(ones, feat, NN), norms)
        return states, norms

    states, norms = own_state(1 - c)
    for h in range(heads):
        for k in range(per_head):
            s_send[h * per_head + k] = states[h][k * srows : (k + 1) * srows].astype(BF16)
    n_send[...] = norms.astype(BF16)
    states, norms = own_state(c)
    for h in range(heads):
        for k in range(per_head):
            s_own[h * per_head + k] = states[h][k * srows : (k + 1) * srows]
    n_own[...] = norms
    kf[c] = kin[:, mine]
    pl.semaphore_wait(barrier, greeted)

    state_copy = send(s_send, s_recv, s_sem.at[0], s_sem.at[1], twin)
    norm_copy = send(n_send, n_recv, s_sem.at[2], s_sem.at[3], twin)
    def y_class(k):
        return y_dev(k * gy + py)

    def z_class(k):
        return z_dev(k * gz + pz)

    for step in far_first(mz):
        send(w_ref.at[:, 0:wk], w_all.at[yc, zc, :, 0:wk], w1_send.at[0], w1_recv.at[0], z_class(ahead(zc, step, mz)))
    for step in far_first(my):
        send(w_ref.at[:, wk:width], w_all.at[yc, zc, :, wk:width], w1_send.at[1], w1_recv.at[1], y_class(ahead(yc, step, my)))

    state_copy.wait_recv()
    norm_copy.wait_recv()
    norms = (n_own[...] + n_recv[...].astype(F32)).astype(BF16)
    for k in range(nz):
        sbuf[k, 0:srows] = (s_own[k] + s_recv[k].astype(F32)).astype(BF16)
        sbuf[k, srows : srows + NORM_ROWS] = norms
    for step in far_first(nz):
        to = ahead(z, step, nz)
        send(sbuf.at[to], abuf.at[z], a_send, a_recv, z_dev(to))
    abuf[z] = sbuf[z]

    swaps = [send(kin.at[:, other], kf.at[c], c_send.at[0], c_recv.at[0], twin)]
    swaps += [
        send(src.at[:, other], dst.at[c], c_send.at[i + 1], c_recv.at[i + 1], twin)
        for i, (src, dst) in enumerate(inputs[1:])
    ]
    swaps.append(send(bin_.at[c], bin_.at[c], c_send.at[5], c_recv.at[5], twin))

    def bundle(half, index, q):
        if half == 0:
            return w_all.at[index, q * (mz // 2) : (q + 1) * (mz // 2), :, 0:wk]
        return w_all.at[q * (my // 2) : (q + 1) * (my // 2), index, :, wk:width]

    laps = {}
    waited = set()

    def arrived(key):
        if key in laps and key not in waited:
            waited.add(key)
            laps[key].wait_recv()

    def lap(s, q):
        for half in range(2):
            for way in range(2):
                n, me = (my, yc) if half == 0 else (mz, zc)
                if s >= n // 2 or (s == n // 2 - 1 and q != way):
                    continue
                arrived((half, way, s - 1, q))
                block = ahead(me, n - s, n) if way == 0 else ahead(me, s, n)
                to = ahead(me, 1, n) if way == 0 else ahead(me, n - 1, n)
                part = bundle(half, block, q)
                laps[(half, way, s, q)] = send(
                    part, part, w2_send.at[half, way, s, q], w2_recv.at[half, way, s, q],
                    y_class(to) if half == 0 else z_class(to),
                )

    for load in loads[2:]:
        load.wait()
    for swap in swaps:
        swap.wait_recv()
    bounds = jnp.concatenate(
        [jnp.broadcast_to(bin_[0, 0:1, :], (rows, HDIM)), jnp.broadcast_to(bin_[1, 0:1, :], (rows, HDIM))]
    )
    row_ids = lax.broadcasted_iota(jnp.int32, (2 * rows, HDIM), 0)
    col_ids = lax.broadcasted_iota(jnp.int32, (2 * rows, HDIM), 1)

    def own_part(h):
        cols = slice(h * HDIM, (h + 1) * HDIM)
        query = qin[:, :, cols].reshape(2 * rows, HDIM)
        q_feat = elu_one(query.astype(F32)).astype(BF16)
        qf[h] = q_feat
        numer = jnp.zeros((2 * rows, HDIM), F32)
        denom = jnp.zeros((2 * rows, 1), F32)
        for e in range(2):
            weight = dot(q_feat, kf[e, :, cols], NT)
            weight = jnp.where(col_ids + (chip * 2 + e) * vlen < bounds, weight, 0.0)
            high, low = split(weight)
            values = vin[e, :, cols]
            numer = numer + dot(high, values, NN) + dot(low, values, NN)
            denom = denom + jnp.sum(weight, axis=1, keepdims=True)
        numer_l[h] = numer
        denom_l[h] = jnp.broadcast_to(denom, (2 * rows, HDIM))
        scores = dot(query, tkin[:, :, cols].reshape(2 * rows, HDIM), NT) * (float(HDIM) ** -0.5)
        causal = jnp.logical_and(col_ids <= row_ids, col_ids // rows == row_ids // rows)
        scores = jnp.where(causal, scores, -jnp.inf)
        expo = jnp.exp(scores - jnp.max(scores, axis=1, keepdims=True))
        probs = (expo / jnp.sum(expo, axis=1, keepdims=True)).astype(BF16)
        local_o[h] = dot(probs, tvin[:, :, cols].reshape(2 * rows, HDIM), NN)

    own_part(0)

    wait_bytes(abuf.at[0 : nz - 1], a_recv)
    total = jnp.zeros((srows + NORM_ROWS, HDIM), F32)
    for k in range(nz):
        rbuf[k] = total
        total = total + abuf[k].astype(F32)
    tsend[...] = total.astype(BF16)
    for step in range(1, ny):

        @pl.when(y + step < ny)
        def _():
            send(tsend, tbuf.at[y], t_send.at[step], t_recv.at[y], y_dev(y + step))

    own_w.wait()
    if mz > 1:
        wait_bytes(w_all.at[0, 0 : mz - 1, :, 0:wk], w1_recv.at[0])
    if my > 1:
        wait_bytes(w_all.at[0 : my - 1, 0, :, wk:width], w1_recv.at[1])
    steps = max(my, mz) // 2
    if steps:
        lap(0, 0)
        lap(0, 1)

    for h in range(1, max(1, heads - 1)):
        own_part(h)

    base[...] = jnp.zeros_like(base)
    for k in range(ny - 1):

        @pl.when(k < y)
        def _():
            wait_bytes(tbuf.at[k], t_recv.at[k])
            base[...] += tbuf[k].astype(F32)

    for k in range(nz):
        pbuf[k] = (base[0:srows] + rbuf[k, 0:srows]).astype(BF16)
    pfx[z] = pbuf[z]
    for step in far_first(nz):
        to = ahead(z, step, nz)
        send(pbuf.at[to], pfx.at[z], p_send, p_recv, z_dev(to))
    norm_high, norm_low = split(base[srows : srows + NORM_ROWS] + rbuf[z, srows : srows + NORM_ROWS])

    for h in range(max(1, heads - 1), heads):
        own_part(h)

    wait_bytes(pfx.at[0 : nz - 1], p_recv)
    for s in range(1, steps):
        lap(s, 0)
        lap(s, 1)

    def retrieve(h):
        query = qf[h]
        first = h * per_head
        state = pfx[first : first + per_head].reshape(HDIM, HDIM)
        numer = numer_l[h] + dot(query, state, NN)
        denom = (dot(query, norm_high, NT) + dot(query, norm_low, NT))[:, h : h + 1] + denom_l[h]
        gate = 1.0 / (1.0 + jnp.exp(-jnp.full((8, HDIM), gate_ref[c * heads + h], F32)))[0:1]
        value = gate * (numer / denom) + (1.0 - gate) * local_o[h]
        mixed[own_class, c * heads + h] = value.astype(BF16)

    split_n = 2 if heads > 1 else 1

    def mixed_part(cls, i):
        return mixed.at[cls, pl.ds(c * heads + i * (heads // split_n), heads // split_n)]

    group_copies, twin_copies = {}, {}
    for i in range(split_n):
        for h in range(i * heads // split_n, (i + 1) * heads // split_n):
            retrieve(h)
        part = mixed_part(own_class, i)
        for r, (dy, dz) in reversed(list(enumerate(offsets))):
            if r == 0:
                twin_copies[r, i] = send(part, part, m_send.at[r, i], m_recv.at[r, i], twin)
            elif r < 3:
                group_copies[r, i] = send(part, part, g_send.at[r, i], g_recv.at[r, i], group_dev(dy, dz, c))
    state_copy.wait_send()
    norm_copy.wait_send()
    for copy in swaps:
        copy.wait_send()
    if mz > 1:
        wait_bytes(w_all.at[0, 0 : mz - 1, :, 0:wk], w1_send.at[0])
    if my > 1:
        wait_bytes(w_all.at[0 : my - 1, 0, :, wk:width], w1_send.at[1])
    wait_bytes(sbuf.at[0 : nz - 1], a_send)
    for step in range(1, ny):

        @pl.when(y + step < ny)
        def _():
            wait_bytes(tsend, t_send.at[step])

    wait_bytes(pbuf.at[0 : nz - 1], p_send)
    for key in list(laps):
        arrived(key)
    for copy in laps.values():
        copy.wait_send()

    yx = my // nx

    def project(cls, xxs):
        both = jnp.concatenate([mixed[cls, h] for h in range(2 * heads)], axis=1)
        block = jnp.concatenate([w_all[pl.ds(xx * yx, yx)].reshape(yx * mz * wc, width) for xx in xxs])
        value = dot(both, block, NT)
        return [value[:, i * HDIM : (i + 1) * HDIM] for i in range(len(xxs))]

    far_copies, dir_copies, fwd_copies = [], [], []

    def forward(r):
        to = ahead(x, 1 if r % 2 == 0 else nx - 1, nx)
        far_copies[r].wait_recv()
        fwd_send[r] = (sum_fwd[r] + far_recv[r].astype(F32)).astype(BF16)
        fwd_copies.append(send(fwd_send.at[r], fwd_recv.at[r], x_send.at[r, 2], x_recv.at[r, 2], x_dev(to)))

    def hand_over(r):
        for i in range(split_n):
            part = mixed_part(class_of(*offsets[r]), i)
            group_copies[r, i].wait_recv()
            if len(offsets) == 4 and r == i + 1:
                group_copies[3, i] = send(
                    part, part, g_send.at[3, i], g_recv.at[3, i], group_dev(*offsets[2 - i], c)
                )
            twin_copies[r, i] = send(part, part, m_send.at[r, i], m_recv.at[r, i], twin)

    for r, (dy, dz) in enumerate(offsets):
        cls = class_of(dy, dz)
        for i in range(split_n):
            twin_copies[r, i].wait_recv()
        if nx == 4:
            near, away = (1, 3) if r % 2 == 0 else (3, 1)
            far, direct = project(cls, [ahead(x, 2, nx), ahead(x, away, nx)])
            far_send[r] = far.astype(BF16)
            far_copies.append(
                send(far_send.at[r], far_recv.at[r], x_send.at[r, 0], x_recv.at[r, 0], x_dev(ahead(x, near, nx)))
            )
            dir_send[r] = direct.astype(BF16)
            dir_copies.append(
                send(dir_send.at[r], dir_recv.at[r], x_send.at[r, 1], x_recv.at[r, 1], x_dev(ahead(x, away, nx)))
            )
            sum_fwd[r], sum_own[r] = project(cls, [ahead(x, near, nx), x])
            if r > 0:
                forward(r - 1)
        elif nx == 2:
            direct, sum_own[r] = project(cls, [1 - x, x])
            dir_send[r] = direct.astype(BF16)
            dir_copies.append(
                send(dir_send.at[r], dir_recv.at[r], x_send.at[r, 1], x_recv.at[r, 1], x_dev(1 - x))
            )
        else:
            (sum_own[r],) = project(cls, [x])
        for later in {0: (1, 2), 1: (3,)}.get(r, ()):
            if later < len(offsets):
                hand_over(later)
    if nx == 4:
        forward(len(offsets) - 1)

    done_copies = []
    for r, (dy, dz) in enumerate(offsets):
        total = sum_own[r]
        for copies, landed in ((dir_copies, dir_recv), (fwd_copies, fwd_recv)):
            if copies:
                copies[r].wait_recv()
                total = total + landed[r].astype(F32)
        total = total.astype(BF16)
        for e in range(2):
            dsend[r, e] = total[e * rows : (e + 1) * rows]
        place = fin.at[own_class * 2 + c]
        if r == 0:
            fin[own_class * 2 + c] = dsend[0, c]
            done_copies.append(send(dsend.at[0, 1 - c], place, d_send, d_recv, twin))
        else:
            for e in range(2):
                done_copies.append(send(dsend.at[r, e], place, d_send, d_recv, group_dev(dy, dz, e)))
    wait_bytes(fin.at[0 : len(done_copies)], d_recv)

    lane = lax.broadcasted_iota(jnp.int32, (rows, HDIM), 1)
    runs = HDIM // wc
    for b in range(out_ref.shape[1] // HDIM):
        value = jnp.zeros((rows, HDIM), F32)
        for k in range(runs):
            shard, e = divmod(b * runs + k, 2)
            yl, zz = divmod(shard, nz)
            pos = ((yl // gy) * mz + zz // gz) * wc
            piece = fin[((yl % gy) * gz + zz % gz) * 2 + e].astype(F32)
            shift = (k * wc - pos) % HDIM
            if shift:
                piece = pltpu.roll(piece, shift, 1)
            value = jnp.where(lane // wc == k, piece, value)
        out_ref[:, b * HDIM : (b + 1) * HDIM] = value.astype(BF16)

    for copies in (twin_copies.values(), group_copies.values(), far_copies, dir_copies, fwd_copies):
        for copy in copies:
            copy.wait_send()
    wait_bytes(fin.at[0 : len(done_copies)], d_send)


def local(grid, vk, vv, q, tk, tv, bounds, gate, w):
    ny, nz, nx, gy, gz = grid
    vlen, width = vk.shape
    rows = q.shape[0]
    half_w = width // 2
    heads = half_w // HDIM
    srows = half_w // nz
    wt = w.T
    wc = wt.shape[0]
    my, mz = ny // gy, nz // gz
    n = gy * gz
    assert (my // nx) * mz * wc == HDIM
    steps = max(my, mz, 2) // 2
    hbm = pl.BlockSpec(memory_space=pltpu.HBM)
    smem = pl.BlockSpec(memory_space=pltpu.SMEM)
    dma = pltpu.SemaphoreType.DMA
    slices = (nz, srows + NORM_ROWS, HDIM)
    states = (nz, srows, HDIM)
    per_head = (heads, 2 * rows, HDIM)
    blocks = (n, 2 * rows, HDIM)
    return pl.pallas_call(
        functools.partial(kernel, ny, nz, nx, gy, gz),
        out_shape=jax.ShapeDtypeStruct((rows, 2 * n * HDIM), BF16),
        in_specs=[smem, smem] + [hbm] * 6,
        out_specs=pl.BlockSpec(memory_space=pltpu.VMEM),
        scratch_shapes=[
            pltpu.VMEM((my, mz, wc, width), BF16),
            pltpu.VMEM((vlen, width), BF16),
            pltpu.VMEM((vlen, width), BF16),
            pltpu.VMEM((2, vlen, half_w), BF16),
            pltpu.VMEM((2, rows, half_w), BF16),
            pltpu.VMEM((2, rows, half_w), BF16),
            pltpu.VMEM((2, rows, half_w), BF16),
            pltpu.VMEM((2, 8, HDIM), jnp.int32),
            pltpu.VMEM((2, vlen, half_w), BF16),
            pltpu.VMEM(per_head, BF16),
            pltpu.VMEM(states, BF16),
            pltpu.VMEM(states, BF16),
            pltpu.VMEM(states, F32),
            pltpu.VMEM((NORM_ROWS, HDIM), BF16),
            pltpu.VMEM((NORM_ROWS, HDIM), BF16),
            pltpu.VMEM((NORM_ROWS, HDIM), F32),
            pltpu.VMEM(slices, BF16),
            pltpu.VMEM(slices, BF16),
            pltpu.VMEM(slices, F32),
            pltpu.VMEM((ny, srows + NORM_ROWS, HDIM), BF16),
            pltpu.VMEM((srows + NORM_ROWS, HDIM), BF16),
            pltpu.VMEM((srows + NORM_ROWS, HDIM), F32),
            pltpu.VMEM(states, BF16),
            pltpu.VMEM(states, BF16),
            pltpu.VMEM(per_head, F32),
            pltpu.VMEM(per_head, F32),
            pltpu.VMEM(per_head, F32),
            pltpu.VMEM((n, 2 * heads, 2 * rows, HDIM), BF16),
            pltpu.VMEM(blocks, BF16),
            pltpu.VMEM(blocks, BF16),
            pltpu.VMEM(blocks, BF16),
            pltpu.VMEM(blocks, BF16),
            pltpu.VMEM(blocks, F32),
            pltpu.VMEM(blocks, F32),
            pltpu.VMEM(blocks, BF16),
            pltpu.VMEM(blocks, BF16),
            pltpu.VMEM((n, 2, rows, HDIM), BF16),
            pltpu.VMEM((2 * n, rows, HDIM), BF16),
            dma((6,)),
            dma((4,)),
            dma,
            dma((6,)),
            dma((6,)),
            dma((2,)),
            dma((2,)),
            dma((2, 2, steps, 2)),
            dma((2, 2, steps, 2)),
            dma,
            dma,
            dma((ny,)),
            dma((ny,)),
            dma,
            dma,
            dma((n, 2)),
            dma((n, 2)),
            dma((n, 2)),
            dma((n, 2)),
            dma((n, 3)),
            dma((n, 3)),
            dma,
            dma,
        ],
        compiler_params=pltpu.CompilerParams(
            collective_id=0, has_side_effects=True, vmem_limit_bytes=60 * 1024 * 1024
        ),
    )(bounds, gate, vk, vv, q, tk, tv, wt)


def solution(mesh):
    nx = mesh.shape["head"]
    specs = (
        P("tm", "head"),
        P("tm", "head"),
        P("tm", "head"),
        P("tm", "head"),
        P("tm", "head"),
        P("tm"),
        P("head"),
        P("head", "tm"),
    )
    return jax.shard_map(
        functools.partial(local, (8, mesh.shape["tm"] // 16, nx, 2, 2)),
        mesh=mesh,
        in_specs=specs,
        out_specs=P("tm", "head"),
        check_vma=False,
    )
```

```python
import functools

import jax
import jax.numpy as jnp
from jax import lax
from jax.experimental import pallas as pl
from jax.experimental.pallas import tpu as pltpu
from jax.sharding import PartitionSpec as P

MESH = pl.DeviceIdType.MESH
F32 = jnp.float32
BF16 = jnp.bfloat16
HDIM = 128
NORM_ROWS = 16
NN = (((1,), (0,)), ((), ()))
NT = (((1,), (1,)), ((), ()))
TN = (((0,), (0,)), ((), ()))


def dot(a, b, dims):
    return lax.dot_general(a, b, dims, preferred_element_type=F32)


def elu_one(values):
    return jnp.where(values > 0, values + 1.0, jnp.exp(jnp.minimum(values, 0.0)))


def split(value):
    high = value.astype(BF16)
    return high, (value - high.astype(F32)).astype(BF16)


def wait_bytes(ref, sem):
    pltpu.make_async_copy(ref, ref, sem).wait()


def kernel(
    ny,
    nz,
    nx,
    gy,
    gz,
    bound_ref,
    gate_ref,
    vk_ref,
    vv_ref,
    q_ref,
    tk_ref,
    tv_ref,
    w_ref,
    out_ref,
    w_all,
    kin,
    vown,
    vin,
    qin,
    tkin,
    tvin,
    bin_,
    kf,
    qf,
    s_send,
    s_recv,
    s_own,
    n_send,
    n_recv,
    n_own,
    sbuf,
    abuf,
    rbuf,
    tbuf,
    tsend,
    base,
    pbuf,
    pfx,
    numer_l,
    denom_l,
    local_o,
    mixed,
    x_out,
    x_in,
    sum_own,
    dsend,
    fin,
    in_sem,
    s_sem,
    w_sem,
    c_send,
    c_recv,
    w1_send,
    w1_recv,
    w2_send,
    w2_recv,
    a_send,
    a_recv,
    t_send,
    t_recv,
    p_send,
    p_recv,
    g_send,
    g_recv,
    m_send,
    m_recv,
    x_send,
    x_recv,
    d_send,
    d_recv,
):
    tm = lax.axis_index("tm")
    x = lax.axis_index("head")
    c = lax.rem(tm, 2)
    chip = tm // 2
    z = lax.rem(chip, nz)
    y = chip // nz

    vlen, width = vk_ref.shape
    rows = q_ref.shape[0]
    half_w = width // 2
    heads = half_w // HDIM
    per_head = nz // heads
    srows = HDIM // per_head
    wc = w_ref.shape[0]
    wh = wc // 2
    my, mz = ny // gy, nz // gz
    py, pz = lax.rem(y, gy), lax.rem(z, gz)
    yc, zc = y // gy, z // gz
    own_class = py * gz + pz
    offsets = [(dy, dz) for dy in range(gy) for dz in range(gz)]
    offsets.sort(key=lambda o: (o[0] + o[1], o[1]))

    def dev(t, xx):
        return {"tm": t, "head": xx}

    def y_dev(yy):
        return dev((yy * nz + z) * 2 + c, x)

    def z_dev(zz):
        return dev((y * nz + zz) * 2 + c, x)

    def x_dev(xx):
        return dev(tm, xx)

    def group_dev(dy, dz, core):
        yy = yc * gy + lax.rem(py + dy, gy)
        zz = zc * gz + lax.rem(pz + dz, gz)
        return dev((yy * nz + zz) * 2 + core, x)

    def class_of(dy, dz):
        return lax.rem(py + dy, gy) * gz + lax.rem(pz + dz, gz)

    twin = dev(tm + 1 - 2 * c, x)

    def ahead(me, step, n):
        return lax.rem(me + step, n)

    def send(src, dst, send_sem, recv_sem, device):
        copy = pltpu.make_async_remote_copy(
            src, dst, send_sem, recv_sem, device_id=device, device_id_type=MESH
        )
        copy.start()
        return copy

    mine = pl.ds(pl.multiple_of(c * half_w, HDIM), half_w)
    other = pl.ds(pl.multiple_of((1 - c) * half_w, HDIM), half_w)
    inputs = ((vk_ref, kin), (vv_ref, vin), (q_ref, qin), (tk_ref, tkin), (tv_ref, tvin))
    loads = [
        pltpu.make_async_copy(vk_ref, kin, in_sem.at[0]),
        pltpu.make_async_copy(vv_ref, vown, in_sem.at[1]),
        pltpu.make_async_copy(vv_ref.at[:, mine], vin.at[c], in_sem.at[5]),
    ] + [
        pltpu.make_async_copy(src.at[:, mine], dst.at[c], in_sem.at[i + 2])
        for i, (src, dst) in enumerate(inputs[2:])
    ]
    for load in loads:
        load.start()
    own_w = pltpu.make_async_copy(w_ref, w_all.at[yc, zc], w_sem)
    own_w.start()

    def far_first(n):
        return sorted(range(1, n), key=lambda step: -min(step, n - step))

    barrier = pltpu.get_barrier_semaphore()

    def greet(device):
        pl.semaphore_signal(barrier, inc=1, device_id=device, device_id_type=MESH)

    for step in far_first(nz):
        greet(z_dev(ahead(z, step, nz)))
    for step in far_first(ny):
        greet(y_dev(ahead(y, step, ny)))
    x_order = far_first(nx) + [0]
    for step in x_order[:-1]:
        greet(x_dev(ahead(x, step, nx)))
    greeted = 1 + (nz - 1) + (ny - 1) + (nx - 1)
    for dy, dz in offsets[1:]:
        greet(group_dev(dy, dz, 1 - c))
        greeted += 1
        if dy and dz:
            greet(group_dev(dy, dz, c))
            greeted += 1
    greet(twin)
    bin_[c] = jnp.full((8, HDIM), bound_ref[0], jnp.int32)

    loads[0].wait()
    kin[...] = elu_one(kin[...].astype(F32)).astype(BF16)
    loads[1].wait()
    ones = jnp.ones((NORM_ROWS, vlen), BF16)
    norm_row = lax.broadcasted_iota(jnp.int32, (NORM_ROWS, HDIM), 0)

    def own_state(core):
        norms = jnp.zeros((NORM_ROWS, HDIM), F32)
        states = []
        for h in range(heads):
            cols = pl.ds(pl.multiple_of(core * half_w + h * HDIM, HDIM), HDIM)
            feat = kin[:, cols]
            states.append(dot(feat, vown[:, cols], TN))
            norms = jnp.where(norm_row == h, dot(ones, feat, NN), norms)
        return states, norms

    states, norms = own_state(1 - c)
    for h in range(heads):
        for k in range(per_head):
            s_send[h * per_head + k] = states[h][k * srows : (k + 1) * srows].astype(BF16)
    n_send[...] = norms.astype(BF16)
    states, norms = own_state(c)
    for h in range(heads):
        for k in range(per_head):
            s_own[h * per_head + k] = states[h][k * srows : (k + 1) * srows]
    n_own[...] = norms
    kf[c] = kin[:, mine]
    pl.semaphore_wait(barrier, greeted)

    state_copy = send(s_send, s_recv, s_sem.at[0], s_sem.at[1], twin)
    norm_copy = send(n_send, n_recv, s_sem.at[2], s_sem.at[3], twin)
    def y_class(k):
        return y_dev(k * gy + py)

    def z_class(k):
        return z_dev(k * gz + pz)

    for step in far_first(mz):
        send(w_ref.at[0:wh], w_all.at[yc, zc, 0:wh], w1_send.at[0], w1_recv.at[0], z_class(ahead(zc, step, mz)))
    for step in far_first(my):
        send(w_ref.at[wh:wc], w_all.at[yc, zc, wh:wc], w1_send.at[1], w1_recv.at[1], y_class(ahead(yc, step, my)))

    state_copy.wait_recv()
    norm_copy.wait_recv()
    norms = (n_own[...] + n_recv[...].astype(F32)).astype(BF16)
    for k in range(nz):
        sbuf[k, 0:srows] = (s_own[k] + s_recv[k].astype(F32)).astype(BF16)
        sbuf[k, srows : srows + NORM_ROWS] = norms
    for step in far_first(nz):
        to = ahead(z, step, nz)
        send(sbuf.at[to], abuf.at[z], a_send, a_recv, z_dev(to))
    abuf[z] = sbuf[z]

    swaps = [send(kin.at[:, other], kf.at[c], c_send.at[0], c_recv.at[0], twin)]
    swaps += [
        send(src.at[:, other], dst.at[c], c_send.at[i + 1], c_recv.at[i + 1], twin)
        for i, (src, dst) in enumerate(inputs[1:])
    ]
    swaps.append(send(bin_.at[c], bin_.at[c], c_send.at[5], c_recv.at[5], twin))

    def bundle(half, index, q):
        if half == 0:
            return w_all.at[index, q * (mz // 2) : (q + 1) * (mz // 2), 0:wh]
        return w_all.at[q * (my // 2) : (q + 1) * (my // 2), index, wh:wc]

    laps = {}
    waited = set()

    def arrived(key):
        if key in laps and key not in waited:
            waited.add(key)
            laps[key].wait_recv()

    def lap(s, q):
        for half in range(2):
            for way in range(2):
                n, me = (my, yc) if half == 0 else (mz, zc)
                if s >= n // 2 or (s == n // 2 - 1 and q != way):
                    continue
                arrived((half, way, s - 1, q))
                block = ahead(me, n - s, n) if way == 0 else ahead(me, s, n)
                to = ahead(me, 1, n) if way == 0 else ahead(me, n - 1, n)
                part = bundle(half, block, q)
                laps[(half, way, s, q)] = send(
                    part, part, w2_send.at[half, way, s, q], w2_recv.at[half, way, s, q],
                    y_class(to) if half == 0 else z_class(to),
                )

    for load in loads[2:]:
        load.wait()
    for swap in swaps:
        swap.wait_recv()
    bounds = jnp.concatenate(
        [jnp.broadcast_to(bin_[0, 0:1, :], (rows, HDIM)), jnp.broadcast_to(bin_[1, 0:1, :], (rows, HDIM))]
    )
    row_ids = lax.broadcasted_iota(jnp.int32, (2 * rows, HDIM), 0)
    col_ids = lax.broadcasted_iota(jnp.int32, (2 * rows, HDIM), 1)

    def own_part(h):
        cols = slice(h * HDIM, (h + 1) * HDIM)
        query = qin[:, :, cols].reshape(2 * rows, HDIM)
        q_feat = elu_one(query.astype(F32)).astype(BF16)
        qf[h] = q_feat
        numer = jnp.zeros((2 * rows, HDIM), F32)
        denom = jnp.zeros((2 * rows, 1), F32)
        for e in range(2):
            weight = dot(q_feat, kf[e, :, cols], NT)
            weight = jnp.where(col_ids + (chip * 2 + e) * vlen < bounds, weight, 0.0)
            high, low = split(weight)
            values = vin[e, :, cols]
            numer = numer + dot(high, values, NN) + dot(low, values, NN)
            denom = denom + jnp.sum(weight, axis=1, keepdims=True)
        numer_l[h] = numer
        denom_l[h] = jnp.broadcast_to(denom, (2 * rows, HDIM))
        scores = dot(query, tkin[:, :, cols].reshape(2 * rows, HDIM), NT) * (float(HDIM) ** -0.5)
        causal = jnp.logical_and(col_ids <= row_ids, col_ids // rows == row_ids // rows)
        scores = jnp.where(causal, scores, -jnp.inf)
        expo = jnp.exp(scores - jnp.max(scores, axis=1, keepdims=True))
        probs = (expo / jnp.sum(expo, axis=1, keepdims=True)).astype(BF16)
        local_o[h] = dot(probs, tvin[:, :, cols].reshape(2 * rows, HDIM), NN)

    own_part(0)

    own_w.wait()
    if mz > 1:
        wait_bytes(w_all.at[0, 0 : mz - 1, 0:wh], w1_recv.at[0])
    if my > 1:
        wait_bytes(w_all.at[0 : my - 1, 0, wh:wc], w1_recv.at[1])
    steps = max(my, mz) // 2
    if steps:
        lap(0, 0)
        lap(0, 1)

    wait_bytes(abuf.at[0 : nz - 1], a_recv)
    total = jnp.zeros((srows + NORM_ROWS, HDIM), F32)
    for k in range(nz):
        rbuf[k] = total
        total = total + abuf[k].astype(F32)
    tsend[...] = total.astype(BF16)
    for step in range(1, ny):

        @pl.when(y + step < ny)
        def _():
            send(tsend, tbuf.at[y], t_send.at[step], t_recv.at[y], y_dev(y + step))

    for h in range(1, max(1, heads - 1)):
        own_part(h)

    base[...] = jnp.zeros_like(base)
    for k in range(ny - 1):

        @pl.when(k < y)
        def _():
            wait_bytes(tbuf.at[k], t_recv.at[k])
            base[...] += tbuf[k].astype(F32)

    for k in range(nz):
        pbuf[k] = (base[0:srows] + rbuf[k, 0:srows]).astype(BF16)
    pfx[z] = pbuf[z]
    for step in far_first(nz):
        to = ahead(z, step, nz)
        send(pbuf.at[to], pfx.at[z], p_send, p_recv, z_dev(to))
    norm_high, norm_low = split(base[srows : srows + NORM_ROWS] + rbuf[z, srows : srows + NORM_ROWS])

    for h in range(max(1, heads - 1), heads):
        own_part(h)

    for s in range(1, steps):
        lap(s, 0)
        lap(s, 1)

    wait_bytes(pfx.at[0 : nz - 1], p_recv)

    def retrieve(h):
        query = qf[h]
        first = h * per_head
        state = pfx[first : first + per_head].reshape(HDIM, HDIM)
        numer = numer_l[h] + dot(query, state, NN)
        denom = (dot(query, norm_high, NT) + dot(query, norm_low, NT))[:, h : h + 1] + denom_l[h]
        gate = 1.0 / (1.0 + jnp.exp(-jnp.full((8, HDIM), gate_ref[c * heads + h], F32)))[0:1]
        value = gate * (numer / denom) + (1.0 - gate) * local_o[h]
        mixed[own_class, c * heads + h] = value.astype(BF16)

    split_n = 2 if heads > 1 else 1

    def mixed_part(cls, i):
        return mixed.at[cls, pl.ds(c * heads + i * (heads // split_n), heads // split_n)]

    group_copies, twin_copies = {}, {}
    for i in range(split_n):
        for h in range(i * heads // split_n, (i + 1) * heads // split_n):
            retrieve(h)
        part = mixed_part(own_class, i)
        for r, (dy, dz) in reversed(list(enumerate(offsets))):
            if r == 0:
                twin_copies[r, i] = send(part, part, m_send.at[r, i], m_recv.at[r, i], twin)
            else:
                group_copies[r, i] = send(part, part, g_send.at[r, i], g_recv.at[r, i], group_dev(dy, dz, c))
    state_copy.wait_send()
    norm_copy.wait_send()
    for copy in swaps:
        copy.wait_send()
    if mz > 1:
        wait_bytes(w_all.at[0, 0 : mz - 1, 0:wh], w1_send.at[0])
    if my > 1:
        wait_bytes(w_all.at[0 : my - 1, 0, wh:wc], w1_send.at[1])
    wait_bytes(sbuf.at[0 : nz - 1], a_send)
    for step in range(1, ny):

        @pl.when(y + step < ny)
        def _():
            wait_bytes(tsend, t_send.at[step])

    wait_bytes(pbuf.at[0 : nz - 1], p_send)
    for key in list(laps):
        arrived(key)
    for copy in laps.values():
        copy.wait_send()

    yx = my // nx

    def project(cls, xxs):
        both = jnp.concatenate([mixed[cls, h] for h in range(2 * heads)], axis=1)
        block = jnp.concatenate([w_all[pl.ds(xx * yx, yx)].reshape(yx * mz * wc, width) for xx in xxs])
        value = dot(both, block, NT)
        return [value[:, i * HDIM : (i + 1) * HDIM] for i in range(len(xxs))]

    x_copies = {}

    def hand_over(r):
        for i in range(split_n):
            part = mixed_part(class_of(*offsets[r]), i)
            group_copies[r, i].wait_recv()
            twin_copies[r, i] = send(part, part, m_send.at[r, i], m_recv.at[r, i], twin)

    for r, (dy, dz) in enumerate(offsets):
        cls = class_of(dy, dz)
        for i in range(split_n):
            twin_copies[r, i].wait_recv()
        for first in range(0, len(x_order), 2):
            part_steps = x_order[first : first + 2]
            for step, value in zip(part_steps, project(cls, [ahead(x, step, nx) for step in part_steps])):
                if step == 0:
                    sum_own[r] = value
                    continue
                x_out[r, step] = value.astype(BF16)
                x_copies[r, step] = send(
                    x_out.at[r, step], x_in.at[r, step], x_send.at[r, step], x_recv.at[r, step],
                    x_dev(ahead(x, step, nx)),
                )
        for later in {0: (1, 2), 1: (3,)}.get(r, ()):
            if later < len(offsets):
                hand_over(later)
    done_copies = []
    for r, (dy, dz) in enumerate(offsets):
        total = sum_own[r]
        for step in x_order[:-1]:
            x_copies[r, step].wait_recv()
            total = total + x_in[r, step].astype(F32)
        total = total.astype(BF16)
        for e in range(2):
            dsend[r, e] = total[e * rows : (e + 1) * rows]
        place = fin.at[own_class * 2 + c]
        if r == 0:
            fin[own_class * 2 + c] = dsend[0, c]
            done_copies.append(send(dsend.at[0, 1 - c], place, d_send, d_recv, twin))
        else:
            for e in range(2):
                done_copies.append(send(dsend.at[r, e], place, d_send, d_recv, group_dev(dy, dz, e)))
    wait_bytes(fin.at[0 : len(done_copies)], d_recv)

    lane = lax.broadcasted_iota(jnp.int32, (rows, HDIM), 1)
    runs = HDIM // wc
    for b in range(out_ref.shape[1] // HDIM):
        value = jnp.zeros((rows, HDIM), F32)
        for k in range(runs):
            shard, e = divmod(b * runs + k, 2)
            yl, zz = divmod(shard, nz)
            pos = ((yl // gy) * mz + zz // gz) * wc
            piece = fin[((yl % gy) * gz + zz % gz) * 2 + e].astype(F32)
            shift = (k * wc - pos) % HDIM
            if shift:
                piece = pltpu.roll(piece, shift, 1)
            value = jnp.where(lane // wc == k, piece, value)
        out_ref[:, b * HDIM : (b + 1) * HDIM] = value.astype(BF16)

    for copies in (twin_copies.values(), group_copies.values(), x_copies.values()):
        for copy in copies:
            copy.wait_send()
    wait_bytes(fin.at[0 : len(done_copies)], d_send)


def local(grid, vk, vv, q, tk, tv, bounds, gate, w):
    ny, nz, nx, gy, gz = grid
    vlen, width = vk.shape
    rows = q.shape[0]
    half_w = width // 2
    heads = half_w // HDIM
    srows = half_w // nz
    wt = w.T
    wc = wt.shape[0]
    my, mz = ny // gy, nz // gz
    n = gy * gz
    assert (my // nx) * mz * wc == HDIM
    steps = max(my, mz, 2) // 2
    hbm = pl.BlockSpec(memory_space=pltpu.HBM)
    smem = pl.BlockSpec(memory_space=pltpu.SMEM)
    dma = pltpu.SemaphoreType.DMA
    slices = (nz, srows + NORM_ROWS, HDIM)
    states = (nz, srows, HDIM)
    per_head = (heads, 2 * rows, HDIM)
    return pl.pallas_call(
        functools.partial(kernel, ny, nz, nx, gy, gz),
        out_shape=jax.ShapeDtypeStruct((rows, 2 * n * HDIM), BF16),
        in_specs=[smem, smem] + [hbm] * 6,
        out_specs=pl.BlockSpec(memory_space=pltpu.VMEM),
        scratch_shapes=[
            pltpu.VMEM((my, mz, wc, width), BF16),
            pltpu.VMEM((vlen, width), BF16),
            pltpu.VMEM((vlen, width), BF16),
            pltpu.VMEM((2, vlen, half_w), BF16),
            pltpu.VMEM((2, rows, half_w), BF16),
            pltpu.VMEM((2, rows, half_w), BF16),
            pltpu.VMEM((2, rows, half_w), BF16),
            pltpu.VMEM((2, 8, HDIM), jnp.int32),
            pltpu.VMEM((2, vlen, half_w), BF16),
            pltpu.VMEM(per_head, BF16),
            pltpu.VMEM(states, BF16),
            pltpu.VMEM(states, BF16),
            pltpu.VMEM(states, F32),
            pltpu.VMEM((NORM_ROWS, HDIM), BF16),
            pltpu.VMEM((NORM_ROWS, HDIM), BF16),
            pltpu.VMEM((NORM_ROWS, HDIM), F32),
            pltpu.VMEM(slices, BF16),
            pltpu.VMEM(slices, BF16),
            pltpu.VMEM(slices, F32),
            pltpu.VMEM((ny, srows + NORM_ROWS, HDIM), BF16),
            pltpu.VMEM((srows + NORM_ROWS, HDIM), BF16),
            pltpu.VMEM((srows + NORM_ROWS, HDIM), F32),
            pltpu.VMEM(states, BF16),
            pltpu.VMEM(states, BF16),
            pltpu.VMEM(per_head, F32),
            pltpu.VMEM(per_head, F32),
            pltpu.VMEM(per_head, F32),
            pltpu.VMEM((n, 2 * heads, 2 * rows, HDIM), BF16),
            pltpu.VMEM((n, nx, 2 * rows, HDIM), BF16),
            pltpu.VMEM((n, nx, 2 * rows, HDIM), BF16),
            pltpu.VMEM((n, 2 * rows, HDIM), F32),
            pltpu.VMEM((n, 2, rows, HDIM), BF16),
            pltpu.VMEM((2 * n, rows, HDIM), BF16),
            dma((6,)),
            dma((4,)),
            dma,
            dma((6,)),
            dma((6,)),
            dma((2,)),
            dma((2,)),
            dma((2, 2, steps, 2)),
            dma((2, 2, steps, 2)),
            dma,
            dma,
            dma((ny,)),
            dma((ny,)),
            dma,
            dma,
            dma((n, 2)),
            dma((n, 2)),
            dma((n, 2)),
            dma((n, 2)),
            dma((n, nx)),
            dma((n, nx)),
            dma,
            dma,
        ],
        compiler_params=pltpu.CompilerParams(
            collective_id=0, has_side_effects=True, vmem_limit_bytes=60 * 1024 * 1024
        ),
    )(bounds, gate, vk, vv, q, tk, tv, wt)


def solution(mesh):
    nx = mesh.shape["head"]
    specs = (
        P("tm", "head"),
        P("tm", "head"),
        P("tm", "head"),
        P("tm", "head"),
        P("tm", "head"),
        P("tm"),
        P("head"),
        P("head", "tm"),
    )
    return jax.shard_map(
        functools.partial(local, (8, mesh.shape["tm"] // 16, nx, 2, 2)),
        mesh=mesh,
        in_specs=specs,
        out_specs=P("tm", "head"),
        check_vma=False,
    )
```

```python
import functools

import jax
import jax.numpy as jnp
from jax import lax
from jax.experimental import pallas as pl
from jax.experimental.pallas import tpu as pltpu
from jax.sharding import PartitionSpec as P

MESH = pl.DeviceIdType.MESH
F32 = jnp.float32
BF16 = jnp.bfloat16
HDIM = 128
NORM_ROWS = 16
NN = (((1,), (0,)), ((), ()))
NT = (((1,), (1,)), ((), ()))
TN = (((0,), (0,)), ((), ()))


def dot(a, b, dims):
    return lax.dot_general(a, b, dims, preferred_element_type=F32)


def elu_one(values):
    return jnp.where(values > 0, values + 1.0, jnp.exp(jnp.minimum(values, 0.0)))


def split(value):
    high = value.astype(BF16)
    return high, (value - high.astype(F32)).astype(BF16)


def wait_bytes(ref, sem):
    pltpu.make_async_copy(ref, ref, sem).wait()


def kernel(
    ny,
    nz,
    nx,
    gy,
    gz,
    bound_ref,
    gate_ref,
    vk_ref,
    vv_ref,
    q_ref,
    tk_ref,
    tv_ref,
    w_ref,
    out_ref,
    w_all,
    kin,
    vown,
    vin,
    qin,
    tkin,
    tvin,
    bin_,
    kf,
    qf,
    s_send,
    s_recv,
    s_own,
    n_send,
    n_recv,
    n_own,
    sbuf,
    abuf,
    rbuf,
    tbuf,
    tsend,
    pbuf,
    pfx,
    numer_l,
    denom_l,
    local_o,
    mixed,
    x_out,
    x_in,
    sum_own,
    dsend,
    fin,
    in_sem,
    s_sem,
    w_sem,
    c_send,
    c_recv,
    w1_send,
    w1_recv,
    w2_send,
    w2_recv,
    a_send,
    a_recv,
    t_send,
    t_recv,
    p_send,
    p_recv,
    g_send,
    g_recv,
    m_send,
    m_recv,
    x_send,
    x_recv,
    d_send,
    d_recv,
):
    tm = lax.axis_index("tm")
    x = lax.axis_index("head")
    c = lax.rem(tm, 2)
    chip = tm // 2
    z = lax.rem(chip, nz)
    y = chip // nz

    vlen, width = vk_ref.shape
    rows = q_ref.shape[0]
    half_w = width // 2
    heads = half_w // HDIM
    per_head = nz // heads
    srows = HDIM // per_head
    wc = w_ref.shape[0]
    wh = wc // 2
    my, mz = ny // gy, nz // gz
    py, pz = lax.rem(y, gy), lax.rem(z, gz)
    yc, zc = y // gy, z // gz
    own_class = py * gz + pz
    offsets = [(dy, dz) for dy in range(gy) for dz in range(gz)]
    offsets.sort(key=lambda o: (o[0] + o[1], o[1]))

    def dev(t, xx):
        return {"tm": t, "head": xx}

    def y_dev(yy):
        return dev((yy * nz + z) * 2 + c, x)

    def z_dev(zz):
        return dev((y * nz + zz) * 2 + c, x)

    def x_dev(xx):
        return dev(tm, xx)

    def group_dev(dy, dz, core):
        yy = yc * gy + lax.rem(py + dy, gy)
        zz = zc * gz + lax.rem(pz + dz, gz)
        return dev((yy * nz + zz) * 2 + core, x)

    def class_of(dy, dz):
        return lax.rem(py + dy, gy) * gz + lax.rem(pz + dz, gz)

    twin = dev(tm + 1 - 2 * c, x)

    def ahead(me, step, n):
        return lax.rem(me + step, n)

    def send(src, dst, send_sem, recv_sem, device):
        copy = pltpu.make_async_remote_copy(
            src, dst, send_sem, recv_sem, device_id=device, device_id_type=MESH
        )
        copy.start()
        return copy

    mine = pl.ds(pl.multiple_of(c * half_w, HDIM), half_w)
    other = pl.ds(pl.multiple_of((1 - c) * half_w, HDIM), half_w)
    inputs = ((vk_ref, kin), (vv_ref, vin), (q_ref, qin), (tk_ref, tkin), (tv_ref, tvin))
    loads = [
        pltpu.make_async_copy(vk_ref.at[:, other], kin.at[0], in_sem.at[0]),
        pltpu.make_async_copy(vv_ref.at[:, other], vown, in_sem.at[1]),
        pltpu.make_async_copy(vk_ref.at[:, mine], kin.at[1], in_sem.at[5]),
        pltpu.make_async_copy(vv_ref.at[:, mine], vin.at[c], in_sem.at[6]),
    ] + [
        pltpu.make_async_copy(src.at[:, mine], dst.at[c], in_sem.at[i + 2])
        for i, (src, dst) in enumerate(inputs[2:])
    ]
    for load in loads:
        load.start()
    own_w = pltpu.make_async_copy(w_ref, w_all.at[yc, zc], w_sem)
    own_w.start()

    def far_first(n):
        return sorted(range(1, n), key=lambda step: -min(step, n - step))

    barrier = pltpu.get_barrier_semaphore()

    def greet(device):
        pl.semaphore_signal(barrier, inc=1, device_id=device, device_id_type=MESH)

    for step in far_first(nz):
        greet(z_dev(ahead(z, step, nz)))
    for step in far_first(ny):
        greet(y_dev(ahead(y, step, ny)))
    x_order = far_first(nx) + [0]
    for step in x_order[:-1]:
        greet(x_dev(ahead(x, step, nx)))
    greeted = 1 + (nz - 1) + (ny - 1) + (nx - 1)
    for dy, dz in offsets[1:]:
        greet(group_dev(dy, dz, 1 - c))
        greeted += 1
        if dy and dz:
            greet(group_dev(dy, dz, c))
            greeted += 1
    greet(twin)
    bin_[c] = jnp.full((8, HDIM), bound_ref[0], jnp.int32)

    loads[0].wait()
    kin[0] = elu_one(kin[0].astype(F32)).astype(BF16)
    loads[1].wait()
    ones = jnp.ones((NORM_ROWS, vlen), BF16)
    norm_row = lax.broadcasted_iota(jnp.int32, (NORM_ROWS, HDIM), 0)

    def own_state(keys, values):
        norms = jnp.zeros((NORM_ROWS, HDIM), F32)
        states = []
        for h in range(heads):
            cols = slice(h * HDIM, (h + 1) * HDIM)
            states.append(dot(keys[:, cols], values[:, cols], TN))
            norms = jnp.where(norm_row == h, dot(ones, keys[:, cols], NN), norms)
        return states, norms

    states, norms = own_state(kin.at[0], vown)
    for h in range(heads):
        for k in range(per_head):
            s_send[h * per_head + k] = states[h][k * srows : (k + 1) * srows].astype(BF16)
    n_send[...] = norms.astype(BF16)
    for k in range(ny):

        @pl.when(k >= y)
        def _():
            tbuf[k] = jnp.zeros(tbuf.shape[1:], BF16)

    pl.semaphore_wait(barrier, greeted)
    state_copy = send(s_send, s_recv, s_sem.at[0], s_sem.at[1], twin)
    norm_copy = send(n_send, n_recv, s_sem.at[2], s_sem.at[3], twin)
    def y_class(k):
        return y_dev(k * gy + py)

    def z_class(k):
        return z_dev(k * gz + pz)

    for step in far_first(mz):
        send(w_ref.at[0:wh], w_all.at[yc, zc, 0:wh], w1_send.at[0], w1_recv.at[0], z_class(ahead(zc, step, mz)))
    for step in far_first(my):
        send(w_ref.at[wh:wc], w_all.at[yc, zc, wh:wc], w1_send.at[1], w1_recv.at[1], y_class(ahead(yc, step, my)))

    loads[2].wait()
    kf[c] = elu_one(kin[1].astype(F32)).astype(BF16)
    loads[3].wait()
    states, norms = own_state(kf.at[c], vin.at[c])
    for h in range(heads):
        for k in range(per_head):
            s_own[h * per_head + k] = states[h][k * srows : (k + 1) * srows]
    n_own[...] = norms
    state_copy.wait_recv()
    norm_copy.wait_recv()
    norms = (n_own[...] + n_recv[...].astype(F32)).astype(BF16)
    for k in range(nz):
        sbuf[k, 0:srows] = (s_own[k] + s_recv[k].astype(F32)).astype(BF16)
        sbuf[k, srows : srows + NORM_ROWS] = norms
    for step in far_first(nz):
        to = ahead(z, step, nz)
        send(sbuf.at[to], abuf.at[z], a_send, a_recv, z_dev(to))
    abuf[z] = sbuf[z]

    swaps = [send(kin.at[0], kf.at[c], c_send.at[0], c_recv.at[0], twin)]
    swaps += [
        send(src.at[:, other], dst.at[c], c_send.at[i + 1], c_recv.at[i + 1], twin)
        for i, (src, dst) in enumerate(inputs[1:])
    ]
    swaps.append(send(bin_.at[c], bin_.at[c], c_send.at[5], c_recv.at[5], twin))

    def bundle(half, index, q):
        if half == 0:
            return w_all.at[index, q * (mz // 2) : (q + 1) * (mz // 2), 0:wh]
        return w_all.at[q * (my // 2) : (q + 1) * (my // 2), index, wh:wc]

    laps = {}
    waited = set()

    def arrived(key):
        if key in laps and key not in waited:
            waited.add(key)
            laps[key].wait_recv()

    def lap(s, q, halves=(0, 1)):
        for half in halves:
            for way in range(2):
                n, me = (my, yc) if half == 0 else (mz, zc)
                if s >= n // 2 or (s == n // 2 - 1 and q != way):
                    continue
                arrived((half, way, s - 1, q))
                block = ahead(me, n - s, n) if way == 0 else ahead(me, s, n)
                to = ahead(me, 1, n) if way == 0 else ahead(me, n - 1, n)
                part = bundle(half, block, q)
                laps[(half, way, s, q)] = send(
                    part, part, w2_send.at[half, way, s, q], w2_recv.at[half, way, s, q],
                    y_class(to) if half == 0 else z_class(to),
                )

    for load in loads[4:]:
        load.wait()
    for swap in swaps:
        swap.wait_recv()
    bounds = jnp.concatenate(
        [jnp.broadcast_to(bin_[0, 0:1, :], (rows, HDIM)), jnp.broadcast_to(bin_[1, 0:1, :], (rows, HDIM))]
    )
    row_ids = lax.broadcasted_iota(jnp.int32, (2 * rows, HDIM), 0)
    col_ids = lax.broadcasted_iota(jnp.int32, (2 * rows, HDIM), 1)

    def own_part(h):
        cols = slice(h * HDIM, (h + 1) * HDIM)
        query = qin[:, :, cols].reshape(2 * rows, HDIM)
        q_feat = elu_one(query.astype(F32)).astype(BF16)
        qf[h] = q_feat
        numer = jnp.zeros((2 * rows, HDIM), F32)
        denom = jnp.zeros((2 * rows, 1), F32)
        for e in range(2):
            weight = dot(q_feat, kf[e, :, cols], NT)
            weight = jnp.where(col_ids + (chip * 2 + e) * vlen < bounds, weight, 0.0)
            high, low = split(weight)
            values = vin[e, :, cols]
            numer = numer + dot(high, values, NN) + dot(low, values, NN)
            denom = denom + jnp.sum(weight, axis=1, keepdims=True)
        numer_l[h] = numer
        denom_l[h] = jnp.broadcast_to(denom, (2 * rows, HDIM))
        scores = dot(query, tkin[:, :, cols].reshape(2 * rows, HDIM), NT) * (float(HDIM) ** -0.5)
        causal = jnp.logical_and(col_ids <= row_ids, col_ids // rows == row_ids // rows)
        scores = jnp.where(causal, scores, -jnp.inf)
        expo = jnp.exp(scores - jnp.max(scores, axis=1, keepdims=True))
        probs = (expo / jnp.sum(expo, axis=1, keepdims=True)).astype(BF16)
        local_o[h] = dot(probs, tvin[:, :, cols].reshape(2 * rows, HDIM), NN)

    steps = max(my, mz) // 2
    own_w.wait()
    if my > 1:
        wait_bytes(w_all.at[0 : my - 1, 0, wh:wc], w1_recv.at[1])
        lap(0, 0, (1,))
        lap(0, 1, (1,))

    wait_bytes(abuf.at[0 : nz - 1], a_recv)
    total = jnp.zeros((srows + NORM_ROWS, HDIM), F32)
    for k in range(nz):
        rbuf[k] = total
        total = total + abuf[k].astype(F32)
    tsend[...] = total.astype(BF16)
    for step in far_first(ny):

        @pl.when(y + step < ny)
        def _():
            send(tsend, tbuf.at[y], t_send.at[step], t_recv.at[y], y_dev(y + step))

    if mz > 1:
        wait_bytes(w_all.at[0, 0 : mz - 1, 0:wh], w1_recv.at[0])
        lap(0, 0, (0,))
        lap(0, 1, (0,))

    for h in range(heads // 2):
        own_part(h)

    for k in range(ny - 1):

        @pl.when(k < y)
        def _():
            wait_bytes(tbuf.at[k], t_recv.at[k])

    base = tbuf[0].astype(F32)
    for k in range(1, ny):
        base = base + tbuf[k].astype(F32)
    for k in range(nz):
        pbuf[k] = (base[0:srows] + rbuf[k, 0:srows]).astype(BF16)
    pfx[z] = pbuf[z]
    for step in far_first(nz):
        to = ahead(z, step, nz)
        send(pbuf.at[to], pfx.at[z], p_send, p_recv, z_dev(to))
    norm_high, norm_low = split(base[srows : srows + NORM_ROWS] + rbuf[z, srows : srows + NORM_ROWS])

    for h in range(heads // 2, heads):
        own_part(h)

    for s in range(1, steps):
        lap(s, 0)
        lap(s, 1)

    wait_bytes(pfx.at[0 : nz - 1], p_recv)

    def retrieve(h):
        query = qf[h]
        first = h * per_head
        state = pfx[first : first + per_head].reshape(HDIM, HDIM)
        numer = numer_l[h] + dot(query, state, NN)
        denom = (dot(query, norm_high, NT) + dot(query, norm_low, NT))[:, h : h + 1] + denom_l[h]
        gate = 1.0 / (1.0 + jnp.exp(-jnp.full((8, HDIM), gate_ref[c * heads + h], F32)))[0:1]
        value = gate * (numer / denom) + (1.0 - gate) * local_o[h]
        mixed[own_class, c * heads + h] = value.astype(BF16)

    split_n = 2 if heads > 1 else 1

    def mixed_part(cls, i):
        return mixed.at[cls, pl.ds(c * heads + i * (heads // split_n), heads // split_n)]

    group_copies, twin_copies = {}, {}
    for i in range(split_n):
        for h in range(i * heads // split_n, (i + 1) * heads // split_n):
            retrieve(h)
        part = mixed_part(own_class, i)
        for r, (dy, dz) in reversed(list(enumerate(offsets))):
            if r == 0:
                twin_copies[r, i] = send(part, part, m_send.at[r, i], m_recv.at[r, i], twin)
            else:
                group_copies[r, i] = send(part, part, g_send.at[r, i], g_recv.at[r, i], group_dev(dy, dz, c))
    state_copy.wait_send()
    norm_copy.wait_send()
    for copy in swaps:
        copy.wait_send()
    if mz > 1:
        wait_bytes(w_all.at[0, 0 : mz - 1, 0:wh], w1_send.at[0])
    if my > 1:
        wait_bytes(w_all.at[0 : my - 1, 0, wh:wc], w1_send.at[1])
    wait_bytes(sbuf.at[0 : nz - 1], a_send)
    for step in range(1, ny):

        @pl.when(y + step < ny)
        def _():
            wait_bytes(tsend, t_send.at[step])

    wait_bytes(pbuf.at[0 : nz - 1], p_send)
    for key in list(laps):
        arrived(key)
    for copy in laps.values():
        copy.wait_send()

    yx = my // nx

    def project(cls, xxs):
        both = jnp.concatenate([mixed[cls, h] for h in range(2 * heads)], axis=1)
        block = jnp.concatenate([w_all[pl.ds(xx * yx, yx)].reshape(yx * mz * wc, width) for xx in xxs])
        value = dot(both, block, NT)
        return [value[:, i * HDIM : (i + 1) * HDIM] for i in range(len(xxs))]

    x_copies = {}

    def hand_over(r):
        for i in range(split_n):
            part = mixed_part(class_of(*offsets[r]), i)
            group_copies[r, i].wait_recv()
            twin_copies[r, i] = send(part, part, m_send.at[r, i], m_recv.at[r, i], twin)

    for r, (dy, dz) in enumerate(offsets):
        cls = class_of(dy, dz)
        for i in range(split_n):
            twin_copies[r, i].wait_recv()
        for first in range(0, len(x_order), 2):
            part_steps = x_order[first : first + 2]
            for step, value in zip(part_steps, project(cls, [ahead(x, step, nx) for step in part_steps])):
                if step == 0:
                    sum_own[r] = value
                    continue
                x_out[r, step] = value.astype(BF16)
                x_copies[r, step] = send(
                    x_out.at[r, step], x_in.at[r, step], x_send.at[r, step], x_recv.at[r, step],
                    x_dev(ahead(x, step, nx)),
                )
        for later in {0: (1, 2), 1: (3,)}.get(r, ()):
            if later < len(offsets):
                hand_over(later)
    done_copies = []
    for r, (dy, dz) in enumerate(offsets):
        total = sum_own[r]
        for step in x_order[:-1]:
            x_copies[r, step].wait_recv()
            total = total + x_in[r, step].astype(F32)
        total = total.astype(BF16)
        for e in range(2):
            dsend[r, e] = total[e * rows : (e + 1) * rows]
        place = fin.at[own_class * 2 + c]
        if r == 0:
            fin[own_class * 2 + c] = dsend[0, c]
            done_copies.append(send(dsend.at[0, 1 - c], place, d_send, d_recv, twin))
        else:
            for e in range(2):
                done_copies.append(send(dsend.at[r, e], place, d_send, d_recv, group_dev(dy, dz, e)))
    wait_bytes(fin.at[0 : len(done_copies)], d_recv)

    lane = lax.broadcasted_iota(jnp.int32, (rows, HDIM), 1)
    runs = HDIM // wc
    for b in range(out_ref.shape[1] // HDIM):
        value = jnp.zeros((rows, HDIM), F32)
        for k in range(runs):
            shard, e = divmod(b * runs + k, 2)
            yl, zz = divmod(shard, nz)
            pos = ((yl // gy) * mz + zz // gz) * wc
            piece = fin[((yl % gy) * gz + zz % gz) * 2 + e].astype(F32)
            shift = (k * wc - pos) % HDIM
            if shift:
                piece = pltpu.roll(piece, shift, 1)
            value = jnp.where(lane // wc == k, piece, value)
        out_ref[:, b * HDIM : (b + 1) * HDIM] = value.astype(BF16)

    for copies in (twin_copies.values(), group_copies.values(), x_copies.values()):
        for copy in copies:
            copy.wait_send()
    wait_bytes(fin.at[0 : len(done_copies)], d_send)


def local(grid, vk, vv, q, tk, tv, bounds, gate, w):
    ny, nz, nx, gy, gz = grid
    vlen, width = vk.shape
    rows = q.shape[0]
    half_w = width // 2
    heads = half_w // HDIM
    srows = half_w // nz
    wt = w.T
    wc = wt.shape[0]
    my, mz = ny // gy, nz // gz
    n = gy * gz
    assert (my // nx) * mz * wc == HDIM
    steps = max(my, mz, 2) // 2
    hbm = pl.BlockSpec(memory_space=pltpu.HBM)
    smem = pl.BlockSpec(memory_space=pltpu.SMEM)
    dma = pltpu.SemaphoreType.DMA
    slices = (nz, srows + NORM_ROWS, HDIM)
    states = (nz, srows, HDIM)
    per_head = (heads, 2 * rows, HDIM)
    return pl.pallas_call(
        functools.partial(kernel, ny, nz, nx, gy, gz),
        out_shape=jax.ShapeDtypeStruct((rows, 2 * n * HDIM), BF16),
        in_specs=[smem, smem] + [hbm] * 6,
        out_specs=pl.BlockSpec(memory_space=pltpu.VMEM),
        scratch_shapes=[
            pltpu.VMEM((my, mz, wc, width), BF16),
            pltpu.VMEM((2, vlen, half_w), BF16),
            pltpu.VMEM((vlen, half_w), BF16),
            pltpu.VMEM((2, vlen, half_w), BF16),
            pltpu.VMEM((2, rows, half_w), BF16),
            pltpu.VMEM((2, rows, half_w), BF16),
            pltpu.VMEM((2, rows, half_w), BF16),
            pltpu.VMEM((2, 8, HDIM), jnp.int32),
            pltpu.VMEM((2, vlen, half_w), BF16),
            pltpu.VMEM(per_head, BF16),
            pltpu.VMEM(states, BF16),
            pltpu.VMEM(states, BF16),
            pltpu.VMEM(states, F32),
            pltpu.VMEM((NORM_ROWS, HDIM), BF16),
            pltpu.VMEM((NORM_ROWS, HDIM), BF16),
            pltpu.VMEM((NORM_ROWS, HDIM), F32),
            pltpu.VMEM(slices, BF16),
            pltpu.VMEM(slices, BF16),
            pltpu.VMEM(slices, F32),
            pltpu.VMEM((ny, srows + NORM_ROWS, HDIM), BF16),
            pltpu.VMEM((srows + NORM_ROWS, HDIM), BF16),
            pltpu.VMEM(states, BF16),
            pltpu.VMEM(states, BF16),
            pltpu.VMEM(per_head, F32),
            pltpu.VMEM(per_head, F32),
            pltpu.VMEM(per_head, F32),
            pltpu.VMEM((n, 2 * heads, 2 * rows, HDIM), BF16),
            pltpu.VMEM((n, nx, 2 * rows, HDIM), BF16),
            pltpu.VMEM((n, nx, 2 * rows, HDIM), BF16),
            pltpu.VMEM((n, 2 * rows, HDIM), F32),
            pltpu.VMEM((n, 2, rows, HDIM), BF16),
            pltpu.VMEM((2 * n, rows, HDIM), BF16),
            dma((7,)),
            dma((4,)),
            dma,
            dma((6,)),
            dma((6,)),
            dma((2,)),
            dma((2,)),
            dma((2, 2, steps, 2)),
            dma((2, 2, steps, 2)),
            dma,
            dma,
            dma((ny,)),
            dma((ny,)),
            dma,
            dma,
            dma((n, 2)),
            dma((n, 2)),
            dma((n, 2)),
            dma((n, 2)),
            dma((n, nx)),
            dma((n, nx)),
            dma,
            dma,
        ],
        compiler_params=pltpu.CompilerParams(
            collective_id=0, has_side_effects=True, vmem_limit_bytes=60 * 1024 * 1024
        ),
    )(bounds, gate, vk, vv, q, tk, tv, wt)


def solution(mesh):
    nx = mesh.shape["head"]
    specs = (
        P("tm", "head"),
        P("tm", "head"),
        P("tm", "head"),
        P("tm", "head"),
        P("tm", "head"),
        P("tm"),
        P("head"),
        P("head", "tm"),
    )
    return jax.shard_map(
        functools.partial(local, (8, mesh.shape["tm"] // 16, nx, 2, 2)),
        mesh=mesh,
        in_specs=specs,
        out_specs=P("tm", "head"),
        check_vma=False,
    )
```

```python
import functools

import jax
import jax.numpy as jnp
from jax import lax
from jax.experimental import pallas as pl
from jax.experimental.pallas import tpu as pltpu
from jax.sharding import PartitionSpec as P

MESH = pl.DeviceIdType.MESH
F32 = jnp.float32
BF16 = jnp.bfloat16
HDIM = 128
NORM_ROWS = 16
NN = (((1,), (0,)), ((), ()))
NT = (((1,), (1,)), ((), ()))
TN = (((0,), (0,)), ((), ()))


def dot(a, b, dims):
    return lax.dot_general(a, b, dims, preferred_element_type=F32)


def elu_one(values):
    return jnp.where(values > 0, values + 1.0, jnp.exp(jnp.minimum(values, 0.0)))


def split(value):
    high = value.astype(BF16)
    return high, (value - high.astype(F32)).astype(BF16)


def wait_bytes(ref, sem):
    pltpu.make_async_copy(ref, ref, sem).wait()


def kernel(
    ny,
    nz,
    nx,
    gy,
    gz,
    bound_ref,
    gate_ref,
    vk_ref,
    vv_ref,
    q_ref,
    tk_ref,
    tv_ref,
    w_ref,
    out_ref,
    w_all,
    kin,
    vown,
    vin,
    qin,
    tkin,
    tvin,
    bin_,
    kf,
    qf,
    s_send,
    s_recv,
    s_own,
    n_send,
    n_recv,
    n_own,
    sbuf,
    abuf,
    rbuf,
    tbuf,
    tsend,
    pbuf,
    pfx,
    numer_l,
    denom_l,
    local_o,
    mixed,
    x_out,
    x_in,
    sum_own,
    dsend,
    fin,
    in_sem,
    s_sem,
    w_sem,
    c_send,
    c_recv,
    w1_send,
    w1_recv,
    w2_send,
    w2_recv,
    a_send,
    a_recv,
    t_send,
    t_recv,
    p_send,
    p_recv,
    g_send,
    g_recv,
    m_send,
    m_recv,
    x_send,
    x_recv,
    d_send,
    d_recv,
):
    tm = lax.axis_index("tm")
    x = lax.axis_index("head")
    c = lax.rem(tm, 2)
    chip = tm // 2
    z = lax.rem(chip, nz)
    y = chip // nz

    vlen, width = vk_ref.shape
    rows = q_ref.shape[0]
    half_w = width // 2
    heads = half_w // HDIM
    per_head = nz // heads
    srows = HDIM // per_head
    wc = w_ref.shape[0]
    wh = wc // 2
    my, mz = ny // gy, nz // gz
    py, pz = lax.rem(y, gy), lax.rem(z, gz)
    yc, zc = y // gy, z // gz
    own_class = py * gz + pz
    offsets = [(dy, dz) for dy in range(gy) for dz in range(gz)]
    offsets.sort(key=lambda o: (o[0] + o[1], o[1]))

    def dev(t, xx):
        return {"tm": t, "head": xx}

    def y_dev(yy):
        return dev((yy * nz + z) * 2 + c, x)

    def z_dev(zz):
        return dev((y * nz + zz) * 2 + c, x)

    def x_dev(xx):
        return dev(tm, xx)

    def group_dev(dy, dz, core):
        yy = yc * gy + lax.rem(py + dy, gy)
        zz = zc * gz + lax.rem(pz + dz, gz)
        return dev((yy * nz + zz) * 2 + core, x)

    def class_of(dy, dz):
        return lax.rem(py + dy, gy) * gz + lax.rem(pz + dz, gz)

    twin = dev(tm + 1 - 2 * c, x)

    def ahead(me, step, n):
        return lax.rem(me + step, n)

    def send(src, dst, send_sem, recv_sem, device):
        copy = pltpu.make_async_remote_copy(
            src, dst, send_sem, recv_sem, device_id=device, device_id_type=MESH
        )
        copy.start()
        return copy

    mine = pl.ds(pl.multiple_of(c * half_w, HDIM), half_w)
    other = pl.ds(pl.multiple_of((1 - c) * half_w, HDIM), half_w)
    inputs = ((vk_ref, kin), (vv_ref, vin), (q_ref, qin), (tk_ref, tkin), (tv_ref, tvin))
    loads = [
        pltpu.make_async_copy(vk_ref.at[:, other], kin.at[0], in_sem.at[0]),
        pltpu.make_async_copy(vv_ref.at[:, other], vown, in_sem.at[1]),
        pltpu.make_async_copy(vk_ref.at[:, mine], kin.at[1], in_sem.at[5]),
        pltpu.make_async_copy(vv_ref.at[:, mine], vin.at[c], in_sem.at[6]),
    ] + [
        pltpu.make_async_copy(src.at[:, mine], dst.at[c], in_sem.at[i + 2])
        for i, (src, dst) in enumerate(inputs[2:])
    ]
    for load in loads:
        load.start()
    own_w = pltpu.make_async_copy(w_ref, w_all.at[yc, zc], w_sem)
    own_w.start()

    def far_first(n):
        return sorted(range(1, n), key=lambda step: -min(step, n - step))

    barrier = pltpu.get_barrier_semaphore()

    def greet(device):
        pl.semaphore_signal(barrier, inc=1, device_id=device, device_id_type=MESH)

    for step in far_first(nz):
        greet(z_dev(ahead(z, step, nz)))
    for step in far_first(ny):
        greet(y_dev(ahead(y, step, ny)))
    x_order = far_first(nx) + [0]
    for step in x_order[:-1]:
        greet(x_dev(ahead(x, step, nx)))
    greeted = 1 + (nz - 1) + (ny - 1) + (nx - 1)
    for dy, dz in offsets[1:]:
        greet(group_dev(dy, dz, 1 - c))
        greeted += 1
        if dy and dz:
            greet(group_dev(dy, dz, c))
            greeted += 1
    greet(twin)
    bin_[c] = jnp.full((8, HDIM), bound_ref[0], jnp.int32)

    loads[0].wait()
    kin[0] = elu_one(kin[0].astype(F32)).astype(BF16)
    loads[1].wait()
    ones = jnp.ones((NORM_ROWS, vlen), BF16)
    norm_row = lax.broadcasted_iota(jnp.int32, (NORM_ROWS, HDIM), 0)

    def own_state(keys, values):
        norms = jnp.zeros((NORM_ROWS, HDIM), F32)
        states = []
        for h in range(heads):
            cols = slice(h * HDIM, (h + 1) * HDIM)
            states.append(dot(keys[:, cols], values[:, cols], TN))
            norms = jnp.where(norm_row == h, dot(ones, keys[:, cols], NN), norms)
        return states, norms

    states, norms = own_state(kin.at[0], vown)
    for h in range(heads):
        for k in range(per_head):
            s_send[h * per_head + k] = states[h][k * srows : (k + 1) * srows].astype(BF16)
    n_send[...] = norms.astype(BF16)
    for k in range(ny):

        @pl.when(k >= y)
        def _():
            tbuf[k] = jnp.zeros(tbuf.shape[1:], BF16)

    pl.semaphore_wait(barrier, greeted)
    state_copy = send(s_send, s_recv, s_sem.at[0], s_sem.at[1], twin)
    norm_copy = send(n_send, n_recv, s_sem.at[2], s_sem.at[3], twin)
    def y_class(k):
        return y_dev(k * gy + py)

    def z_class(k):
        return z_dev(k * gz + pz)

    for step in far_first(mz):
        send(w_ref.at[0:wh], w_all.at[yc, zc, 0:wh], w1_send.at[0], w1_recv.at[0], z_class(ahead(zc, step, mz)))
    for step in far_first(my):
        send(w_ref.at[wh:wc], w_all.at[yc, zc, wh:wc], w1_send.at[1], w1_recv.at[1], y_class(ahead(yc, step, my)))

    loads[2].wait()
    kf[c] = elu_one(kin[1].astype(F32)).astype(BF16)
    loads[3].wait()
    states, norms = own_state(kf.at[c], vin.at[c])
    for h in range(heads):
        for k in range(per_head):
            s_own[h * per_head + k] = states[h][k * srows : (k + 1) * srows]
    n_own[...] = norms
    state_copy.wait_recv()
    norm_copy.wait_recv()
    norms = (n_own[...] + n_recv[...].astype(F32)).astype(BF16)
    for k in range(nz):
        sbuf[k, 0:srows] = (s_own[k] + s_recv[k].astype(F32)).astype(BF16)
        sbuf[k, srows : srows + NORM_ROWS] = norms
    for step in far_first(nz):
        to = ahead(z, step, nz)
        send(sbuf.at[to], abuf.at[z], a_send, a_recv, z_dev(to))
    abuf[z] = sbuf[z]

    swaps = [send(kin.at[0], kf.at[c], c_send.at[0], c_recv.at[0], twin)]
    swaps += [
        send(src.at[:, other], dst.at[c], c_send.at[i + 1], c_recv.at[i + 1], twin)
        for i, (src, dst) in enumerate(inputs[1:])
    ]
    swaps.append(send(bin_.at[c], bin_.at[c], c_send.at[5], c_recv.at[5], twin))

    def bundle(half, index, q):
        if half == 0:
            return w_all.at[index, q * (mz // 2) : (q + 1) * (mz // 2), 0:wh]
        return w_all.at[q * (my // 2) : (q + 1) * (my // 2), index, wh:wc]

    laps = {}
    waited = set()

    def arrived(key):
        if key in laps and key not in waited:
            waited.add(key)
            laps[key].wait_recv()

    def lap(s, q, halves=(0, 1)):
        for half in halves:
            for way in range(2):
                n, me = (my, yc) if half == 0 else (mz, zc)
                if s >= n // 2 or (s == n // 2 - 1 and q != way):
                    continue
                arrived((half, way, s - 1, q))
                block = ahead(me, n - s, n) if way == 0 else ahead(me, s, n)
                to = ahead(me, 1, n) if way == 0 else ahead(me, n - 1, n)
                part = bundle(half, block, q)
                laps[(half, way, s, q)] = send(
                    part, part, w2_send.at[half, way, s, q], w2_recv.at[half, way, s, q],
                    y_class(to) if half == 0 else z_class(to),
                )

    for load in loads[4:]:
        load.wait()
    for swap in swaps:
        swap.wait_recv()
    bounds = jnp.concatenate(
        [jnp.broadcast_to(bin_[0, 0:1, :], (rows, HDIM)), jnp.broadcast_to(bin_[1, 0:1, :], (rows, HDIM))]
    )
    row_ids = lax.broadcasted_iota(jnp.int32, (2 * rows, HDIM), 0)
    col_ids = lax.broadcasted_iota(jnp.int32, (2 * rows, HDIM), 1)

    def own_part(h):
        cols = slice(h * HDIM, (h + 1) * HDIM)
        query = qin[:, :, cols].reshape(2 * rows, HDIM)
        q_feat = elu_one(query.astype(F32)).astype(BF16)
        qf[h] = q_feat
        numer = jnp.zeros((2 * rows, HDIM), F32)
        denom = jnp.zeros((2 * rows, 1), F32)
        for e in range(2):
            weight = dot(q_feat, kf[e, :, cols], NT)
            weight = jnp.where(col_ids + (chip * 2 + e) * vlen < bounds, weight, 0.0)
            high, low = split(weight)
            values = vin[e, :, cols]
            numer = numer + dot(high, values, NN) + dot(low, values, NN)
            denom = denom + jnp.sum(weight, axis=1, keepdims=True)
        numer_l[h] = numer
        denom_l[h] = jnp.broadcast_to(denom, (2 * rows, HDIM))
        scores = dot(query, tkin[:, :, cols].reshape(2 * rows, HDIM), NT) * (float(HDIM) ** -0.5)
        causal = jnp.logical_and(col_ids <= row_ids, col_ids // rows == row_ids // rows)
        scores = jnp.where(causal, scores, -jnp.inf)
        expo = jnp.exp(scores - jnp.max(scores, axis=1, keepdims=True))
        probs = (expo / jnp.sum(expo, axis=1, keepdims=True)).astype(BF16)
        local_o[h] = dot(probs, tvin[:, :, cols].reshape(2 * rows, HDIM), NN)

    steps = max(my, mz) // 2
    own_w.wait()
    if my > 1:
        wait_bytes(w_all.at[0 : my - 1, 0, wh:wc], w1_recv.at[1])
        lap(0, 0, (1,))
        lap(0, 1, (1,))

    wait_bytes(abuf.at[0 : nz - 1], a_recv)
    total = jnp.zeros((srows + NORM_ROWS, HDIM), F32)
    for k in range(nz):
        rbuf[k] = total
        total = total + abuf[k].astype(F32)
    tsend[...] = total.astype(BF16)
    for step in far_first(ny):

        @pl.when(y + step < ny)
        def _():
            send(tsend, tbuf.at[y], t_send.at[step], t_recv.at[y], y_dev(y + step))

    if mz > 1:
        wait_bytes(w_all.at[0, 0 : mz - 1, 0:wh], w1_recv.at[0])
        lap(0, 0, (0,))
        lap(0, 1, (0,))

    for h in range(heads // 2):
        own_part(h)

    for k in range(ny - 1):

        @pl.when(k < y)
        def _():
            wait_bytes(tbuf.at[k], t_recv.at[k])

    base = tbuf[0].astype(F32)
    for k in range(1, ny):
        base = base + tbuf[k].astype(F32)
    for k in range(nz):
        pbuf[k] = (base[0:srows] + rbuf[k, 0:srows]).astype(BF16)
    pfx[z] = pbuf[z]
    for step in far_first(nz):
        to = ahead(z, step, nz)
        send(pbuf.at[to], pfx.at[z], p_send, p_recv.at[z], z_dev(to))
    norm_high, norm_low = split(base[srows : srows + NORM_ROWS] + rbuf[z, srows : srows + NORM_ROWS])

    for h in range(heads // 2, heads):
        own_part(h)

    for s in range(1, steps):
        lap(s, 0)
        lap(s, 1)


    def retrieve(h):
        query = qf[h]
        first = h * per_head
        for k in range(first, first + per_head):

            @pl.when(z != k)
            def _():
                wait_bytes(pfx.at[k], p_recv.at[k])

        state = pfx[first : first + per_head].reshape(HDIM, HDIM)
        numer = numer_l[h] + dot(query, state, NN)
        denom = (dot(query, norm_high, NT) + dot(query, norm_low, NT))[:, h : h + 1] + denom_l[h]
        gate = 1.0 / (1.0 + jnp.exp(-jnp.full((8, HDIM), gate_ref[c * heads + h], F32)))[0:1]
        value = gate * (numer / denom) + (1.0 - gate) * local_o[h]
        mixed[own_class, c * heads + h] = value.astype(BF16)

    split_n = 2 if heads > 1 else 1

    def mixed_part(cls, i):
        return mixed.at[cls, pl.ds(c * heads + i * (heads // split_n), heads // split_n)]

    group_copies, twin_copies = {}, {}

    def to_group(r, i):
        part = mixed_part(own_class, i)
        if r == 0:
            twin_copies[r, i] = send(part, part, m_send.at[r, i], m_recv.at[r, i], twin)
        else:
            group_copies[r, i] = send(part, part, g_send.at[r, i], g_recv.at[r, i], group_dev(*offsets[r], c))

    for i in range(split_n):
        for h in range(i * heads // split_n, (i + 1) * heads // split_n):
            retrieve(h)
        for r in range(min(3, len(offsets))):
            to_group(r, i)
    for i in range(split_n):
        for r in range(3, len(offsets)):
            to_group(r, i)

    state_copy.wait_send()
    norm_copy.wait_send()
    for copy in swaps:
        copy.wait_send()
    if mz > 1:
        wait_bytes(w_all.at[0, 0 : mz - 1, 0:wh], w1_send.at[0])
    if my > 1:
        wait_bytes(w_all.at[0 : my - 1, 0, wh:wc], w1_send.at[1])
    wait_bytes(sbuf.at[0 : nz - 1], a_send)
    for step in range(1, ny):

        @pl.when(y + step < ny)
        def _():
            wait_bytes(tsend, t_send.at[step])

    wait_bytes(pbuf.at[0 : nz - 1], p_send)
    for key in list(laps):
        arrived(key)
    for copy in laps.values():
        copy.wait_send()

    yx = my // nx

    def project(cls, xxs):
        both = jnp.concatenate([mixed[cls, h] for h in range(2 * heads)], axis=1)
        block = jnp.concatenate([w_all[pl.ds(xx * yx, yx)].reshape(yx * mz * wc, width) for xx in xxs])
        value = dot(both, block, NT)
        return [value[:, i * HDIM : (i + 1) * HDIM] for i in range(len(xxs))]

    x_copies = {}

    def hand_over(r):
        for i in range(split_n):
            part = mixed_part(class_of(*offsets[r]), i)
            group_copies[r, i].wait_recv()
            twin_copies[r, i] = send(part, part, m_send.at[r, i], m_recv.at[r, i], twin)

    done_copies, finished = [], set()

    def finish(r):
        if r in finished:
            return
        finished.add(r)
        total = sum_own[r]
        for step in x_order[:-1]:
            x_copies[r, step].wait_recv()
            total = total + x_in[r, step].astype(F32)
        total = total.astype(BF16)
        for e in range(2):
            dsend[r, e] = total[e * rows : (e + 1) * rows]
        place = fin.at[own_class * 2 + c]
        if r == 0:
            fin[own_class * 2 + c] = dsend[0, c]
            done_copies.append(send(dsend.at[0, 1 - c], place, d_send, d_recv, twin))
        else:
            for e in range(2):
                done_copies.append(send(dsend.at[r, e], place, d_send, d_recv, group_dev(*offsets[r], e)))

    for r, (dy, dz) in enumerate(offsets):
        cls = class_of(dy, dz)
        for i in range(split_n):
            twin_copies[r, i].wait_recv()
        for first in range(0, len(x_order), 2):
            part_steps = x_order[first : first + 2]
            for step, value in zip(part_steps, project(cls, [ahead(x, step, nx) for step in part_steps])):
                if step == 0:
                    sum_own[r] = value
                    continue
                x_out[r, step] = value.astype(BF16)
                x_copies[r, step] = send(
                    x_out.at[r, step], x_in.at[r, step], x_send.at[r, step], x_recv.at[r, step],
                    x_dev(ahead(x, step, nx)),
                )
        if r == 2:
            finish(0)
            finish(1)
        for later in {0: (1, 2), 2: (3,)}.get(r, ()):
            if later < len(offsets):
                hand_over(later)
        if r == 2:
            finish(2)
    for r in range(len(offsets)):
        finish(r)
    wait_bytes(fin.at[0 : len(done_copies)], d_recv)

    lane = lax.broadcasted_iota(jnp.int32, (rows, HDIM), 1)
    runs = HDIM // wc
    for b in range(out_ref.shape[1] // HDIM):
        value = jnp.zeros((rows, HDIM), F32)
        for k in range(runs):
            shard, e = divmod(b * runs + k, 2)
            yl, zz = divmod(shard, nz)
            pos = ((yl // gy) * mz + zz // gz) * wc
            piece = fin[((yl % gy) * gz + zz % gz) * 2 + e].astype(F32)
            shift = (k * wc - pos) % HDIM
            if shift:
                piece = pltpu.roll(piece, shift, 1)
            value = jnp.where(lane // wc == k, piece, value)
        out_ref[:, b * HDIM : (b + 1) * HDIM] = value.astype(BF16)

    for copies in (twin_copies.values(), group_copies.values(), x_copies.values()):
        for copy in copies:
            copy.wait_send()
    wait_bytes(fin.at[0 : len(done_copies)], d_send)


def local(grid, vk, vv, q, tk, tv, bounds, gate, w):
    ny, nz, nx, gy, gz = grid
    vlen, width = vk.shape
    rows = q.shape[0]
    half_w = width // 2
    heads = half_w // HDIM
    srows = half_w // nz
    wt = w.T
    wc = wt.shape[0]
    my, mz = ny // gy, nz // gz
    n = gy * gz
    assert (my // nx) * mz * wc == HDIM
    steps = max(my, mz, 2) // 2
    hbm = pl.BlockSpec(memory_space=pltpu.HBM)
    smem = pl.BlockSpec(memory_space=pltpu.SMEM)
    dma = pltpu.SemaphoreType.DMA
    slices = (nz, srows + NORM_ROWS, HDIM)
    states = (nz, srows, HDIM)
    per_head = (heads, 2 * rows, HDIM)
    return pl.pallas_call(
        functools.partial(kernel, ny, nz, nx, gy, gz),
        out_shape=jax.ShapeDtypeStruct((rows, 2 * n * HDIM), BF16),
        in_specs=[smem, smem] + [hbm] * 6,
        out_specs=pl.BlockSpec(memory_space=pltpu.VMEM),
        scratch_shapes=[
            pltpu.VMEM((my, mz, wc, width), BF16),
            pltpu.VMEM((2, vlen, half_w), BF16),
            pltpu.VMEM((vlen, half_w), BF16),
            pltpu.VMEM((2, vlen, half_w), BF16),
            pltpu.VMEM((2, rows, half_w), BF16),
            pltpu.VMEM((2, rows, half_w), BF16),
            pltpu.VMEM((2, rows, half_w), BF16),
            pltpu.VMEM((2, 8, HDIM), jnp.int32),
            pltpu.VMEM((2, vlen, half_w), BF16),
            pltpu.VMEM(per_head, BF16),
            pltpu.VMEM(states, BF16),
            pltpu.VMEM(states, BF16),
            pltpu.VMEM(states, F32),
            pltpu.VMEM((NORM_ROWS, HDIM), BF16),
            pltpu.VMEM((NORM_ROWS, HDIM), BF16),
            pltpu.VMEM((NORM_ROWS, HDIM), F32),
            pltpu.VMEM(slices, BF16),
            pltpu.VMEM(slices, BF16),
            pltpu.VMEM(slices, F32),
            pltpu.VMEM((ny, srows + NORM_ROWS, HDIM), BF16),
            pltpu.VMEM((srows + NORM_ROWS, HDIM), BF16),
            pltpu.VMEM(states, BF16),
            pltpu.VMEM(states, BF16),
            pltpu.VMEM(per_head, F32),
            pltpu.VMEM(per_head, F32),
            pltpu.VMEM(per_head, F32),
            pltpu.VMEM((n, 2 * heads, 2 * rows, HDIM), BF16),
            pltpu.VMEM((n, nx, 2 * rows, HDIM), BF16),
            pltpu.VMEM((n, nx, 2 * rows, HDIM), BF16),
            pltpu.VMEM((n, 2 * rows, HDIM), F32),
            pltpu.VMEM((n, 2, rows, HDIM), BF16),
            pltpu.VMEM((2 * n, rows, HDIM), BF16),
            dma((7,)),
            dma((4,)),
            dma,
            dma((6,)),
            dma((6,)),
            dma((2,)),
            dma((2,)),
            dma((2, 2, steps, 2)),
            dma((2, 2, steps, 2)),
            dma,
            dma,
            dma((ny,)),
            dma((ny,)),
            dma,
            dma((nz,)),
            dma((n, 2)),
            dma((n, 2)),
            dma((n, 2)),
            dma((n, 2)),
            dma((n, nx)),
            dma((n, nx)),
            dma,
            dma,
        ],
        compiler_params=pltpu.CompilerParams(
            collective_id=0, has_side_effects=True, vmem_limit_bytes=60 * 1024 * 1024
        ),
    )(bounds, gate, vk, vv, q, tk, tv, wt)


def solution(mesh):
    nx = mesh.shape["head"]
    specs = (
        P("tm", "head"),
        P("tm", "head"),
        P("tm", "head"),
        P("tm", "head"),
        P("tm", "head"),
        P("tm"),
        P("head"),
        P("head", "tm"),
    )
    return jax.shard_map(
        functools.partial(local, (8, mesh.shape["tm"] // 16, nx, 2, 2)),
        mesh=mesh,
        in_specs=specs,
        out_specs=P("tm", "head"),
        check_vma=False,
    )
```

```python
import functools

import jax
import jax.numpy as jnp
from jax import lax
from jax.experimental import pallas as pl
from jax.experimental.pallas import tpu as pltpu
from jax.sharding import PartitionSpec as P

MESH = pl.DeviceIdType.MESH
F32 = jnp.float32
BF16 = jnp.bfloat16
HDIM = 128
NORM_ROWS = 16
NN = (((1,), (0,)), ((), ()))
NT = (((1,), (1,)), ((), ()))
TN = (((0,), (0,)), ((), ()))


def dot(a, b, dims):
    return lax.dot_general(a, b, dims, preferred_element_type=F32)


def elu_one(values):
    return jnp.where(values > 0, values + 1.0, jnp.exp(jnp.minimum(values, 0.0)))


def split(value):
    high = value.astype(BF16)
    return high, (value - high.astype(F32)).astype(BF16)


def wait_bytes(ref, sem):
    pltpu.make_async_copy(ref, ref, sem).wait()


def kernel(
    ny,
    nz,
    nx,
    gy,
    gz,
    bound_ref,
    gate_ref,
    vk_ref,
    vv_ref,
    q_ref,
    tk_ref,
    tv_ref,
    w_ref,
    out_ref,
    w_all,
    kin,
    vown,
    vin,
    qin,
    tkin,
    tvin,
    bin_,
    kf,
    qf,
    s_send,
    s_recv,
    s_own,
    n_send,
    n_recv,
    n_own,
    sbuf,
    abuf,
    rbuf,
    tbuf,
    tsend,
    pbuf,
    pfx,
    numer_l,
    denom_l,
    local_o,
    mixed,
    x_out,
    x_in,
    sum_own,
    dsend,
    fin,
    in_sem,
    s_sem,
    w_sem,
    c_send,
    c_recv,
    w1_send,
    w1_recv,
    w2_send,
    w2_recv,
    a_send,
    a_recv,
    t_send,
    t_recv,
    p_send,
    p_recv,
    g_send,
    g_recv,
    m_send,
    m_recv,
    x_send,
    x_recv,
    d_send,
    d_recv,
):
    tm = lax.axis_index("tm")
    x = lax.axis_index("head")
    c = lax.rem(tm, 2)
    chip = tm // 2
    z = lax.rem(chip, nz)
    y = chip // nz

    vlen, width = vk_ref.shape
    rows = q_ref.shape[0]
    half_w = width // 2
    heads = half_w // HDIM
    per_head = nz // heads
    srows = HDIM // per_head
    wc = w_ref.shape[0]
    wh = wc // 2
    my, mz = ny // gy, nz // gz
    py, pz = lax.rem(y, gy), lax.rem(z, gz)
    yc, zc = y // gy, z // gz
    own_class = py * gz + pz
    offsets = [(dy, dz) for dy in range(gy) for dz in range(gz)]
    offsets.sort(key=lambda o: (o[0] + o[1], o[1]))

    def dev(t, xx):
        return {"tm": t, "head": xx}

    def y_dev(yy):
        return dev((yy * nz + z) * 2 + c, x)

    def z_dev(zz):
        return dev((y * nz + zz) * 2 + c, x)

    def x_dev(xx):
        return dev(tm, xx)

    def group_dev(dy, dz, core):
        yy = yc * gy + lax.rem(py + dy, gy)
        zz = zc * gz + lax.rem(pz + dz, gz)
        return dev((yy * nz + zz) * 2 + core, x)

    def class_of(dy, dz):
        return lax.rem(py + dy, gy) * gz + lax.rem(pz + dz, gz)

    twin = dev(tm + 1 - 2 * c, x)

    def ahead(me, step, n):
        return lax.rem(me + step, n)

    def send(src, dst, send_sem, recv_sem, device):
        copy = pltpu.make_async_remote_copy(
            src, dst, send_sem, recv_sem, device_id=device, device_id_type=MESH
        )
        copy.start()
        return copy

    mine = pl.ds(pl.multiple_of(c * half_w, HDIM), half_w)
    other = pl.ds(pl.multiple_of((1 - c) * half_w, HDIM), half_w)
    inputs = ((vk_ref, kin), (vv_ref, vin), (q_ref, qin), (tk_ref, tkin), (tv_ref, tvin))
    loads = [
        pltpu.make_async_copy(vk_ref.at[:, other], kin.at[0], in_sem.at[0]),
        pltpu.make_async_copy(vv_ref.at[:, other], vown, in_sem.at[1]),
        pltpu.make_async_copy(vk_ref.at[:, mine], kin.at[1], in_sem.at[5]),
        pltpu.make_async_copy(vv_ref.at[:, mine], vin.at[c], in_sem.at[6]),
    ] + [
        pltpu.make_async_copy(src.at[:, mine], dst.at[c], in_sem.at[i + 2])
        for i, (src, dst) in enumerate(inputs[2:])
    ]
    for load in loads:
        load.start()
    own_w = pltpu.make_async_copy(w_ref, w_all.at[yc, zc], w_sem)
    own_w.start()

    def far_first(n):
        return sorted(range(1, n), key=lambda step: -min(step, n - step))

    barrier = pltpu.get_barrier_semaphore()

    def greet(device):
        pl.semaphore_signal(barrier, inc=1, device_id=device, device_id_type=MESH)

    for step in far_first(nz):
        greet(z_dev(ahead(z, step, nz)))
    for step in far_first(ny):
        greet(y_dev(ahead(y, step, ny)))
    x_order = far_first(nx) + [0]
    for step in x_order[:-1]:
        greet(x_dev(ahead(x, step, nx)))
    greeted = 1 + (nz - 1) + (ny - 1) + (nx - 1)
    for dy, dz in offsets[1:]:
        greet(group_dev(dy, dz, 1 - c))
        greeted += 1
        if dy and dz:
            greet(group_dev(dy, dz, c))
            greeted += 1
    greet(twin)
    bin_[c] = jnp.full((8, HDIM), bound_ref[0], jnp.int32)

    loads[0].wait()
    kin[0] = elu_one(kin[0].astype(F32)).astype(BF16)
    loads[1].wait()
    ones = jnp.ones((NORM_ROWS, vlen), BF16)
    norm_row = lax.broadcasted_iota(jnp.int32, (NORM_ROWS, HDIM), 0)

    def own_state(keys, values):
        norms = jnp.zeros((NORM_ROWS, HDIM), F32)
        states = []
        for h in range(heads):
            cols = slice(h * HDIM, (h + 1) * HDIM)
            states.append(dot(keys[:, cols], values[:, cols], TN))
            norms = jnp.where(norm_row == h, dot(ones, keys[:, cols], NN), norms)
        return states, norms

    states, norms = own_state(kin.at[0], vown)
    for h in range(heads):
        for k in range(per_head):
            s_send[h * per_head + k] = states[h][k * srows : (k + 1) * srows].astype(BF16)
    n_send[...] = norms.astype(BF16)
    for k in range(ny):

        @pl.when(k >= y)
        def _():
            tbuf[k] = jnp.zeros(tbuf.shape[1:], BF16)

    pl.semaphore_wait(barrier, greeted)
    state_copy = send(s_send, s_recv, s_sem.at[0], s_sem.at[1], twin)
    norm_copy = send(n_send, n_recv, s_sem.at[2], s_sem.at[3], twin)
    def y_class(k):
        return y_dev(k * gy + py)

    def z_class(k):
        return z_dev(k * gz + pz)

    for step in far_first(mz):
        send(w_ref.at[0:wh], w_all.at[yc, zc, 0:wh], w1_send.at[0], w1_recv.at[0], z_class(ahead(zc, step, mz)))
    for step in far_first(my):
        send(w_ref.at[wh:wc], w_all.at[yc, zc, wh:wc], w1_send.at[1], w1_recv.at[1], y_class(ahead(yc, step, my)))

    loads[2].wait()
    kf[c] = elu_one(kin[1].astype(F32)).astype(BF16)
    loads[3].wait()
    states, norms = own_state(kf.at[c], vin.at[c])
    for h in range(heads):
        for k in range(per_head):
            s_own[h * per_head + k] = states[h][k * srows : (k + 1) * srows]
    n_own[...] = norms
    state_copy.wait_recv()
    norm_copy.wait_recv()
    norms = (n_own[...] + n_recv[...].astype(F32)).astype(BF16)
    for k in range(nz):
        sbuf[k, 0:srows] = (s_own[k] + s_recv[k].astype(F32)).astype(BF16)
        sbuf[k, srows : srows + NORM_ROWS] = norms
    for step in far_first(nz):
        to = ahead(z, step, nz)
        send(sbuf.at[to], abuf.at[z], a_send, a_recv, z_dev(to))
    abuf[z] = sbuf[z]

    swaps = [send(kin.at[0], kf.at[c], c_send.at[0], c_recv.at[0], twin)]
    swaps += [
        send(src.at[:, other], dst.at[c], c_send.at[i + 1], c_recv.at[i + 1], twin)
        for i, (src, dst) in enumerate(inputs[1:])
    ]
    swaps.append(send(bin_.at[c], bin_.at[c], c_send.at[5], c_recv.at[5], twin))

    def bundle(half, index, q):
        if half == 0:
            return w_all.at[index, q * (mz // 2) : (q + 1) * (mz // 2), 0:wh]
        return w_all.at[q * (my // 2) : (q + 1) * (my // 2), index, wh:wc]

    laps = {}
    waited = set()

    def arrived(key):
        if key in laps and key not in waited:
            waited.add(key)
            laps[key].wait_recv()

    def lap(s, q, halves=(0, 1)):
        for half in halves:
            for way in range(2):
                n, me = (my, yc) if half == 0 else (mz, zc)
                if s >= n // 2 or (s == n // 2 - 1 and q != way):
                    continue
                arrived((half, way, s - 1, q))
                block = ahead(me, n - s, n) if way == 0 else ahead(me, s, n)
                to = ahead(me, 1, n) if way == 0 else ahead(me, n - 1, n)
                part = bundle(half, block, q)
                laps[(half, way, s, q)] = send(
                    part, part, w2_send.at[half, way, s, q], w2_recv.at[half, way, s, q],
                    y_class(to) if half == 0 else z_class(to),
                )

    row_ids = lax.broadcasted_iota(jnp.int32, (2 * rows, HDIM), 0)
    col_ids = lax.broadcasted_iota(jnp.int32, (2 * rows, HDIM), 1)

    def own_part(h, bounds):
        cols = slice(h * HDIM, (h + 1) * HDIM)
        query = qin[:, :, cols].reshape(2 * rows, HDIM)
        q_feat = elu_one(query.astype(F32)).astype(BF16)
        qf[h] = q_feat
        numer = jnp.zeros((2 * rows, HDIM), F32)
        denom = jnp.zeros((2 * rows, 1), F32)
        for e in range(2):
            weight = dot(q_feat, kf[e, :, cols], NT)
            weight = jnp.where(col_ids + (chip * 2 + e) * vlen < bounds, weight, 0.0)
            high, low = split(weight)
            values = vin[e, :, cols]
            numer = numer + dot(high, values, NN) + dot(low, values, NN)
            denom = denom + jnp.sum(weight, axis=1, keepdims=True)
        numer_l[h] = numer
        denom_l[h] = jnp.broadcast_to(denom, (2 * rows, HDIM))
        scores = dot(query, tkin[:, :, cols].reshape(2 * rows, HDIM), NT) * (float(HDIM) ** -0.5)
        causal = jnp.logical_and(col_ids <= row_ids, col_ids // rows == row_ids // rows)
        scores = jnp.where(causal, scores, -jnp.inf)
        expo = jnp.exp(scores - jnp.max(scores, axis=1, keepdims=True))
        probs = (expo / jnp.sum(expo, axis=1, keepdims=True)).astype(BF16)
        local_o[h] = dot(probs, tvin[:, :, cols].reshape(2 * rows, HDIM), NN)

    steps = max(my, mz) // 2
    own_w.wait()
    if my > 1:
        wait_bytes(w_all.at[0 : my - 1, 0, wh:wc], w1_recv.at[1])
        lap(0, 0, (1,))
        lap(0, 1, (1,))

    wait_bytes(abuf.at[0 : nz - 1], a_recv)
    total = jnp.zeros((srows + NORM_ROWS, HDIM), F32)
    for k in range(nz):
        rbuf[k] = total
        total = total + abuf[k].astype(F32)
    tsend[...] = total.astype(BF16)
    for step in far_first(ny):

        @pl.when(y + step < ny)
        def _():
            send(tsend, tbuf.at[y], t_send.at[step], t_recv.at[y], y_dev(y + step))

    if mz > 1:
        wait_bytes(w_all.at[0, 0 : mz - 1, 0:wh], w1_recv.at[0])
        lap(0, 0, (0,))
        lap(0, 1, (0,))

    for k in range(ny - 1):

        @pl.when(k < y)
        def _():
            wait_bytes(tbuf.at[k], t_recv.at[k])

    base = tbuf[0].astype(F32)
    for k in range(1, ny):
        base = base + tbuf[k].astype(F32)
    for k in range(nz):
        pbuf[k] = (base[0:srows] + rbuf[k, 0:srows]).astype(BF16)
    pfx[z] = pbuf[z]
    for step in far_first(nz):
        to = ahead(z, step, nz)
        send(pbuf.at[to], pfx.at[z], p_send, p_recv, z_dev(to))
    norm_high, norm_low = split(base[srows : srows + NORM_ROWS] + rbuf[z, srows : srows + NORM_ROWS])

    for load in loads[4:]:
        load.wait()
    for swap in swaps:
        swap.wait_recv()
    bounds = jnp.concatenate(
        [jnp.broadcast_to(bin_[0, 0:1, :], (rows, HDIM)), jnp.broadcast_to(bin_[1, 0:1, :], (rows, HDIM))]
    )
    for h in range(heads):
        own_part(h, bounds)

    for s in range(1, steps):
        lap(s, 0)
        lap(s, 1)

    wait_bytes(pfx.at[0 : nz - 1], p_recv)

    def retrieve(h):
        query = qf[h]
        first = h * per_head
        state = pfx[first : first + per_head].reshape(HDIM, HDIM)
        numer = numer_l[h] + dot(query, state, NN)
        denom = (dot(query, norm_high, NT) + dot(query, norm_low, NT))[:, h : h + 1] + denom_l[h]
        gate = 1.0 / (1.0 + jnp.exp(-jnp.full((8, HDIM), gate_ref[c * heads + h], F32)))[0:1]
        value = gate * (numer / denom) + (1.0 - gate) * local_o[h]
        mixed[own_class, c * heads + h] = value.astype(BF16)

    split_n = 2 if heads > 1 else 1

    def mixed_part(cls, i):
        return mixed.at[cls, pl.ds(c * heads + i * (heads // split_n), heads // split_n)]

    group_copies, twin_copies = {}, {}
    for i in range(split_n):
        for h in range(i * heads // split_n, (i + 1) * heads // split_n):
            retrieve(h)
        part = mixed_part(own_class, i)
        for r, (dy, dz) in reversed(list(enumerate(offsets))):
            if r == 0:
                twin_copies[r, i] = send(part, part, m_send.at[r, i], m_recv.at[r, i], twin)
            else:
                group_copies[r, i] = send(part, part, g_send.at[r, i], g_recv.at[r, i], group_dev(dy, dz, c))
    state_copy.wait_send()
    norm_copy.wait_send()
    for copy in swaps:
        copy.wait_send()
    if mz > 1:
        wait_bytes(w_all.at[0, 0 : mz - 1, 0:wh], w1_send.at[0])
    if my > 1:
        wait_bytes(w_all.at[0 : my - 1, 0, wh:wc], w1_send.at[1])
    wait_bytes(sbuf.at[0 : nz - 1], a_send)
    for step in range(1, ny):

        @pl.when(y + step < ny)
        def _():
            wait_bytes(tsend, t_send.at[step])

    wait_bytes(pbuf.at[0 : nz - 1], p_send)
    for key in list(laps):
        arrived(key)
    for copy in laps.values():
        copy.wait_send()

    yx = my // nx

    def project(cls, xxs):
        both = jnp.concatenate([mixed[cls, h] for h in range(2 * heads)], axis=1)
        block = jnp.concatenate([w_all[pl.ds(xx * yx, yx)].reshape(yx * mz * wc, width) for xx in xxs])
        value = dot(both, block, NT)
        return [value[:, i * HDIM : (i + 1) * HDIM] for i in range(len(xxs))]

    x_copies = {}

    def hand_over(r):
        for i in range(split_n):
            part = mixed_part(class_of(*offsets[r]), i)
            group_copies[r, i].wait_recv()
            twin_copies[r, i] = send(part, part, m_send.at[r, i], m_recv.at[r, i], twin)

    done_copies, finished = [], set()

    def finish(r):
        if r in finished:
            return
        finished.add(r)
        total = sum_own[r]
        for step in x_order[:-1]:
            x_copies[r, step].wait_recv()
            total = total + x_in[r, step].astype(F32)
        total = total.astype(BF16)
        for e in range(2):
            dsend[r, e] = total[e * rows : (e + 1) * rows]
        place = fin.at[own_class * 2 + c]
        if r == 0:
            fin[own_class * 2 + c] = dsend[0, c]
            done_copies.append(send(dsend.at[0, 1 - c], place, d_send, d_recv, twin))
        else:
            for e in range(2):
                done_copies.append(send(dsend.at[r, e], place, d_send, d_recv, group_dev(*offsets[r], e)))

    for r, (dy, dz) in enumerate(offsets):
        cls = class_of(dy, dz)
        for i in range(split_n):
            twin_copies[r, i].wait_recv()
        for first in range(0, len(x_order), 2):
            part_steps = x_order[first : first + 2]
            for step, value in zip(part_steps, project(cls, [ahead(x, step, nx) for step in part_steps])):
                if step == 0:
                    sum_own[r] = value
                    continue
                x_out[r, step] = value.astype(BF16)
                x_copies[r, step] = send(
                    x_out.at[r, step], x_in.at[r, step], x_send.at[r, step], x_recv.at[r, step],
                    x_dev(ahead(x, step, nx)),
                )
        for later in {0: (1, 2), 1: (3,)}.get(r, ()):
            if later < len(offsets):
                hand_over(later)
        if r == 2:
            finish(0)
    for r in range(len(offsets)):
        finish(r)
    wait_bytes(fin.at[0 : len(done_copies)], d_recv)

    lane = lax.broadcasted_iota(jnp.int32, (rows, HDIM), 1)
    runs = HDIM // wc
    for b in range(out_ref.shape[1] // HDIM):
        value = jnp.zeros((rows, HDIM), F32)
        for k in range(runs):
            shard, e = divmod(b * runs + k, 2)
            yl, zz = divmod(shard, nz)
            pos = ((yl // gy) * mz + zz // gz) * wc
            piece = fin[((yl % gy) * gz + zz % gz) * 2 + e].astype(F32)
            shift = (k * wc - pos) % HDIM
            if shift:
                piece = pltpu.roll(piece, shift, 1)
            value = jnp.where(lane // wc == k, piece, value)
        out_ref[:, b * HDIM : (b + 1) * HDIM] = value.astype(BF16)

    for copies in (twin_copies.values(), group_copies.values(), x_copies.values()):
        for copy in copies:
            copy.wait_send()
    wait_bytes(fin.at[0 : len(done_copies)], d_send)


def local(grid, vk, vv, q, tk, tv, bounds, gate, w):
    ny, nz, nx, gy, gz = grid
    vlen, width = vk.shape
    rows = q.shape[0]
    half_w = width // 2
    heads = half_w // HDIM
    srows = half_w // nz
    wt = w.T
    wc = wt.shape[0]
    my, mz = ny // gy, nz // gz
    n = gy * gz
    assert (my // nx) * mz * wc == HDIM
    steps = max(my, mz, 2) // 2
    hbm = pl.BlockSpec(memory_space=pltpu.HBM)
    smem = pl.BlockSpec(memory_space=pltpu.SMEM)
    dma = pltpu.SemaphoreType.DMA
    slices = (nz, srows + NORM_ROWS, HDIM)
    states = (nz, srows, HDIM)
    per_head = (heads, 2 * rows, HDIM)
    return pl.pallas_call(
        functools.partial(kernel, ny, nz, nx, gy, gz),
        out_shape=jax.ShapeDtypeStruct((rows, 2 * n * HDIM), BF16),
        in_specs=[smem, smem] + [hbm] * 6,
        out_specs=pl.BlockSpec(memory_space=pltpu.VMEM),
        scratch_shapes=[
            pltpu.VMEM((my, mz, wc, width), BF16),
            pltpu.VMEM((2, vlen, half_w), BF16),
            pltpu.VMEM((vlen, half_w), BF16),
            pltpu.VMEM((2, vlen, half_w), BF16),
            pltpu.VMEM((2, rows, half_w), BF16),
            pltpu.VMEM((2, rows, half_w), BF16),
            pltpu.VMEM((2, rows, half_w), BF16),
            pltpu.VMEM((2, 8, HDIM), jnp.int32),
            pltpu.VMEM((2, vlen, half_w), BF16),
            pltpu.VMEM(per_head, BF16),
            pltpu.VMEM(states, BF16),
            pltpu.VMEM(states, BF16),
            pltpu.VMEM(states, F32),
            pltpu.VMEM((NORM_ROWS, HDIM), BF16),
            pltpu.VMEM((NORM_ROWS, HDIM), BF16),
            pltpu.VMEM((NORM_ROWS, HDIM), F32),
            pltpu.VMEM(slices, BF16),
            pltpu.VMEM(slices, BF16),
            pltpu.VMEM(slices, F32),
            pltpu.VMEM((ny, srows + NORM_ROWS, HDIM), BF16),
            pltpu.VMEM((srows + NORM_ROWS, HDIM), BF16),
            pltpu.VMEM(states, BF16),
            pltpu.VMEM(states, BF16),
            pltpu.VMEM(per_head, F32),
            pltpu.VMEM(per_head, F32),
            pltpu.VMEM(per_head, F32),
            pltpu.VMEM((n, 2 * heads, 2 * rows, HDIM), BF16),
            pltpu.VMEM((n, nx, 2 * rows, HDIM), BF16),
            pltpu.VMEM((n, nx, 2 * rows, HDIM), BF16),
            pltpu.VMEM((n, 2 * rows, HDIM), F32),
            pltpu.VMEM((n, 2, rows, HDIM), BF16),
            pltpu.VMEM((2 * n, rows, HDIM), BF16),
            dma((7,)),
            dma((4,)),
            dma,
            dma((6,)),
            dma((6,)),
            dma((2,)),
            dma((2,)),
            dma((2, 2, steps, 2)),
            dma((2, 2, steps, 2)),
            dma,
            dma,
            dma((ny,)),
            dma((ny,)),
            dma,
            dma,
            dma((n, 2)),
            dma((n, 2)),
            dma((n, 2)),
            dma((n, 2)),
            dma((n, nx)),
            dma((n, nx)),
            dma,
            dma,
        ],
        compiler_params=pltpu.CompilerParams(
            collective_id=0, has_side_effects=True, vmem_limit_bytes=60 * 1024 * 1024
        ),
    )(bounds, gate, vk, vv, q, tk, tv, wt)


def solution(mesh):
    nx = mesh.shape["head"]
    specs = (
        P("tm", "head"),
        P("tm", "head"),
        P("tm", "head"),
        P("tm", "head"),
        P("tm", "head"),
        P("tm"),
        P("head"),
        P("head", "tm"),
    )
    return jax.shard_map(
        functools.partial(local, (8, mesh.shape["tm"] // 16, nx, 2, 2)),
        mesh=mesh,
        in_specs=specs,
        out_specs=P("tm", "head"),
        check_vma=False,
    )
```

```python
import functools

import jax
import jax.numpy as jnp
from jax import lax
from jax.experimental import pallas as pl
from jax.experimental.pallas import tpu as pltpu
from jax.sharding import PartitionSpec as P

MESH = pl.DeviceIdType.MESH
F32 = jnp.float32
BF16 = jnp.bfloat16
HDIM = 128
NORM_ROWS = 16
NN = (((1,), (0,)), ((), ()))
NT = (((1,), (1,)), ((), ()))
TN = (((0,), (0,)), ((), ()))


def dot(a, b, dims):
    return lax.dot_general(a, b, dims, preferred_element_type=F32)


def elu_one(values):
    return jnp.where(values > 0, values + 1.0, jnp.exp(jnp.minimum(values, 0.0)))


def split(value):
    high = value.astype(BF16)
    return high, (value - high.astype(F32)).astype(BF16)


def wait_bytes(ref, sem):
    pltpu.make_async_copy(ref, ref, sem).wait()


def kernel(
    ny,
    nz,
    nx,
    gy,
    gz,
    bound_ref,
    gate_ref,
    vk_ref,
    vv_ref,
    q_ref,
    tk_ref,
    tv_ref,
    w_ref,
    out_ref,
    w_all,
    kin,
    vown,
    vin,
    qin,
    tkin,
    tvin,
    bin_,
    kf,
    qf,
    s_send,
    s_recv,
    s_own,
    n_send,
    n_recv,
    n_own,
    sbuf,
    abuf,
    rbuf,
    tbuf,
    tsend,
    pbuf,
    pfx,
    numer_l,
    denom_l,
    local_o,
    mixed,
    x_out,
    x_in,
    sum_own,
    dsend,
    fin,
    in_sem,
    s_sem,
    w_sem,
    c_send,
    c_recv,
    w1_send,
    w1_recv,
    w2_send,
    w2_recv,
    a_send,
    a_recv,
    t_send,
    t_recv,
    p_send,
    p_recv,
    g_send,
    g_recv,
    m_send,
    m_recv,
    x_send,
    x_recv,
    d_send,
    d_recv,
):
    tm = lax.axis_index("tm")
    x = lax.axis_index("head")
    c = lax.rem(tm, 2)
    chip = tm // 2
    z = lax.rem(chip, nz)
    y = chip // nz

    vlen, width = vk_ref.shape
    rows = q_ref.shape[0]
    half_w = width // 2
    heads = half_w // HDIM
    per_head = nz // heads
    srows = HDIM // per_head
    wc = w_ref.shape[0]
    wh = wc // 2
    my, mz = ny // gy, nz // gz
    py, pz = lax.rem(y, gy), lax.rem(z, gz)
    yc, zc = y // gy, z // gz
    own_class = py * gz + pz
    offsets = [(dy, dz) for dy in range(gy) for dz in range(gz)]
    offsets.sort(key=lambda o: (o[0] + o[1], o[1]))

    def dev(t, xx):
        return {"tm": t, "head": xx}

    def y_dev(yy):
        return dev((yy * nz + z) * 2 + c, x)

    def z_dev(zz):
        return dev((y * nz + zz) * 2 + c, x)

    def x_dev(xx):
        return dev(tm, xx)

    def group_dev(dy, dz, core):
        yy = yc * gy + lax.rem(py + dy, gy)
        zz = zc * gz + lax.rem(pz + dz, gz)
        return dev((yy * nz + zz) * 2 + core, x)

    def class_of(dy, dz):
        return lax.rem(py + dy, gy) * gz + lax.rem(pz + dz, gz)

    twin = dev(tm + 1 - 2 * c, x)

    def ahead(me, step, n):
        return lax.rem(me + step, n)

    def send(src, dst, send_sem, recv_sem, device):
        copy = pltpu.make_async_remote_copy(
            src, dst, send_sem, recv_sem, device_id=device, device_id_type=MESH
        )
        copy.start()
        return copy

    mine = pl.ds(pl.multiple_of(c * half_w, HDIM), half_w)
    other = pl.ds(pl.multiple_of((1 - c) * half_w, HDIM), half_w)
    inputs = ((vk_ref, kin), (vv_ref, vin), (q_ref, qin), (tk_ref, tkin), (tv_ref, tvin))
    loads = [
        pltpu.make_async_copy(vk_ref.at[:, other], kin.at[0], in_sem.at[0]),
        pltpu.make_async_copy(vv_ref.at[:, other], vown, in_sem.at[1]),
        pltpu.make_async_copy(vk_ref.at[:, mine], kin.at[1], in_sem.at[5]),
        pltpu.make_async_copy(vv_ref.at[:, mine], vin.at[c], in_sem.at[6]),
    ] + [
        pltpu.make_async_copy(src.at[:, mine], dst.at[c], in_sem.at[i + 2])
        for i, (src, dst) in enumerate(inputs[2:])
    ]
    for load in loads:
        load.start()
    own_w = pltpu.make_async_copy(w_ref, w_all.at[yc, zc], w_sem)
    own_w.start()

    def far_first(n):
        return sorted(range(1, n), key=lambda step: -min(step, n - step))

    barrier = pltpu.get_barrier_semaphore()

    def greet(device):
        pl.semaphore_signal(barrier, inc=1, device_id=device, device_id_type=MESH)

    for step in far_first(nz):
        greet(z_dev(ahead(z, step, nz)))
    for step in far_first(ny):
        greet(y_dev(ahead(y, step, ny)))
    x_order = far_first(nx) + [0]
    for step in x_order[:-1]:
        greet(x_dev(ahead(x, step, nx)))
    greeted = 1 + (nz - 1) + (ny - 1) + (nx - 1)
    for dy, dz in offsets[1:]:
        greet(group_dev(dy, dz, 1 - c))
        greeted += 1
        if dy and dz:
            greet(group_dev(dy, dz, c))
            greeted += 1
    greet(twin)
    bin_[c] = jnp.full((8, HDIM), bound_ref[0], jnp.int32)

    loads[0].wait()
    kin[0] = elu_one(kin[0].astype(F32)).astype(BF16)
    loads[1].wait()
    ones = jnp.ones((NORM_ROWS, vlen), BF16)
    norm_row = lax.broadcasted_iota(jnp.int32, (NORM_ROWS, HDIM), 0)

    def own_state(keys, values):
        norms = jnp.zeros((NORM_ROWS, HDIM), F32)
        states = []
        for h in range(heads):
            cols = slice(h * HDIM, (h + 1) * HDIM)
            states.append(dot(keys[:, cols], values[:, cols], TN))
            norms = jnp.where(norm_row == h, dot(ones, keys[:, cols], NN), norms)
        return states, norms

    states, norms = own_state(kin.at[0], vown)
    for h in range(heads):
        for k in range(per_head):
            s_send[h * per_head + k] = states[h][k * srows : (k + 1) * srows].astype(BF16)
    n_send[...] = norms.astype(BF16)
    for k in range(ny):

        @pl.when(k >= y)
        def _():
            tbuf[k] = jnp.zeros(tbuf.shape[1:], BF16)

    pl.semaphore_wait(barrier, greeted)
    state_copy = send(s_send, s_recv, s_sem.at[0], s_sem.at[1], twin)
    norm_copy = send(n_send, n_recv, s_sem.at[2], s_sem.at[3], twin)
    def y_class(k):
        return y_dev(k * gy + py)

    def z_class(k):
        return z_dev(k * gz + pz)

    for step in far_first(my):
        send(w_ref.at[wh:wc], w_all.at[yc, zc, wh:wc], w1_send.at[1], w1_recv.at[1], y_class(ahead(yc, step, my)))

    loads[2].wait()
    kf[c] = elu_one(kin[1].astype(F32)).astype(BF16)
    loads[3].wait()
    states, norms = own_state(kf.at[c], vin.at[c])
    for h in range(heads):
        for k in range(per_head):
            s_own[h * per_head + k] = states[h][k * srows : (k + 1) * srows]
    n_own[...] = norms
    state_copy.wait_recv()
    norm_copy.wait_recv()
    norms = (n_own[...] + n_recv[...].astype(F32)).astype(BF16)
    for k in range(nz):
        sbuf[k, 0:srows] = (s_own[k] + s_recv[k].astype(F32)).astype(BF16)
        sbuf[k, srows : srows + NORM_ROWS] = norms
    for step in far_first(nz):
        to = ahead(z, step, nz)
        send(sbuf.at[to], abuf.at[z], a_send, a_recv, z_dev(to))
    abuf[z] = sbuf[z]
    for step in far_first(mz):
        send(w_ref.at[0:wh], w_all.at[yc, zc, 0:wh], w1_send.at[0], w1_recv.at[0], z_class(ahead(zc, step, mz)))

    swaps = [send(kin.at[0], kf.at[c], c_send.at[0], c_recv.at[0], twin)]
    swaps += [
        send(src.at[:, other], dst.at[c], c_send.at[i + 1], c_recv.at[i + 1], twin)
        for i, (src, dst) in enumerate(inputs[1:])
    ]
    swaps.append(send(bin_.at[c], bin_.at[c], c_send.at[5], c_recv.at[5], twin))

    def bundle(half, index, q):
        if half == 0:
            return w_all.at[index, q * (mz // 2) : (q + 1) * (mz // 2), 0:wh]
        return w_all.at[q * (my // 2) : (q + 1) * (my // 2), index, wh:wc]

    laps = {}
    waited = set()

    def arrived(key):
        if key in laps and key not in waited:
            waited.add(key)
            laps[key].wait_recv()

    def lap(s, q, halves=(0, 1)):
        for half in halves:
            for way in range(2):
                n, me = (my, yc) if half == 0 else (mz, zc)
                if s >= n // 2 or (s == n // 2 - 1 and q != way):
                    continue
                arrived((half, way, s - 1, q))
                block = ahead(me, n - s, n) if way == 0 else ahead(me, s, n)
                to = ahead(me, 1, n) if way == 0 else ahead(me, n - 1, n)
                part = bundle(half, block, q)
                laps[(half, way, s, q)] = send(
                    part, part, w2_send.at[half, way, s, q], w2_recv.at[half, way, s, q],
                    y_class(to) if half == 0 else z_class(to),
                )

    row_ids = lax.broadcasted_iota(jnp.int32, (2 * rows, HDIM), 0)
    col_ids = lax.broadcasted_iota(jnp.int32, (2 * rows, HDIM), 1)

    def own_part(h, bounds):
        cols = slice(h * HDIM, (h + 1) * HDIM)
        query = qin[:, :, cols].reshape(2 * rows, HDIM)
        q_feat = elu_one(query.astype(F32)).astype(BF16)
        qf[h] = q_feat
        numer = jnp.zeros((2 * rows, HDIM), F32)
        denom = jnp.zeros((2 * rows, 1), F32)
        for e in range(2):
            weight = dot(q_feat, kf[e, :, cols], NT)
            weight = jnp.where(col_ids + (chip * 2 + e) * vlen < bounds, weight, 0.0)
            high, low = split(weight)
            values = vin[e, :, cols]
            numer = numer + dot(high, values, NN) + dot(low, values, NN)
            denom = denom + jnp.sum(weight, axis=1, keepdims=True)
        numer_l[h] = numer
        denom_l[h] = jnp.broadcast_to(denom, (2 * rows, HDIM))
        scores = dot(query, tkin[:, :, cols].reshape(2 * rows, HDIM), NT) * (float(HDIM) ** -0.5)
        causal = jnp.logical_and(col_ids <= row_ids, col_ids // rows == row_ids // rows)
        scores = jnp.where(causal, scores, -jnp.inf)
        expo = jnp.exp(scores - jnp.max(scores, axis=1, keepdims=True))
        probs = (expo / jnp.sum(expo, axis=1, keepdims=True)).astype(BF16)
        local_o[h] = dot(probs, tvin[:, :, cols].reshape(2 * rows, HDIM), NN)

    steps = max(my, mz) // 2
    own_w.wait()
    if my > 1:
        wait_bytes(w_all.at[0 : my - 1, 0, wh:wc], w1_recv.at[1])
        lap(0, 0, (1,))
        lap(0, 1, (1,))

    wait_bytes(abuf.at[0 : nz - 1], a_recv)
    total = jnp.zeros((srows + NORM_ROWS, HDIM), F32)
    for k in range(nz):
        rbuf[k] = total
        total = total + abuf[k].astype(F32)
    tsend[...] = total.astype(BF16)
    for step in far_first(ny):

        @pl.when(y + step < ny)
        def _():
            send(tsend, tbuf.at[y], t_send.at[step], t_recv.at[y], y_dev(y + step))

    if mz > 1:
        wait_bytes(w_all.at[0, 0 : mz - 1, 0:wh], w1_recv.at[0])
        lap(0, 0, (0,))
        lap(0, 1, (0,))

    for k in range(ny - 1):

        @pl.when(k < y)
        def _():
            wait_bytes(tbuf.at[k], t_recv.at[k])

    base = tbuf[0].astype(F32)
    for k in range(1, ny):
        base = base + tbuf[k].astype(F32)
    for k in range(nz):
        pbuf[k] = (base[0:srows] + rbuf[k, 0:srows]).astype(BF16)
    pfx[z] = pbuf[z]
    for step in far_first(nz):
        to = ahead(z, step, nz)
        send(pbuf.at[to], pfx.at[z], p_send, p_recv, z_dev(to))
    norm_high, norm_low = split(base[srows : srows + NORM_ROWS] + rbuf[z, srows : srows + NORM_ROWS])

    for load in loads[4:]:
        load.wait()
    for swap in swaps:
        swap.wait_recv()
    bounds = jnp.concatenate(
        [jnp.broadcast_to(bin_[0, 0:1, :], (rows, HDIM)), jnp.broadcast_to(bin_[1, 0:1, :], (rows, HDIM))]
    )
    for h in range(heads):
        own_part(h, bounds)

    for s in range(1, steps):
        lap(s, 0)
        lap(s, 1)

    wait_bytes(pfx.at[0 : nz - 1], p_recv)

    def retrieve(h):
        query = qf[h]
        first = h * per_head
        state = pfx[first : first + per_head].reshape(HDIM, HDIM)
        numer = numer_l[h] + dot(query, state, NN)
        denom = (dot(query, norm_high, NT) + dot(query, norm_low, NT))[:, h : h + 1] + denom_l[h]
        gate = 1.0 / (1.0 + jnp.exp(-jnp.full((8, HDIM), gate_ref[c * heads + h], F32)))[0:1]
        value = gate * (numer / denom) + (1.0 - gate) * local_o[h]
        mixed[own_class, c * heads + h] = value.astype(BF16)

    split_n = 2 if heads > 1 else 1

    def mixed_part(cls, i):
        return mixed.at[cls, pl.ds(c * heads + i * (heads // split_n), heads // split_n)]

    group_copies, twin_copies = {}, {}
    for i in range(split_n):
        for h in range(i * heads // split_n, (i + 1) * heads // split_n):
            retrieve(h)
        part = mixed_part(own_class, i)
        for r, (dy, dz) in reversed(list(enumerate(offsets))):
            if r == 0:
                twin_copies[r, i] = send(part, part, m_send.at[r, i], m_recv.at[r, i], twin)
            else:
                group_copies[r, i] = send(part, part, g_send.at[r, i], g_recv.at[r, i], group_dev(dy, dz, c))
    state_copy.wait_send()
    norm_copy.wait_send()
    for copy in swaps:
        copy.wait_send()
    if mz > 1:
        wait_bytes(w_all.at[0, 0 : mz - 1, 0:wh], w1_send.at[0])
    if my > 1:
        wait_bytes(w_all.at[0 : my - 1, 0, wh:wc], w1_send.at[1])
    wait_bytes(sbuf.at[0 : nz - 1], a_send)
    for step in range(1, ny):

        @pl.when(y + step < ny)
        def _():
            wait_bytes(tsend, t_send.at[step])

    wait_bytes(pbuf.at[0 : nz - 1], p_send)
    for key in list(laps):
        arrived(key)
    for copy in laps.values():
        copy.wait_send()

    yx = my // nx

    def project(cls, xxs):
        both = jnp.concatenate([mixed[cls, h] for h in range(2 * heads)], axis=1)
        block = jnp.concatenate([w_all[pl.ds(xx * yx, yx)].reshape(yx * mz * wc, width) for xx in xxs])
        value = dot(both, block, NT)
        return [value[:, i * HDIM : (i + 1) * HDIM] for i in range(len(xxs))]

    x_copies = {}

    def hand_over(r):
        for i in range(split_n):
            part = mixed_part(class_of(*offsets[r]), i)
            group_copies[r, i].wait_recv()
            twin_copies[r, i] = send(part, part, m_send.at[r, i], m_recv.at[r, i], twin)

    done_copies, finished = [], set()

    def finish(r):
        if r in finished:
            return
        finished.add(r)
        total = sum_own[r]
        for step in x_order[:-1]:
            x_copies[r, step].wait_recv()
            total = total + x_in[r, step].astype(F32)
        total = total.astype(BF16)
        for e in range(2):
            dsend[r, e] = total[e * rows : (e + 1) * rows]
        place = fin.at[own_class * 2 + c]
        if r == 0:
            fin[own_class * 2 + c] = dsend[0, c]
            done_copies.append(send(dsend.at[0, 1 - c], place, d_send, d_recv, twin))
        else:
            for e in range(2):
                done_copies.append(send(dsend.at[r, e], place, d_send, d_recv, group_dev(*offsets[r], e)))

    for r, (dy, dz) in enumerate(offsets):
        cls = class_of(dy, dz)
        for i in range(split_n):
            twin_copies[r, i].wait_recv()
        for first in range(0, len(x_order), 2):
            part_steps = x_order[first : first + 2]
            for step, value in zip(part_steps, project(cls, [ahead(x, step, nx) for step in part_steps])):
                if step == 0:
                    sum_own[r] = value
                    continue
                x_out[r, step] = value.astype(BF16)
                x_copies[r, step] = send(
                    x_out.at[r, step], x_in.at[r, step], x_send.at[r, step], x_recv.at[r, step],
                    x_dev(ahead(x, step, nx)),
                )
        for later in {0: (1, 2), 1: (3,)}.get(r, ()):
            if later < len(offsets):
                hand_over(later)
        if r == 2:
            finish(0)
    for r in range(len(offsets)):
        finish(r)
    wait_bytes(fin.at[0 : len(done_copies)], d_recv)

    lane = lax.broadcasted_iota(jnp.int32, (rows, HDIM), 1)
    runs = HDIM // wc
    for b in range(out_ref.shape[1] // HDIM):
        value = jnp.zeros((rows, HDIM), F32)
        for k in range(runs):
            shard, e = divmod(b * runs + k, 2)
            yl, zz = divmod(shard, nz)
            pos = ((yl // gy) * mz + zz // gz) * wc
            piece = fin[((yl % gy) * gz + zz % gz) * 2 + e].astype(F32)
            shift = (k * wc - pos) % HDIM
            if shift:
                piece = pltpu.roll(piece, shift, 1)
            value = jnp.where(lane // wc == k, piece, value)
        out_ref[:, b * HDIM : (b + 1) * HDIM] = value.astype(BF16)

    for copies in (twin_copies.values(), group_copies.values(), x_copies.values()):
        for copy in copies:
            copy.wait_send()
    wait_bytes(fin.at[0 : len(done_copies)], d_send)


def local(grid, vk, vv, q, tk, tv, bounds, gate, w):
    ny, nz, nx, gy, gz = grid
    vlen, width = vk.shape
    rows = q.shape[0]
    half_w = width // 2
    heads = half_w // HDIM
    srows = half_w // nz
    wt = w.T
    wc = wt.shape[0]
    my, mz = ny // gy, nz // gz
    n = gy * gz
    assert (my // nx) * mz * wc == HDIM
    steps = max(my, mz, 2) // 2
    hbm = pl.BlockSpec(memory_space=pltpu.HBM)
    smem = pl.BlockSpec(memory_space=pltpu.SMEM)
    dma = pltpu.SemaphoreType.DMA
    slices = (nz, srows + NORM_ROWS, HDIM)
    states = (nz, srows, HDIM)
    per_head = (heads, 2 * rows, HDIM)
    return pl.pallas_call(
        functools.partial(kernel, ny, nz, nx, gy, gz),
        out_shape=jax.ShapeDtypeStruct((rows, 2 * n * HDIM), BF16),
        in_specs=[smem, smem] + [hbm] * 6,
        out_specs=pl.BlockSpec(memory_space=pltpu.VMEM),
        scratch_shapes=[
            pltpu.VMEM((my, mz, wc, width), BF16),
            pltpu.VMEM((2, vlen, half_w), BF16),
            pltpu.VMEM((vlen, half_w), BF16),
            pltpu.VMEM((2, vlen, half_w), BF16),
            pltpu.VMEM((2, rows, half_w), BF16),
            pltpu.VMEM((2, rows, half_w), BF16),
            pltpu.VMEM((2, rows, half_w), BF16),
            pltpu.VMEM((2, 8, HDIM), jnp.int32),
            pltpu.VMEM((2, vlen, half_w), BF16),
            pltpu.VMEM(per_head, BF16),
            pltpu.VMEM(states, BF16),
            pltpu.VMEM(states, BF16),
            pltpu.VMEM(states, F32),
            pltpu.VMEM((NORM_ROWS, HDIM), BF16),
            pltpu.VMEM((NORM_ROWS, HDIM), BF16),
            pltpu.VMEM((NORM_ROWS, HDIM), F32),
            pltpu.VMEM(slices, BF16),
            pltpu.VMEM(slices, BF16),
            pltpu.VMEM(slices, F32),
            pltpu.VMEM((ny, srows + NORM_ROWS, HDIM), BF16),
            pltpu.VMEM((srows + NORM_ROWS, HDIM), BF16),
            pltpu.VMEM(states, BF16),
            pltpu.VMEM(states, BF16),
            pltpu.VMEM(per_head, F32),
            pltpu.VMEM(per_head, F32),
            pltpu.VMEM(per_head, F32),
            pltpu.VMEM((n, 2 * heads, 2 * rows, HDIM), BF16),
            pltpu.VMEM((n, nx, 2 * rows, HDIM), BF16),
            pltpu.VMEM((n, nx, 2 * rows, HDIM), BF16),
            pltpu.VMEM((n, 2 * rows, HDIM), F32),
            pltpu.VMEM((n, 2, rows, HDIM), BF16),
            pltpu.VMEM((2 * n, rows, HDIM), BF16),
            dma((7,)),
            dma((4,)),
            dma,
            dma((6,)),
            dma((6,)),
            dma((2,)),
            dma((2,)),
            dma((2, 2, steps, 2)),
            dma((2, 2, steps, 2)),
            dma,
            dma,
            dma((ny,)),
            dma((ny,)),
            dma,
            dma,
            dma((n, 2)),
            dma((n, 2)),
            dma((n, 2)),
            dma((n, 2)),
            dma((n, nx)),
            dma((n, nx)),
            dma,
            dma,
        ],
        compiler_params=pltpu.CompilerParams(
            collective_id=0, has_side_effects=True, vmem_limit_bytes=60 * 1024 * 1024
        ),
    )(bounds, gate, vk, vv, q, tk, tv, wt)


def solution(mesh):
    nx = mesh.shape["head"]
    specs = (
        P("tm", "head"),
        P("tm", "head"),
        P("tm", "head"),
        P("tm", "head"),
        P("tm", "head"),
        P("tm"),
        P("head"),
        P("head", "tm"),
    )
    return jax.shard_map(
        functools.partial(local, (8, mesh.shape["tm"] // 16, nx, 2, 2)),
        mesh=mesh,
        in_specs=specs,
        out_specs=P("tm", "head"),
        check_vma=False,
    )
```

```python
import functools

import jax
import jax.numpy as jnp
from jax import lax
from jax.experimental import pallas as pl
from jax.experimental.pallas import tpu as pltpu
from jax.sharding import PartitionSpec as P

MESH = pl.DeviceIdType.MESH
F32 = jnp.float32
BF16 = jnp.bfloat16
HDIM = 128
NORM_ROWS = 16
NN = (((1,), (0,)), ((), ()))
NT = (((1,), (1,)), ((), ()))
TN = (((0,), (0,)), ((), ()))


def dot(a, b, dims):
    return lax.dot_general(a, b, dims, preferred_element_type=F32)


def elu_one(values):
    return jnp.where(values > 0, values + 1.0, jnp.exp(jnp.minimum(values, 0.0)))


def split(value):
    high = value.astype(BF16)
    return high, (value - high.astype(F32)).astype(BF16)


def wait_bytes(ref, sem):
    pltpu.make_async_copy(ref, ref, sem).wait()


def kernel(
    ny,
    nz,
    nx,
    gy,
    gz,
    bound_ref,
    gate_ref,
    vk_ref,
    vv_ref,
    q_ref,
    tk_ref,
    tv_ref,
    w_ref,
    out_ref,
    w_all,
    kin,
    vown,
    vin,
    qin,
    tkin,
    tvin,
    bin_,
    kf,
    qf,
    s_send,
    s_recv,
    s_own,
    n_send,
    n_recv,
    n_own,
    sbuf,
    abuf,
    rbuf,
    tbuf,
    tsend,
    pbuf,
    pfx,
    numer_l,
    denom_l,
    local_o,
    mixed,
    x_out,
    x_in,
    sum_own,
    dsend,
    fin,
    in_sem,
    s_sem,
    w_sem,
    c_send,
    c_recv,
    w1_send,
    w1_recv,
    w2_send,
    w2_recv,
    a_send,
    a_recv,
    t_send,
    t_recv,
    p_send,
    p_recv,
    g_send,
    g_recv,
    m_send,
    m_recv,
    x_send,
    x_recv,
    d_send,
    d_recv,
):
    tm = lax.axis_index("tm")
    x = lax.axis_index("head")
    c = lax.rem(tm, 2)
    chip = tm // 2
    z = lax.rem(chip, nz)
    y = chip // nz

    vlen, width = vk_ref.shape
    rows = q_ref.shape[0]
    half_w = width // 2
    heads = half_w // HDIM
    per_head = nz // heads
    srows = HDIM // per_head
    wc = w_ref.shape[0]
    wh = wc // 2
    my, mz = ny // gy, nz // gz
    py, pz = lax.rem(y, gy), lax.rem(z, gz)
    yc, zc = y // gy, z // gz
    own_class = py * gz + pz
    offsets = [(dy, dz) for dy in range(gy) for dz in range(gz)]
    offsets.sort(key=lambda o: (o[0] + o[1], o[1]))

    def dev(t, xx):
        return {"tm": t, "head": xx}

    def y_dev(yy):
        return dev((yy * nz + z) * 2 + c, x)

    def z_dev(zz):
        return dev((y * nz + zz) * 2 + c, x)

    def x_dev(xx):
        return dev(tm, xx)

    def group_dev(dy, dz, core):
        yy = yc * gy + lax.rem(py + dy, gy)
        zz = zc * gz + lax.rem(pz + dz, gz)
        return dev((yy * nz + zz) * 2 + core, x)

    def class_of(dy, dz):
        return lax.rem(py + dy, gy) * gz + lax.rem(pz + dz, gz)

    twin = dev(tm + 1 - 2 * c, x)

    def ahead(me, step, n):
        return lax.rem(me + step, n)

    def send(src, dst, send_sem, recv_sem, device):
        copy = pltpu.make_async_remote_copy(
            src, dst, send_sem, recv_sem, device_id=device, device_id_type=MESH
        )
        copy.start()
        return copy

    mine = pl.ds(pl.multiple_of(c * half_w, HDIM), half_w)
    other = pl.ds(pl.multiple_of((1 - c) * half_w, HDIM), half_w)
    inputs = ((vk_ref, kin), (vv_ref, vin), (q_ref, qin), (tk_ref, tkin), (tv_ref, tvin))
    loads = [
        pltpu.make_async_copy(vk_ref.at[:, other], kin.at[0], in_sem.at[0]),
        pltpu.make_async_copy(vv_ref.at[:, other], vown, in_sem.at[1]),
        pltpu.make_async_copy(vk_ref.at[:, mine], kin.at[1], in_sem.at[5]),
        pltpu.make_async_copy(vv_ref.at[:, mine], vin.at[c], in_sem.at[6]),
    ] + [
        pltpu.make_async_copy(src.at[:, mine], dst.at[c], in_sem.at[i + 2])
        for i, (src, dst) in enumerate(inputs[2:])
    ]
    for load in loads:
        load.start()
    own_w = pltpu.make_async_copy(w_ref, w_all.at[yc, zc], w_sem)
    own_w.start()

    def far_first(n):
        return sorted(range(1, n), key=lambda step: -min(step, n - step))

    barrier = pltpu.get_barrier_semaphore()

    def greet(device):
        pl.semaphore_signal(barrier, inc=1, device_id=device, device_id_type=MESH)

    for step in far_first(nz):
        greet(z_dev(ahead(z, step, nz)))
    for step in far_first(ny):
        greet(y_dev(ahead(y, step, ny)))
    x_order = far_first(nx) + [0]
    for step in x_order[:-1]:
        greet(x_dev(ahead(x, step, nx)))
    greeted = 1 + (nz - 1) + (ny - 1) + (nx - 1)
    for dy, dz in offsets[1:]:
        greet(group_dev(dy, dz, 1 - c))
        greeted += 1
        if dy and dz:
            greet(group_dev(dy, dz, c))
            greeted += 1
    greet(twin)
    bin_[c] = jnp.full((8, HDIM), bound_ref[0], jnp.int32)

    loads[0].wait()
    kin[0] = elu_one(kin[0].astype(F32)).astype(BF16)
    loads[1].wait()
    ones = jnp.ones((NORM_ROWS, vlen), BF16)
    norm_row = lax.broadcasted_iota(jnp.int32, (NORM_ROWS, HDIM), 0)

    def own_state(keys, values):
        norms = jnp.zeros((NORM_ROWS, HDIM), F32)
        states = []
        for h in range(heads):
            cols = slice(h * HDIM, (h + 1) * HDIM)
            states.append(dot(keys[:, cols], values[:, cols], TN))
            norms = jnp.where(norm_row == h, dot(ones, keys[:, cols], NN), norms)
        return states, norms

    states, norms = own_state(kin.at[0], vown)
    for h in range(heads):
        for k in range(per_head):
            s_send[h * per_head + k] = states[h][k * srows : (k + 1) * srows].astype(BF16)
    n_send[...] = norms.astype(BF16)
    for k in range(ny):

        @pl.when(k >= y)
        def _():
            tbuf[k] = jnp.zeros(tbuf.shape[1:], BF16)

    pl.semaphore_wait(barrier, greeted)
    state_copy = send(s_send, s_recv, s_sem.at[0], s_sem.at[1], twin)
    norm_copy = send(n_send, n_recv, s_sem.at[2], s_sem.at[3], twin)
    def y_class(k):
        return y_dev(k * gy + py)

    def z_class(k):
        return z_dev(k * gz + pz)

    for step in far_first(mz):
        send(w_ref.at[0:wh], w_all.at[yc, zc, 0:wh], w1_send.at[0], w1_recv.at[0], z_class(ahead(zc, step, mz)))
    for step in far_first(my):
        send(w_ref.at[wh:wc], w_all.at[yc, zc, wh:wc], w1_send.at[1], w1_recv.at[1], y_class(ahead(yc, step, my)))

    loads[2].wait()
    kf[c] = elu_one(kin[1].astype(F32)).astype(BF16)
    loads[3].wait()
    states, norms = own_state(kf.at[c], vin.at[c])
    for h in range(heads):
        for k in range(per_head):
            s_own[h * per_head + k] = states[h][k * srows : (k + 1) * srows]
    n_own[...] = norms
    state_copy.wait_recv()
    norm_copy.wait_recv()
    norms = (n_own[...] + n_recv[...].astype(F32)).astype(BF16)
    for k in range(nz):
        sbuf[k, 0:srows] = (s_own[k] + s_recv[k].astype(F32)).astype(BF16)
        sbuf[k, srows : srows + NORM_ROWS] = norms
    for step in far_first(nz):
        to = ahead(z, step, nz)
        send(sbuf.at[to], abuf.at[z], a_send, a_recv, z_dev(to))
    abuf[z] = sbuf[z]

    swaps = [send(kin.at[0], kf.at[c], c_send.at[0], c_recv.at[0], twin)]
    swaps += [
        send(src.at[:, other], dst.at[c], c_send.at[i + 1], c_recv.at[i + 1], twin)
        for i, (src, dst) in enumerate(inputs[1:])
    ]
    swaps.append(send(bin_.at[c], bin_.at[c], c_send.at[5], c_recv.at[5], twin))

    def bundle(half, index, q):
        if half == 0:
            return w_all.at[index, q * (mz // 2) : (q + 1) * (mz // 2), 0:wh]
        return w_all.at[q * (my // 2) : (q + 1) * (my // 2), index, wh:wc]

    laps = {}
    waited = set()

    def arrived(key):
        if key in laps and key not in waited:
            waited.add(key)
            laps[key].wait_recv()

    def lap(s, q, halves=(0, 1)):
        for half in halves:
            for way in range(2):
                n, me = (my, yc) if half == 0 else (mz, zc)
                if s >= n // 2 or (s == n // 2 - 1 and q != way):
                    continue
                arrived((half, way, s - 1, q))
                block = ahead(me, n - s, n) if way == 0 else ahead(me, s, n)
                to = ahead(me, 1, n) if way == 0 else ahead(me, n - 1, n)
                part = bundle(half, block, q)
                laps[(half, way, s, q)] = send(
                    part, part, w2_send.at[half, way, s, q], w2_recv.at[half, way, s, q],
                    y_class(to) if half == 0 else z_class(to),
                )

    row_ids = lax.broadcasted_iota(jnp.int32, (2 * rows, HDIM), 0)
    col_ids = lax.broadcasted_iota(jnp.int32, (2 * rows, HDIM), 1)

    def own_part(h, bounds):
        cols = slice(h * HDIM, (h + 1) * HDIM)
        query = qin[:, :, cols].reshape(2 * rows, HDIM)
        q_feat = elu_one(query.astype(F32)).astype(BF16)
        qf[h] = q_feat
        numer = jnp.zeros((2 * rows, HDIM), F32)
        denom = jnp.zeros((2 * rows, 1), F32)
        for e in range(2):
            weight = dot(q_feat, kf[e, :, cols], NT)
            weight = jnp.where(col_ids + (chip * 2 + e) * vlen < bounds, weight, 0.0)
            high, low = split(weight)
            values = vin[e, :, cols]
            numer = numer + dot(high, values, NN) + dot(low, values, NN)
            denom = denom + jnp.sum(weight, axis=1, keepdims=True)
        numer_l[h] = numer
        denom_l[h] = jnp.broadcast_to(denom, (2 * rows, HDIM))
        scores = dot(query, tkin[:, :, cols].reshape(2 * rows, HDIM), NT) * (float(HDIM) ** -0.5)
        causal = jnp.logical_and(col_ids <= row_ids, col_ids // rows == row_ids // rows)
        scores = jnp.where(causal, scores, -jnp.inf)
        expo = jnp.exp(scores - jnp.max(scores, axis=1, keepdims=True))
        probs = (expo / jnp.sum(expo, axis=1, keepdims=True)).astype(BF16)
        local_o[h] = dot(probs, tvin[:, :, cols].reshape(2 * rows, HDIM), NN)

    steps = max(my, mz) // 2
    own_w.wait()
    if my > 1:
        wait_bytes(w_all.at[0 : my - 1, 0, wh:wc], w1_recv.at[1])
        lap(0, 0, (1,))
        lap(0, 1, (1,))
    if mz > 1:
        wait_bytes(w_all.at[0, 0 : mz - 1, 0:wh], w1_recv.at[0])
        lap(0, 0, (0,))

    wait_bytes(abuf.at[0 : nz - 1], a_recv)
    total = jnp.zeros((srows + NORM_ROWS, HDIM), F32)
    for k in range(nz):
        rbuf[k] = total
        total = total + abuf[k].astype(F32)
    tsend[...] = total.astype(BF16)
    for step in far_first(ny):

        @pl.when(y + step < ny)
        def _():
            send(tsend, tbuf.at[y], t_send.at[step], t_recv.at[y], y_dev(y + step))

    if mz > 1:
        lap(0, 1, (0,))

    for k in range(ny - 1):

        @pl.when(k < y)
        def _():
            wait_bytes(tbuf.at[k], t_recv.at[k])

    base = tbuf[0].astype(F32)
    for k in range(1, ny):
        base = base + tbuf[k].astype(F32)
    for k in range(nz):
        pbuf[k] = (base[0:srows] + rbuf[k, 0:srows]).astype(BF16)
    pfx[z] = pbuf[z]
    for step in far_first(nz):
        to = ahead(z, step, nz)
        send(pbuf.at[to], pfx.at[z], p_send, p_recv, z_dev(to))
    norm_high, norm_low = split(base[srows : srows + NORM_ROWS] + rbuf[z, srows : srows + NORM_ROWS])

    for s in range(1, steps):
        lap(s, 0, (1,))
        lap(s, 1, (1,))
    for load in loads[4:]:
        load.wait()
    for swap in swaps:
        swap.wait_recv()
    bounds = jnp.concatenate(
        [jnp.broadcast_to(bin_[0, 0:1, :], (rows, HDIM)), jnp.broadcast_to(bin_[1, 0:1, :], (rows, HDIM))]
    )
    for h in range(heads // 2):
        own_part(h, bounds)
    for s in range(1, steps):
        lap(s, 0, (0,))
        lap(s, 1, (0,))
    for h in range(heads // 2, heads):
        own_part(h, bounds)

    wait_bytes(pfx.at[0 : nz - 1], p_recv)

    def retrieve(h):
        query = qf[h]
        first = h * per_head
        state = pfx[first : first + per_head].reshape(HDIM, HDIM)
        numer = numer_l[h] + dot(query, state, NN)
        denom = (dot(query, norm_high, NT) + dot(query, norm_low, NT))[:, h : h + 1] + denom_l[h]
        gate = 1.0 / (1.0 + jnp.exp(-jnp.full((8, HDIM), gate_ref[c * heads + h], F32)))[0:1]
        value = gate * (numer / denom) + (1.0 - gate) * local_o[h]
        mixed[own_class, c * heads + h] = value.astype(BF16)

    split_n = 2 if heads > 1 else 1

    def mixed_part(cls, i):
        return mixed.at[cls, pl.ds(c * heads + i * (heads // split_n), heads // split_n)]

    group_copies, twin_copies = {}, {}
    for i in range(split_n):
        for h in range(i * heads // split_n, (i + 1) * heads // split_n):
            retrieve(h)
        part = mixed_part(own_class, i)
        for r, (dy, dz) in reversed(list(enumerate(offsets))):
            if r == 0:
                twin_copies[r, i] = send(part, part, m_send.at[r, i], m_recv.at[r, i], twin)
            else:
                group_copies[r, i] = send(part, part, g_send.at[r, i], g_recv.at[r, i], group_dev(dy, dz, c))
    state_copy.wait_send()
    norm_copy.wait_send()
    for copy in swaps:
        copy.wait_send()
    if mz > 1:
        wait_bytes(w_all.at[0, 0 : mz - 1, 0:wh], w1_send.at[0])
    if my > 1:
        wait_bytes(w_all.at[0 : my - 1, 0, wh:wc], w1_send.at[1])
    wait_bytes(sbuf.at[0 : nz - 1], a_send)
    for step in range(1, ny):

        @pl.when(y + step < ny)
        def _():
            wait_bytes(tsend, t_send.at[step])

    wait_bytes(pbuf.at[0 : nz - 1], p_send)
    for key in list(laps):
        arrived(key)
    for copy in laps.values():
        copy.wait_send()

    yx = my // nx

    def project(cls, xxs):
        both = jnp.concatenate([mixed[cls, h] for h in range(2 * heads)], axis=1)
        block = jnp.concatenate([w_all[pl.ds(xx * yx, yx)].reshape(yx * mz * wc, width) for xx in xxs])
        value = dot(both, block, NT)
        return [value[:, i * HDIM : (i + 1) * HDIM] for i in range(len(xxs))]

    x_copies = {}

    def hand_over(r):
        for i in range(split_n):
            part = mixed_part(class_of(*offsets[r]), i)
            group_copies[r, i].wait_recv()
            twin_copies[r, i] = send(part, part, m_send.at[r, i], m_recv.at[r, i], twin)

    done_copies, finished = [], set()

    def finish(r):
        if r in finished:
            return
        finished.add(r)
        total = sum_own[r]
        for step in x_order[:-1]:
            x_copies[r, step].wait_recv()
            total = total + x_in[r, step].astype(F32)
        total = total.astype(BF16)
        for e in range(2):
            dsend[r, e] = total[e * rows : (e + 1) * rows]
        place = fin.at[own_class * 2 + c]
        if r == 0:
            fin[own_class * 2 + c] = dsend[0, c]
            done_copies.append(send(dsend.at[0, 1 - c], place, d_send, d_recv, twin))
        else:
            for e in range(2):
                done_copies.append(send(dsend.at[r, e], place, d_send, d_recv, group_dev(*offsets[r], e)))

    for r, (dy, dz) in enumerate(offsets):
        cls = class_of(dy, dz)
        for i in range(split_n):
            twin_copies[r, i].wait_recv()
        for first in range(0, len(x_order), 2):
            part_steps = x_order[first : first + 2]
            for step, value in zip(part_steps, project(cls, [ahead(x, step, nx) for step in part_steps])):
                if step == 0:
                    sum_own[r] = value
                    continue
                x_out[r, step] = value.astype(BF16)
                x_copies[r, step] = send(
                    x_out.at[r, step], x_in.at[r, step], x_send.at[r, step], x_recv.at[r, step],
                    x_dev(ahead(x, step, nx)),
                )
        for later in {0: (1, 2), 1: (3,)}.get(r, ()):
            if later < len(offsets):
                hand_over(later)
        if r == 2:
            finish(0)
    for r in range(len(offsets)):
        finish(r)
    wait_bytes(fin.at[0 : len(done_copies)], d_recv)

    lane = lax.broadcasted_iota(jnp.int32, (rows, HDIM), 1)
    runs = HDIM // wc
    for b in range(out_ref.shape[1] // HDIM):
        value = jnp.zeros((rows, HDIM), F32)
        for k in range(runs):
            shard, e = divmod(b * runs + k, 2)
            yl, zz = divmod(shard, nz)
            pos = ((yl // gy) * mz + zz // gz) * wc
            piece = fin[((yl % gy) * gz + zz % gz) * 2 + e].astype(F32)
            shift = (k * wc - pos) % HDIM
            if shift:
                piece = pltpu.roll(piece, shift, 1)
            value = jnp.where(lane // wc == k, piece, value)
        out_ref[:, b * HDIM : (b + 1) * HDIM] = value.astype(BF16)

    for copies in (twin_copies.values(), group_copies.values(), x_copies.values()):
        for copy in copies:
            copy.wait_send()
    wait_bytes(fin.at[0 : len(done_copies)], d_send)


def local(grid, vk, vv, q, tk, tv, bounds, gate, w):
    ny, nz, nx, gy, gz = grid
    vlen, width = vk.shape
    rows = q.shape[0]
    half_w = width // 2
    heads = half_w // HDIM
    srows = half_w // nz
    wt = w.T
    wc = wt.shape[0]
    my, mz = ny // gy, nz // gz
    n = gy * gz
    assert (my // nx) * mz * wc == HDIM
    steps = max(my, mz, 2) // 2
    hbm = pl.BlockSpec(memory_space=pltpu.HBM)
    smem = pl.BlockSpec(memory_space=pltpu.SMEM)
    dma = pltpu.SemaphoreType.DMA
    slices = (nz, srows + NORM_ROWS, HDIM)
    states = (nz, srows, HDIM)
    per_head = (heads, 2 * rows, HDIM)
    return pl.pallas_call(
        functools.partial(kernel, ny, nz, nx, gy, gz),
        out_shape=jax.ShapeDtypeStruct((rows, 2 * n * HDIM), BF16),
        in_specs=[smem, smem] + [hbm] * 6,
        out_specs=pl.BlockSpec(memory_space=pltpu.VMEM),
        scratch_shapes=[
            pltpu.VMEM((my, mz, wc, width), BF16),
            pltpu.VMEM((2, vlen, half_w), BF16),
            pltpu.VMEM((vlen, half_w), BF16),
            pltpu.VMEM((2, vlen, half_w), BF16),
            pltpu.VMEM((2, rows, half_w), BF16),
            pltpu.VMEM((2, rows, half_w), BF16),
            pltpu.VMEM((2, rows, half_w), BF16),
            pltpu.VMEM((2, 8, HDIM), jnp.int32),
            pltpu.VMEM((2, vlen, half_w), BF16),
            pltpu.VMEM(per_head, BF16),
            pltpu.VMEM(states, BF16),
            pltpu.VMEM(states, BF16),
            pltpu.VMEM(states, F32),
            pltpu.VMEM((NORM_ROWS, HDIM), BF16),
            pltpu.VMEM((NORM_ROWS, HDIM), BF16),
            pltpu.VMEM((NORM_ROWS, HDIM), F32),
            pltpu.VMEM(slices, BF16),
            pltpu.VMEM(slices, BF16),
            pltpu.VMEM(slices, F32),
            pltpu.VMEM((ny, srows + NORM_ROWS, HDIM), BF16),
            pltpu.VMEM((srows + NORM_ROWS, HDIM), BF16),
            pltpu.VMEM(states, BF16),
            pltpu.VMEM(states, BF16),
            pltpu.VMEM(per_head, F32),
            pltpu.VMEM(per_head, F32),
            pltpu.VMEM(per_head, F32),
            pltpu.VMEM((n, 2 * heads, 2 * rows, HDIM), BF16),
            pltpu.VMEM((n, nx, 2 * rows, HDIM), BF16),
            pltpu.VMEM((n, nx, 2 * rows, HDIM), BF16),
            pltpu.VMEM((n, 2 * rows, HDIM), F32),
            pltpu.VMEM((n, 2, rows, HDIM), BF16),
            pltpu.VMEM((2 * n, rows, HDIM), BF16),
            dma((7,)),
            dma((4,)),
            dma,
            dma((6,)),
            dma((6,)),
            dma((2,)),
            dma((2,)),
            dma((2, 2, steps, 2)),
            dma((2, 2, steps, 2)),
            dma,
            dma,
            dma((ny,)),
            dma((ny,)),
            dma,
            dma,
            dma((n, 2)),
            dma((n, 2)),
            dma((n, 2)),
            dma((n, 2)),
            dma((n, nx)),
            dma((n, nx)),
            dma,
            dma,
        ],
        compiler_params=pltpu.CompilerParams(
            collective_id=0, has_side_effects=True, vmem_limit_bytes=60 * 1024 * 1024
        ),
    )(bounds, gate, vk, vv, q, tk, tv, wt)


def solution(mesh):
    nx = mesh.shape["head"]
    specs = (
        P("tm", "head"),
        P("tm", "head"),
        P("tm", "head"),
        P("tm", "head"),
        P("tm", "head"),
        P("tm"),
        P("head"),
        P("head", "tm"),
    )
    return jax.shard_map(
        functools.partial(local, (8, mesh.shape["tm"] // 16, nx, 2, 2)),
        mesh=mesh,
        in_specs=specs,
        out_specs=P("tm", "head"),
        check_vma=False,
    )
```

```python
import functools

import jax
import jax.numpy as jnp
from jax import lax
from jax.experimental import pallas as pl
from jax.experimental.pallas import tpu as pltpu
from jax.sharding import PartitionSpec as P

MESH = pl.DeviceIdType.MESH
F32 = jnp.float32
BF16 = jnp.bfloat16
HDIM = 128
NORM_ROWS = 16
NN = (((1,), (0,)), ((), ()))
NT = (((1,), (1,)), ((), ()))
TN = (((0,), (0,)), ((), ()))


def dot(a, b, dims):
    return lax.dot_general(a, b, dims, preferred_element_type=F32)


def elu_one(values):
    return jnp.where(values > 0, values + 1.0, jnp.exp(jnp.minimum(values, 0.0)))


def split(value):
    high = value.astype(BF16)
    return high, (value - high.astype(F32)).astype(BF16)


def wait_bytes(ref, sem):
    pltpu.make_async_copy(ref, ref, sem).wait()


def kernel(
    ny,
    nz,
    nx,
    gy,
    gz,
    bound_ref,
    gate_ref,
    vk_ref,
    vv_ref,
    q_ref,
    tk_ref,
    tv_ref,
    w_ref,
    out_ref,
    w_all,
    kin,
    vown,
    vin,
    qin,
    tkin,
    tvin,
    bin_,
    kf,
    qf,
    s_send,
    s_recv,
    s_own,
    n_send,
    n_recv,
    n_own,
    sbuf,
    abuf,
    rbuf,
    tbuf,
    tsend,
    pbuf,
    pfx,
    numer_l,
    denom_l,
    local_o,
    mixed,
    x_out,
    x_in,
    sum_own,
    sum_fwd,
    dsend,
    fin,
    in_sem,
    s_sem,
    w_sem,
    c_send,
    c_recv,
    w1_send,
    w1_recv,
    w2_send,
    w2_recv,
    a_send,
    a_recv,
    t_send,
    t_recv,
    p_send,
    p_recv,
    g_send,
    g_recv,
    m_send,
    m_recv,
    x_send,
    x_recv,
    d_send,
    d_recv,
):
    tm = lax.axis_index("tm")
    x = lax.axis_index("head")
    c = lax.rem(tm, 2)
    chip = tm // 2
    z = lax.rem(chip, nz)
    y = chip // nz

    vlen, width = vk_ref.shape
    rows = q_ref.shape[0]
    half_w = width // 2
    heads = half_w // HDIM
    per_head = nz // heads
    srows = HDIM // per_head
    wc = w_ref.shape[0]
    wh = wc // 2
    my, mz = ny // gy, nz // gz
    py, pz = lax.rem(y, gy), lax.rem(z, gz)
    yc, zc = y // gy, z // gz
    own_class = py * gz + pz
    offsets = [(dy, dz) for dy in range(gy) for dz in range(gz)]
    offsets.sort(key=lambda o: (o[0] + o[1], o[1]))

    def dev(t, xx):
        return {"tm": t, "head": xx}

    def y_dev(yy):
        return dev((yy * nz + z) * 2 + c, x)

    def z_dev(zz):
        return dev((y * nz + zz) * 2 + c, x)

    def x_dev(xx):
        return dev(tm, xx)

    def group_dev(dy, dz, core):
        yy = yc * gy + lax.rem(py + dy, gy)
        zz = zc * gz + lax.rem(pz + dz, gz)
        return dev((yy * nz + zz) * 2 + core, x)

    def class_of(dy, dz):
        return lax.rem(py + dy, gy) * gz + lax.rem(pz + dz, gz)

    twin = dev(tm + 1 - 2 * c, x)

    def ahead(me, step, n):
        return lax.rem(me + step, n)

    def send(src, dst, send_sem, recv_sem, device):
        copy = pltpu.make_async_remote_copy(
            src, dst, send_sem, recv_sem, device_id=device, device_id_type=MESH
        )
        copy.start()
        return copy

    mine = pl.ds(pl.multiple_of(c * half_w, HDIM), half_w)
    other = pl.ds(pl.multiple_of((1 - c) * half_w, HDIM), half_w)
    inputs = ((vk_ref, kin), (vv_ref, vin), (q_ref, qin), (tk_ref, tkin), (tv_ref, tvin))
    loads = [
        pltpu.make_async_copy(vk_ref.at[:, other], kin.at[0], in_sem.at[0]),
        pltpu.make_async_copy(vv_ref.at[:, other], vown, in_sem.at[1]),
        pltpu.make_async_copy(vk_ref.at[:, mine], kin.at[1], in_sem.at[5]),
        pltpu.make_async_copy(vv_ref.at[:, mine], vin.at[c], in_sem.at[6]),
    ] + [
        pltpu.make_async_copy(src.at[:, mine], dst.at[c], in_sem.at[i + 2])
        for i, (src, dst) in enumerate(inputs[2:])
    ]
    for load in loads:
        load.start()
    own_w = pltpu.make_async_copy(w_ref, w_all.at[yc, zc], w_sem)
    own_w.start()

    def far_first(n):
        return sorted(range(1, n), key=lambda step: -min(step, n - step))

    barrier = pltpu.get_barrier_semaphore()

    def greet(device):
        pl.semaphore_signal(barrier, inc=1, device_id=device, device_id_type=MESH)

    for step in far_first(nz):
        greet(z_dev(ahead(z, step, nz)))
    for step in far_first(ny):
        greet(y_dev(ahead(y, step, ny)))
    x_order = far_first(nx) + [0]
    for step in x_order[:-1]:
        greet(x_dev(ahead(x, step, nx)))
    greeted = 1 + (nz - 1) + (ny - 1) + (nx - 1)
    for dy, dz in offsets[1:]:
        greet(group_dev(dy, dz, 1 - c))
        greeted += 1
        if dy and dz:
            greet(group_dev(dy, dz, c))
            greeted += 1
    greet(twin)
    bin_[c] = jnp.full((8, HDIM), bound_ref[0], jnp.int32)

    loads[0].wait()
    kin[0] = elu_one(kin[0].astype(F32)).astype(BF16)
    loads[1].wait()
    ones = jnp.ones((NORM_ROWS, vlen), BF16)
    norm_row = lax.broadcasted_iota(jnp.int32, (NORM_ROWS, HDIM), 0)

    def own_state(keys, values):
        norms = jnp.zeros((NORM_ROWS, HDIM), F32)
        states = []
        for h in range(heads):
            cols = slice(h * HDIM, (h + 1) * HDIM)
            states.append(dot(keys[:, cols], values[:, cols], TN))
            norms = jnp.where(norm_row == h, dot(ones, keys[:, cols], NN), norms)
        return states, norms

    states, norms = own_state(kin.at[0], vown)
    for h in range(heads):
        for k in range(per_head):
            s_send[h * per_head + k] = states[h][k * srows : (k + 1) * srows].astype(BF16)
    n_send[...] = norms.astype(BF16)
    for k in range(ny):

        @pl.when(k >= y)
        def _():
            tbuf[k] = jnp.zeros(tbuf.shape[1:], BF16)

    pl.semaphore_wait(barrier, greeted)
    state_copy = send(s_send, s_recv, s_sem.at[0], s_sem.at[1], twin)
    norm_copy = send(n_send, n_recv, s_sem.at[2], s_sem.at[3], twin)
    def y_class(k):
        return y_dev(k * gy + py)

    def z_class(k):
        return z_dev(k * gz + pz)

    for step in far_first(mz):
        send(w_ref.at[0:wh], w_all.at[yc, zc, 0:wh], w1_send.at[0], w1_recv.at[0], z_class(ahead(zc, step, mz)))
    for step in far_first(my):
        send(w_ref.at[wh:wc], w_all.at[yc, zc, wh:wc], w1_send.at[1], w1_recv.at[1], y_class(ahead(yc, step, my)))

    loads[2].wait()
    kf[c] = elu_one(kin[1].astype(F32)).astype(BF16)
    loads[3].wait()
    states, norms = own_state(kf.at[c], vin.at[c])
    for h in range(heads):
        for k in range(per_head):
            s_own[h * per_head + k] = states[h][k * srows : (k + 1) * srows]
    n_own[...] = norms
    state_copy.wait_recv()
    norm_copy.wait_recv()
    norms = (n_own[...] + n_recv[...].astype(F32)).astype(BF16)
    for k in range(nz):
        sbuf[k, 0:srows] = (s_own[k] + s_recv[k].astype(F32)).astype(BF16)
        sbuf[k, srows : srows + NORM_ROWS] = norms
    for step in far_first(nz):
        to = ahead(z, step, nz)
        send(sbuf.at[to], abuf.at[z], a_send, a_recv, z_dev(to))
    abuf[z] = sbuf[z]

    swaps = [send(kin.at[0], kf.at[c], c_send.at[0], c_recv.at[0], twin)]
    swaps += [
        send(src.at[:, other], dst.at[c], c_send.at[i + 1], c_recv.at[i + 1], twin)
        for i, (src, dst) in enumerate(inputs[1:])
    ]
    swaps.append(send(bin_.at[c], bin_.at[c], c_send.at[5], c_recv.at[5], twin))

    def bundle(half, index, q):
        if half == 0:
            return w_all.at[index, q * (mz // 2) : (q + 1) * (mz // 2), 0:wh]
        return w_all.at[q * (my // 2) : (q + 1) * (my // 2), index, wh:wc]

    laps = {}
    waited = set()

    def arrived(key):
        if key in laps and key not in waited:
            waited.add(key)
            laps[key].wait_recv()

    def lap(s, q, halves=(0, 1)):
        for half in halves:
            for way in range(2):
                n, me = (my, yc) if half == 0 else (mz, zc)
                if s >= n // 2 or (s == n // 2 - 1 and q != way):
                    continue
                arrived((half, way, s - 1, q))
                block = ahead(me, n - s, n) if way == 0 else ahead(me, s, n)
                to = ahead(me, 1, n) if way == 0 else ahead(me, n - 1, n)
                part = bundle(half, block, q)
                laps[(half, way, s, q)] = send(
                    part, part, w2_send.at[half, way, s, q], w2_recv.at[half, way, s, q],
                    y_class(to) if half == 0 else z_class(to),
                )

    row_ids = lax.broadcasted_iota(jnp.int32, (2 * rows, HDIM), 0)
    col_ids = lax.broadcasted_iota(jnp.int32, (2 * rows, HDIM), 1)

    def own_part(h, bounds):
        cols = slice(h * HDIM, (h + 1) * HDIM)
        query = qin[:, :, cols].reshape(2 * rows, HDIM)
        q_feat = elu_one(query.astype(F32)).astype(BF16)
        qf[h] = q_feat
        numer = jnp.zeros((2 * rows, HDIM), F32)
        denom = jnp.zeros((2 * rows, 1), F32)
        for e in range(2):
            weight = dot(q_feat, kf[e, :, cols], NT)
            weight = jnp.where(col_ids + (chip * 2 + e) * vlen < bounds, weight, 0.0)
            high, low = split(weight)
            values = vin[e, :, cols]
            numer = numer + dot(high, values, NN) + dot(low, values, NN)
            denom = denom + jnp.sum(weight, axis=1, keepdims=True)
        numer_l[h] = numer
        denom_l[h] = jnp.broadcast_to(denom, (2 * rows, HDIM))
        scores = dot(query, tkin[:, :, cols].reshape(2 * rows, HDIM), NT) * (float(HDIM) ** -0.5)
        causal = jnp.logical_and(col_ids <= row_ids, col_ids // rows == row_ids // rows)
        scores = jnp.where(causal, scores, -jnp.inf)
        expo = jnp.exp(scores - jnp.max(scores, axis=1, keepdims=True))
        probs = (expo / jnp.sum(expo, axis=1, keepdims=True)).astype(BF16)
        local_o[h] = dot(probs, tvin[:, :, cols].reshape(2 * rows, HDIM), NN)

    steps = max(my, mz) // 2
    own_w.wait()
    if my > 1:
        wait_bytes(w_all.at[0 : my - 1, 0, wh:wc], w1_recv.at[1])
        lap(0, 0, (1,))
        lap(0, 1, (1,))
    if mz > 1:
        wait_bytes(w_all.at[0, 0 : mz - 1, 0:wh], w1_recv.at[0])
        lap(0, 0, (0,))

    wait_bytes(abuf.at[0 : nz - 1], a_recv)
    total = jnp.zeros((srows + NORM_ROWS, HDIM), F32)
    for k in range(nz):
        rbuf[k] = total
        total = total + abuf[k].astype(F32)
    tsend[...] = total.astype(BF16)
    for step in far_first(ny):

        @pl.when(y + step < ny)
        def _():
            send(tsend, tbuf.at[y], t_send.at[step], t_recv.at[y], y_dev(y + step))

    if mz > 1:
        lap(0, 1, (0,))

    for k in range(ny - 1):

        @pl.when(k < y)
        def _():
            wait_bytes(tbuf.at[k], t_recv.at[k])

    base = tbuf[0].astype(F32)
    for k in range(1, ny):
        base = base + tbuf[k].astype(F32)
    for k in range(nz):
        pbuf[k] = (base[0:srows] + rbuf[k, 0:srows]).astype(BF16)
    pfx[z] = pbuf[z]
    for step in far_first(nz):
        to = ahead(z, step, nz)
        send(pbuf.at[to], pfx.at[z], p_send, p_recv, z_dev(to))
    norm_high, norm_low = split(base[srows : srows + NORM_ROWS] + rbuf[z, srows : srows + NORM_ROWS])

    for s in range(1, steps):
        lap(s, 0, (1,))
        lap(s, 1, (1,))
    for load in loads[4:]:
        load.wait()
    for swap in swaps:
        swap.wait_recv()
    bounds = jnp.concatenate(
        [jnp.broadcast_to(bin_[0, 0:1, :], (rows, HDIM)), jnp.broadcast_to(bin_[1, 0:1, :], (rows, HDIM))]
    )
    for h in range(heads // 2):
        own_part(h, bounds)
    for s in range(1, steps):
        lap(s, 0, (0,))
        lap(s, 1, (0,))
    for h in range(heads // 2, heads):
        own_part(h, bounds)

    wait_bytes(pfx.at[0 : nz - 1], p_recv)

    def retrieve(h):
        query = qf[h]
        first = h * per_head
        state = pfx[first : first + per_head].reshape(HDIM, HDIM)
        numer = numer_l[h] + dot(query, state, NN)
        denom = (dot(query, norm_high, NT) + dot(query, norm_low, NT))[:, h : h + 1] + denom_l[h]
        gate = 1.0 / (1.0 + jnp.exp(-jnp.full((8, HDIM), gate_ref[c * heads + h], F32)))[0:1]
        value = gate * (numer / denom) + (1.0 - gate) * local_o[h]
        mixed[own_class, c * heads + h] = value.astype(BF16)

    split_n = 2 if heads > 1 else 1

    def mixed_part(cls, i):
        return mixed.at[cls, pl.ds(c * heads + i * (heads // split_n), heads // split_n)]

    group_copies, twin_copies = {}, {}
    for i in range(split_n):
        for h in range(i * heads // split_n, (i + 1) * heads // split_n):
            retrieve(h)
        part = mixed_part(own_class, i)
        for r, (dy, dz) in reversed(list(enumerate(offsets))):
            if r == 0:
                twin_copies[r, i] = send(part, part, m_send.at[r, i], m_recv.at[r, i], twin)
            else:
                group_copies[r, i] = send(part, part, g_send.at[r, i], g_recv.at[r, i], group_dev(dy, dz, c))
    state_copy.wait_send()
    norm_copy.wait_send()
    for copy in swaps:
        copy.wait_send()
    if mz > 1:
        wait_bytes(w_all.at[0, 0 : mz - 1, 0:wh], w1_send.at[0])
    if my > 1:
        wait_bytes(w_all.at[0 : my - 1, 0, wh:wc], w1_send.at[1])
    wait_bytes(sbuf.at[0 : nz - 1], a_send)
    for step in range(1, ny):

        @pl.when(y + step < ny)
        def _():
            wait_bytes(tsend, t_send.at[step])

    wait_bytes(pbuf.at[0 : nz - 1], p_send)
    for key in list(laps):
        arrived(key)
    for copy in laps.values():
        copy.wait_send()

    yx = my // nx

    def project(cls, xxs):
        both = jnp.concatenate([mixed[cls, h] for h in range(2 * heads)], axis=1)
        block = jnp.concatenate([w_all[pl.ds(xx * yx, yx)].reshape(yx * mz * wc, width) for xx in xxs])
        value = dot(both, block, NT)
        return [value[:, i * HDIM : (i + 1) * HDIM] for i in range(len(xxs))]

    x_copies = {}

    def hand_over(r):
        for i in range(split_n):
            part = mixed_part(class_of(*offsets[r]), i)
            group_copies[r, i].wait_recv()
            twin_copies[r, i] = send(part, part, m_send.at[r, i], m_recv.at[r, i], twin)

    def relayed(r):
        return nx == 4 and r < len(offsets) - 1

    def near(r):
        return 1 if r % 2 == 0 else 3

    def to_peer(r, step, hop):
        x_copies[r, step] = send(
            x_out.at[r, step], x_in.at[r, step], x_send.at[r, step], x_recv.at[r, step], x_dev(ahead(x, hop, nx))
        )

    def forward(r):
        if relayed(r):
            x_copies[r, 2].wait_recv()
            x_out[r, near(r)] = (sum_fwd[r] + x_in[r, 2].astype(F32)).astype(BF16)
            to_peer(r, near(r), near(r))

    done_copies, finished = [], set()

    def finish(r):
        if r in finished:
            return
        finished.add(r)
        total = sum_own[r]
        for step in (1, 3) if relayed(r) else x_order[:-1]:
            x_copies[r, step].wait_recv()
            total = total + x_in[r, step].astype(F32)
        total = total.astype(BF16)
        for e in range(2):
            dsend[r, e] = total[e * rows : (e + 1) * rows]
        place = fin.at[own_class * 2 + c]
        if r == 0:
            fin[own_class * 2 + c] = dsend[0, c]
            done_copies.append(send(dsend.at[0, 1 - c], place, d_send, d_recv, twin))
        else:
            for e in range(2):
                done_copies.append(send(dsend.at[r, e], place, d_send, d_recv, group_dev(*offsets[r], e)))

    for r, (dy, dz) in enumerate(offsets):
        cls = class_of(dy, dz)
        for i in range(split_n):
            twin_copies[r, i].wait_recv()
        for first in range(0, len(x_order), 2):
            part_steps = x_order[first : first + 2]
            for step, value in zip(part_steps, project(cls, [ahead(x, step, nx) for step in part_steps])):
                if step == 0:
                    sum_own[r] = value
                elif relayed(r) and step == near(r):
                    sum_fwd[r] = value
                else:
                    x_out[r, step] = value.astype(BF16)
                    to_peer(r, step, near(r) if relayed(r) and step == 2 else step)
        if r > 0:
            forward(r - 1)
        for later in {0: (1, 2), 1: (3,)}.get(r, ()):
            if later < len(offsets):
                hand_over(later)
        if r == 2:
            finish(0)
    for r in range(len(offsets)):
        finish(r)
    wait_bytes(fin.at[0 : len(done_copies)], d_recv)

    lane = lax.broadcasted_iota(jnp.int32, (rows, HDIM), 1)
    runs = HDIM // wc
    for b in range(out_ref.shape[1] // HDIM):
        value = jnp.zeros((rows, HDIM), F32)
        for k in range(runs):
            shard, e = divmod(b * runs + k, 2)
            yl, zz = divmod(shard, nz)
            pos = ((yl // gy) * mz + zz // gz) * wc
            piece = fin[((yl % gy) * gz + zz % gz) * 2 + e].astype(F32)
            shift = (k * wc - pos) % HDIM
            if shift:
                piece = pltpu.roll(piece, shift, 1)
            value = jnp.where(lane // wc == k, piece, value)
        out_ref[:, b * HDIM : (b + 1) * HDIM] = value.astype(BF16)

    for copies in (twin_copies.values(), group_copies.values(), x_copies.values()):
        for copy in copies:
            copy.wait_send()
    wait_bytes(fin.at[0 : len(done_copies)], d_send)


def local(grid, vk, vv, q, tk, tv, bounds, gate, w):
    ny, nz, nx, gy, gz = grid
    vlen, width = vk.shape
    rows = q.shape[0]
    half_w = width // 2
    heads = half_w // HDIM
    srows = half_w // nz
    wt = w.T
    wc = wt.shape[0]
    my, mz = ny // gy, nz // gz
    n = gy * gz
    assert (my // nx) * mz * wc == HDIM
    steps = max(my, mz, 2) // 2
    hbm = pl.BlockSpec(memory_space=pltpu.HBM)
    smem = pl.BlockSpec(memory_space=pltpu.SMEM)
    dma = pltpu.SemaphoreType.DMA
    slices = (nz, srows + NORM_ROWS, HDIM)
    states = (nz, srows, HDIM)
    per_head = (heads, 2 * rows, HDIM)
    return pl.pallas_call(
        functools.partial(kernel, ny, nz, nx, gy, gz),
        out_shape=jax.ShapeDtypeStruct((rows, 2 * n * HDIM), BF16),
        in_specs=[smem, smem] + [hbm] * 6,
        out_specs=pl.BlockSpec(memory_space=pltpu.VMEM),
        scratch_shapes=[
            pltpu.VMEM((my, mz, wc, width), BF16),
            pltpu.VMEM((2, vlen, half_w), BF16),
            pltpu.VMEM((vlen, half_w), BF16),
            pltpu.VMEM((2, vlen, half_w), BF16),
            pltpu.VMEM((2, rows, half_w), BF16),
            pltpu.VMEM((2, rows, half_w), BF16),
            pltpu.VMEM((2, rows, half_w), BF16),
            pltpu.VMEM((2, 8, HDIM), jnp.int32),
            pltpu.VMEM((2, vlen, half_w), BF16),
            pltpu.VMEM(per_head, BF16),
            pltpu.VMEM(states, BF16),
            pltpu.VMEM(states, BF16),
            pltpu.VMEM(states, F32),
            pltpu.VMEM((NORM_ROWS, HDIM), BF16),
            pltpu.VMEM((NORM_ROWS, HDIM), BF16),
            pltpu.VMEM((NORM_ROWS, HDIM), F32),
            pltpu.VMEM(slices, BF16),
            pltpu.VMEM(slices, BF16),
            pltpu.VMEM(slices, F32),
            pltpu.VMEM((ny, srows + NORM_ROWS, HDIM), BF16),
            pltpu.VMEM((srows + NORM_ROWS, HDIM), BF16),
            pltpu.VMEM(states, BF16),
            pltpu.VMEM(states, BF16),
            pltpu.VMEM(per_head, F32),
            pltpu.VMEM(per_head, F32),
            pltpu.VMEM(per_head, F32),
            pltpu.VMEM((n, 2 * heads, 2 * rows, HDIM), BF16),
            pltpu.VMEM((n, nx, 2 * rows, HDIM), BF16),
            pltpu.VMEM((n, nx, 2 * rows, HDIM), BF16),
            pltpu.VMEM((n, 2 * rows, HDIM), F32),
            pltpu.VMEM((n, 2 * rows, HDIM), F32),
            pltpu.VMEM((n, 2, rows, HDIM), BF16),
            pltpu.VMEM((2 * n, rows, HDIM), BF16),
            dma((7,)),
            dma((4,)),
            dma,
            dma((6,)),
            dma((6,)),
            dma((2,)),
            dma((2,)),
            dma((2, 2, steps, 2)),
            dma((2, 2, steps, 2)),
            dma,
            dma,
            dma((ny,)),
            dma((ny,)),
            dma,
            dma,
            dma((n, 2)),
            dma((n, 2)),
            dma((n, 2)),
            dma((n, 2)),
            dma((n, nx)),
            dma((n, nx)),
            dma,
            dma,
        ],
        compiler_params=pltpu.CompilerParams(
            collective_id=0, has_side_effects=True, vmem_limit_bytes=60 * 1024 * 1024
        ),
    )(bounds, gate, vk, vv, q, tk, tv, wt)


def solution(mesh):
    nx = mesh.shape["head"]
    specs = (
        P("tm", "head"),
        P("tm", "head"),
        P("tm", "head"),
        P("tm", "head"),
        P("tm", "head"),
        P("tm"),
        P("head"),
        P("head", "tm"),
    )
    return jax.shard_map(
        functools.partial(local, (8, mesh.shape["tm"] // 16, nx, 2, 2)),
        mesh=mesh,
        in_specs=specs,
        out_specs=P("tm", "head"),
        check_vma=False,
    )
```

```python
import functools

import jax
import jax.numpy as jnp
from jax import lax
from jax.experimental import pallas as pl
from jax.experimental.pallas import tpu as pltpu
from jax.sharding import PartitionSpec as P

MESH = pl.DeviceIdType.MESH
F32 = jnp.float32
BF16 = jnp.bfloat16
HDIM = 128
NORM_ROWS = 16
NN = (((1,), (0,)), ((), ()))
NT = (((1,), (1,)), ((), ()))
TN = (((0,), (0,)), ((), ()))


def dot(a, b, dims):
    return lax.dot_general(a, b, dims, preferred_element_type=F32)


def elu_one(values):
    return jnp.where(values > 0, values + 1.0, jnp.exp(jnp.minimum(values, 0.0)))


def split(value):
    high = value.astype(BF16)
    return high, (value - high.astype(F32)).astype(BF16)


def wait_bytes(ref, sem):
    pltpu.make_async_copy(ref, ref, sem).wait()


def kernel(
    ny,
    nz,
    nx,
    gy,
    gz,
    bound_ref,
    gate_ref,
    vk_ref,
    vv_ref,
    q_ref,
    tk_ref,
    tv_ref,
    w_ref,
    out_ref,
    w_all,
    kin,
    vown,
    vin,
    qin,
    tkin,
    tvin,
    bin_,
    kf,
    qf,
    s_send,
    s_recv,
    s_own,
    n_send,
    n_recv,
    n_own,
    sbuf,
    abuf,
    rbuf,
    tbuf,
    tsend,
    pbuf,
    pfx,
    numer_l,
    denom_l,
    local_o,
    mixed,
    x_out,
    x_in,
    sum_own,
    dsend,
    fin,
    in_sem,
    s_sem,
    w_sem,
    c_send,
    c_recv,
    w1_send,
    w1_recv,
    w2_send,
    w2_recv,
    a_send,
    a_recv,
    t_send,
    t_recv,
    p_send,
    p_recv,
    g_send,
    g_recv,
    m_send,
    m_recv,
    x_send,
    x_recv,
    d_send,
    d_recv,
):
    tm = lax.axis_index("tm")
    x = lax.axis_index("head")
    c = lax.rem(tm, 2)
    chip = tm // 2
    z = lax.rem(chip, nz)
    y = chip // nz

    vlen, width = vk_ref.shape
    rows = q_ref.shape[0]
    half_w = width // 2
    heads = half_w // HDIM
    per_head = nz // heads
    srows = HDIM // per_head
    wc = w_ref.shape[0]
    wh = wc // 2
    my, mz = ny // gy, nz // gz
    py, pz = lax.rem(y, gy), lax.rem(z, gz)
    yc, zc = y // gy, z // gz
    own_class = py * gz + pz
    offsets = [(dy, dz) for dy in range(gy) for dz in range(gz)]
    offsets.sort(key=lambda o: (o[0] + o[1], o[1]))

    def dev(t, xx):
        return {"tm": t, "head": xx}

    def y_dev(yy):
        return dev((yy * nz + z) * 2 + c, x)

    def z_dev(zz):
        return dev((y * nz + zz) * 2 + c, x)

    def x_dev(xx):
        return dev(tm, xx)

    def group_dev(dy, dz, core):
        yy = yc * gy + lax.rem(py + dy, gy)
        zz = zc * gz + lax.rem(pz + dz, gz)
        return dev((yy * nz + zz) * 2 + core, x)

    def class_of(dy, dz):
        return lax.rem(py + dy, gy) * gz + lax.rem(pz + dz, gz)

    twin = dev(tm + 1 - 2 * c, x)

    def ahead(me, step, n):
        return lax.rem(me + step, n)

    def send(src, dst, send_sem, recv_sem, device):
        copy = pltpu.make_async_remote_copy(
            src, dst, send_sem, recv_sem, device_id=device, device_id_type=MESH
        )
        copy.start()
        return copy

    mine = pl.ds(pl.multiple_of(c * half_w, HDIM), half_w)
    other = pl.ds(pl.multiple_of((1 - c) * half_w, HDIM), half_w)
    inputs = ((vk_ref, kin), (vv_ref, vin), (q_ref, qin), (tk_ref, tkin), (tv_ref, tvin))
    loads = [
        pltpu.make_async_copy(vk_ref.at[:, other], kin.at[0], in_sem.at[0]),
        pltpu.make_async_copy(vv_ref.at[:, other], vown, in_sem.at[1]),
        pltpu.make_async_copy(vk_ref.at[:, mine], kin.at[1], in_sem.at[5]),
        pltpu.make_async_copy(vv_ref.at[:, mine], vin.at[c], in_sem.at[6]),
    ] + [
        pltpu.make_async_copy(src.at[:, mine], dst.at[c], in_sem.at[i + 2])
        for i, (src, dst) in enumerate(inputs[2:])
    ]
    for load in loads:
        load.start()
    own_w = pltpu.make_async_copy(w_ref, w_all.at[yc, zc], w_sem)
    own_w.start()

    def far_first(n):
        return sorted(range(1, n), key=lambda step: -min(step, n - step))

    barrier = pltpu.get_barrier_semaphore()

    def greet(device):
        pl.semaphore_signal(barrier, inc=1, device_id=device, device_id_type=MESH)

    for step in far_first(nz):
        greet(z_dev(ahead(z, step, nz)))
    for step in far_first(ny):
        greet(y_dev(ahead(y, step, ny)))
    x_order = far_first(nx) + [0]
    for step in x_order[:-1]:
        greet(x_dev(ahead(x, step, nx)))
    greeted = 1 + (nz - 1) + (ny - 1) + (nx - 1)
    for dy, dz in offsets[1:]:
        greet(group_dev(dy, dz, 1 - c))
        greeted += 1
        if dy and dz:
            greet(group_dev(dy, dz, c))
            greeted += 1
    greet(twin)
    bin_[c] = jnp.full((8, HDIM), bound_ref[0], jnp.int32)

    loads[0].wait()
    kin[0] = elu_one(kin[0].astype(F32)).astype(BF16)
    loads[1].wait()
    ones = jnp.ones((NORM_ROWS, vlen), BF16)
    norm_row = lax.broadcasted_iota(jnp.int32, (NORM_ROWS, HDIM), 0)

    def own_state(keys, values):
        norms = jnp.zeros((NORM_ROWS, HDIM), F32)
        states = []
        for h in range(heads):
            cols = slice(h * HDIM, (h + 1) * HDIM)
            states.append(dot(keys[:, cols], values[:, cols], TN))
            norms = jnp.where(norm_row == h, dot(ones, keys[:, cols], NN), norms)
        return states, norms

    states, norms = own_state(kin.at[0], vown)
    for h in range(heads):
        for k in range(per_head):
            s_send[h * per_head + k] = states[h][k * srows : (k + 1) * srows].astype(BF16)
    n_send[...] = norms.astype(BF16)
    for k in range(ny):

        @pl.when(k >= y)
        def _():
            tbuf[k] = jnp.zeros(tbuf.shape[1:], BF16)

    pl.semaphore_wait(barrier, greeted)
    state_copy = send(s_send, s_recv, s_sem.at[0], s_sem.at[1], twin)
    norm_copy = send(n_send, n_recv, s_sem.at[2], s_sem.at[3], twin)
    def y_class(k):
        return y_dev(k * gy + py)

    def z_class(k):
        return z_dev(k * gz + pz)

    for step in far_first(mz):
        send(w_ref.at[0:wh], w_all.at[yc, zc, 0:wh], w1_send.at[0], w1_recv.at[0], z_class(ahead(zc, step, mz)))
    for step in far_first(my):
        send(w_ref.at[wh:wc], w_all.at[yc, zc, wh:wc], w1_send.at[1], w1_recv.at[1], y_class(ahead(yc, step, my)))

    loads[2].wait()
    kf[c] = elu_one(kin[1].astype(F32)).astype(BF16)
    loads[3].wait()
    states, norms = own_state(kf.at[c], vin.at[c])
    for h in range(heads):
        for k in range(per_head):
            s_own[h * per_head + k] = states[h][k * srows : (k + 1) * srows]
    n_own[...] = norms
    state_copy.wait_recv()
    norm_copy.wait_recv()
    norms = (n_own[...] + n_recv[...].astype(F32)).astype(BF16)
    for k in range(nz):
        sbuf[k, 0:srows] = (s_own[k] + s_recv[k].astype(F32)).astype(BF16)
        sbuf[k, srows : srows + NORM_ROWS] = norms
    for step in far_first(nz):
        to = ahead(z, step, nz)
        send(sbuf.at[to], abuf.at[z], a_send, a_recv, z_dev(to))
    abuf[z] = sbuf[z]

    swaps = [send(kin.at[0], kf.at[c], c_send.at[0], c_recv.at[0], twin)]
    swaps += [
        send(src.at[:, other], dst.at[c], c_send.at[i + 1], c_recv.at[i + 1], twin)
        for i, (src, dst) in enumerate(inputs[1:])
    ]
    swaps.append(send(bin_.at[c], bin_.at[c], c_send.at[5], c_recv.at[5], twin))

    def bundle(half, index, q):
        if half == 0:
            return w_all.at[index, q * (mz // 2) : (q + 1) * (mz // 2), 0:wh]
        return w_all.at[q * (my // 2) : (q + 1) * (my // 2), index, wh:wc]

    laps = {}
    waited = set()

    def arrived(key):
        if key in laps and key not in waited:
            waited.add(key)
            laps[key].wait_recv()

    def lap(s, q, halves=(0, 1)):
        for half in halves:
            for way in range(2):
                n, me = (my, yc) if half == 0 else (mz, zc)
                if s >= n // 2 or (s == n // 2 - 1 and q != way):
                    continue
                arrived((half, way, s - 1, q))
                block = ahead(me, n - s, n) if way == 0 else ahead(me, s, n)
                to = ahead(me, 1, n) if way == 0 else ahead(me, n - 1, n)
                part = bundle(half, block, q)
                laps[(half, way, s, q)] = send(
                    part, part, w2_send.at[half, way, s, q], w2_recv.at[half, way, s, q],
                    y_class(to) if half == 0 else z_class(to),
                )

    row_ids = lax.broadcasted_iota(jnp.int32, (2 * rows, HDIM), 0)
    col_ids = lax.broadcasted_iota(jnp.int32, (2 * rows, HDIM), 1)

    def own_part(h, bounds):
        cols = slice(h * HDIM, (h + 1) * HDIM)
        query = qin[:, :, cols].reshape(2 * rows, HDIM)
        q_feat = elu_one(query.astype(F32)).astype(BF16)
        qf[h] = q_feat
        numer = jnp.zeros((2 * rows, HDIM), F32)
        denom = jnp.zeros((2 * rows, 1), F32)
        for e in range(2):
            weight = dot(q_feat, kf[e, :, cols], NT)
            weight = jnp.where(col_ids + (chip * 2 + e) * vlen < bounds, weight, 0.0)
            high, low = split(weight)
            values = vin[e, :, cols]
            numer = numer + dot(high, values, NN) + dot(low, values, NN)
            denom = denom + jnp.sum(weight, axis=1, keepdims=True)
        numer_l[h] = numer
        denom_l[h] = jnp.broadcast_to(denom, (2 * rows, HDIM))
        scores = dot(query, tkin[:, :, cols].reshape(2 * rows, HDIM), NT) * (float(HDIM) ** -0.5)
        causal = jnp.logical_and(col_ids <= row_ids, col_ids // rows == row_ids // rows)
        scores = jnp.where(causal, scores, -jnp.inf)
        expo = jnp.exp(scores - jnp.max(scores, axis=1, keepdims=True))
        probs = (expo / jnp.sum(expo, axis=1, keepdims=True)).astype(BF16)
        local_o[h] = dot(probs, tvin[:, :, cols].reshape(2 * rows, HDIM), NN)

    steps = max(my, mz) // 2
    own_w.wait()
    if my > 1:
        wait_bytes(w_all.at[0 : my - 1, 0, wh:wc], w1_recv.at[1])
        lap(0, 0, (1,))
        lap(0, 1, (1,))
    if mz > 1:
        wait_bytes(w_all.at[0, 0 : mz - 1, 0:wh], w1_recv.at[0])
        lap(0, 0, (0,))

    wait_bytes(abuf.at[0 : nz - 1], a_recv)
    total = jnp.zeros((srows + NORM_ROWS, HDIM), F32)
    for k in range(nz):
        rbuf[k] = total
        total = total + abuf[k].astype(F32)
    tsend[...] = total.astype(BF16)
    for step in far_first(ny):

        @pl.when(y + step < ny)
        def _():
            send(tsend, tbuf.at[y], t_send.at[step], t_recv.at[y], y_dev(y + step))

    if mz > 1:
        lap(0, 1, (0,))

    for k in range(ny - 1):

        @pl.when(k < y)
        def _():
            wait_bytes(tbuf.at[k], t_recv.at[k])

    base = tbuf[0].astype(F32)
    for k in range(1, ny):
        base = base + tbuf[k].astype(F32)
    for k in range(nz):
        pbuf[k] = (base[0:srows] + rbuf[k, 0:srows]).astype(BF16)
    pfx[z] = pbuf[z]
    for step in far_first(nz):
        to = ahead(z, step, nz)
        send(pbuf.at[to], pfx.at[z], p_send, p_recv, z_dev(to))
    norm_high, norm_low = split(base[srows : srows + NORM_ROWS] + rbuf[z, srows : srows + NORM_ROWS])

    for s in range(1, steps):
        lap(s, 0, (1,))
        lap(s, 1, (1,))
    for load in loads[4:]:
        load.wait()
    for swap in swaps:
        swap.wait_recv()
    bounds = jnp.concatenate(
        [jnp.broadcast_to(bin_[0, 0:1, :], (rows, HDIM)), jnp.broadcast_to(bin_[1, 0:1, :], (rows, HDIM))]
    )
    for h in range(heads // 2):
        own_part(h, bounds)
    for s in range(1, steps):
        lap(s, 0, (0,))
        lap(s, 1, (0,))
    for h in range(heads // 2, heads):
        own_part(h, bounds)

    wait_bytes(pfx.at[0 : nz - 1], p_recv)

    def retrieve(h):
        query = qf[h]
        first = h * per_head
        state = pfx[first : first + per_head].reshape(HDIM, HDIM)
        numer = numer_l[h] + dot(query, state, NN)
        denom = (dot(query, norm_high, NT) + dot(query, norm_low, NT))[:, h : h + 1] + denom_l[h]
        gate = 1.0 / (1.0 + jnp.exp(-jnp.full((8, HDIM), gate_ref[c * heads + h], F32)))[0:1]
        value = gate * (numer / denom) + (1.0 - gate) * local_o[h]
        mixed[own_class, c * heads + h] = value.astype(BF16)

    split_n = 2 if heads > 1 else 1

    def mixed_part(cls, i):
        return mixed.at[cls, pl.ds(c * heads + i * (heads // split_n), heads // split_n)]

    group_copies, twin_copies = {}, {}
    for i in range(split_n):
        for h in range(i * heads // split_n, (i + 1) * heads // split_n):
            retrieve(h)
        part = mixed_part(own_class, i)
        for r, (dy, dz) in reversed(list(enumerate(offsets))):
            if r == 0:
                twin_copies[r, i] = send(part, part, m_send.at[r, i], m_recv.at[r, i], twin)
            else:
                group_copies[r, i] = send(part, part, g_send.at[r, i], g_recv.at[r, i], group_dev(dy, dz, c))
    state_copy.wait_send()
    norm_copy.wait_send()
    for copy in swaps:
        copy.wait_send()
    if mz > 1:
        wait_bytes(w_all.at[0, 0 : mz - 1, 0:wh], w1_send.at[0])
    if my > 1:
        wait_bytes(w_all.at[0 : my - 1, 0, wh:wc], w1_send.at[1])
    wait_bytes(sbuf.at[0 : nz - 1], a_send)
    for step in range(1, ny):

        @pl.when(y + step < ny)
        def _():
            wait_bytes(tsend, t_send.at[step])

    wait_bytes(pbuf.at[0 : nz - 1], p_send)
    for key in list(laps):
        arrived(key)
    for copy in laps.values():
        copy.wait_send()

    yx = my // nx

    def project(cls, xxs):
        both = jnp.concatenate([mixed[cls, h] for h in range(2 * heads)], axis=1)
        block = jnp.concatenate([w_all[pl.ds(xx * yx, yx)].reshape(yx * mz * wc, width) for xx in xxs])
        value = dot(both, block, NT)
        return [value[:, i * HDIM : (i + 1) * HDIM] for i in range(len(xxs))]

    x_copies = {}

    def hand_over(r):
        for i in range(split_n):
            part = mixed_part(class_of(*offsets[r]), i)
            group_copies[r, i].wait_recv()
            twin_copies[r, i] = send(part, part, m_send.at[r, i], m_recv.at[r, i], twin)

    done_copies, finished = [], set()

    def finish(r):
        if r in finished:
            return
        finished.add(r)
        total = sum_own[r]
        for step in x_order[:-1]:
            x_copies[r, step].wait_recv()
            total = total + x_in[r, step].astype(F32)
        total = total.astype(BF16)
        for e in range(2):
            dsend[r, e] = total[e * rows : (e + 1) * rows]
        place = fin.at[own_class * 2 + c]
        if r == 0:
            fin[own_class * 2 + c] = dsend[0, c]
            done_copies.append(send(dsend.at[0, 1 - c], place, d_send, d_recv, twin))
        else:
            for e in range(2):
                done_copies.append(send(dsend.at[r, e], place, d_send, d_recv, group_dev(*offsets[r], e)))

    for r, (dy, dz) in enumerate(offsets):
        cls = class_of(dy, dz)
        for i in range(split_n):
            twin_copies[r, i].wait_recv()
        for first in range(0, len(x_order), 2):
            part_steps = x_order[first : first + 2]
            for step, value in zip(part_steps, project(cls, [ahead(x, step, nx) for step in part_steps])):
                if step == 0:
                    sum_own[r] = value
                    continue
                x_out[r, step] = value.astype(BF16)
                x_copies[r, step] = send(
                    x_out.at[r, step], x_in.at[r, step], x_send.at[r, step], x_recv.at[r, step],
                    x_dev(ahead(x, step, nx)),
                )
        for later in range(1, len(offsets)) if r == 0 else ():
            hand_over(later)
        if r == 2:
            finish(0)
    for r in range(len(offsets)):
        finish(r)
    wait_bytes(fin.at[0 : len(done_copies)], d_recv)

    lane = lax.broadcasted_iota(jnp.int32, (rows, HDIM), 1)
    runs = HDIM // wc
    for b in range(out_ref.shape[1] // HDIM):
        value = jnp.zeros((rows, HDIM), F32)
        for k in range(runs):
            shard, e = divmod(b * runs + k, 2)
            yl, zz = divmod(shard, nz)
            pos = ((yl // gy) * mz + zz // gz) * wc
            piece = fin[((yl % gy) * gz + zz % gz) * 2 + e].astype(F32)
            shift = (k * wc - pos) % HDIM
            if shift:
                piece = pltpu.roll(piece, shift, 1)
            value = jnp.where(lane // wc == k, piece, value)
        out_ref[:, b * HDIM : (b + 1) * HDIM] = value.astype(BF16)

    for copies in (twin_copies.values(), group_copies.values(), x_copies.values()):
        for copy in copies:
            copy.wait_send()
    wait_bytes(fin.at[0 : len(done_copies)], d_send)


def local(grid, vk, vv, q, tk, tv, bounds, gate, w):
    ny, nz, nx, gy, gz = grid
    vlen, width = vk.shape
    rows = q.shape[0]
    half_w = width // 2
    heads = half_w // HDIM
    srows = half_w // nz
    wt = w.T
    wc = wt.shape[0]
    my, mz = ny // gy, nz // gz
    n = gy * gz
    assert (my // nx) * mz * wc == HDIM
    steps = max(my, mz, 2) // 2
    hbm = pl.BlockSpec(memory_space=pltpu.HBM)
    smem = pl.BlockSpec(memory_space=pltpu.SMEM)
    dma = pltpu.SemaphoreType.DMA
    slices = (nz, srows + NORM_ROWS, HDIM)
    states = (nz, srows, HDIM)
    per_head = (heads, 2 * rows, HDIM)
    return pl.pallas_call(
        functools.partial(kernel, ny, nz, nx, gy, gz),
        out_shape=jax.ShapeDtypeStruct((rows, 2 * n * HDIM), BF16),
        in_specs=[smem, smem] + [hbm] * 6,
        out_specs=pl.BlockSpec(memory_space=pltpu.VMEM),
        scratch_shapes=[
            pltpu.VMEM((my, mz, wc, width), BF16),
            pltpu.VMEM((2, vlen, half_w), BF16),
            pltpu.VMEM((vlen, half_w), BF16),
            pltpu.VMEM((2, vlen, half_w), BF16),
            pltpu.VMEM((2, rows, half_w), BF16),
            pltpu.VMEM((2, rows, half_w), BF16),
            pltpu.VMEM((2, rows, half_w), BF16),
            pltpu.VMEM((2, 8, HDIM), jnp.int32),
            pltpu.VMEM((2, vlen, half_w), BF16),
            pltpu.VMEM(per_head, BF16),
            pltpu.VMEM(states, BF16),
            pltpu.VMEM(states, BF16),
            pltpu.VMEM(states, F32),
            pltpu.VMEM((NORM_ROWS, HDIM), BF16),
            pltpu.VMEM((NORM_ROWS, HDIM), BF16),
            pltpu.VMEM((NORM_ROWS, HDIM), F32),
            pltpu.VMEM(slices, BF16),
            pltpu.VMEM(slices, BF16),
            pltpu.VMEM(slices, F32),
            pltpu.VMEM((ny, srows + NORM_ROWS, HDIM), BF16),
            pltpu.VMEM((srows + NORM_ROWS, HDIM), BF16),
            pltpu.VMEM(states, BF16),
            pltpu.VMEM(states, BF16),
            pltpu.VMEM(per_head, F32),
            pltpu.VMEM(per_head, F32),
            pltpu.VMEM(per_head, F32),
            pltpu.VMEM((n, 2 * heads, 2 * rows, HDIM), BF16),
            pltpu.VMEM((n, nx, 2 * rows, HDIM), BF16),
            pltpu.VMEM((n, nx, 2 * rows, HDIM), BF16),
            pltpu.VMEM((n, 2 * rows, HDIM), F32),
            pltpu.VMEM((n, 2, rows, HDIM), BF16),
            pltpu.VMEM((2 * n, rows, HDIM), BF16),
            dma((7,)),
            dma((4,)),
            dma,
            dma((6,)),
            dma((6,)),
            dma((2,)),
            dma((2,)),
            dma((2, 2, steps, 2)),
            dma((2, 2, steps, 2)),
            dma,
            dma,
            dma((ny,)),
            dma((ny,)),
            dma,
            dma,
            dma((n, 2)),
            dma((n, 2)),
            dma((n, 2)),
            dma((n, 2)),
            dma((n, nx)),
            dma((n, nx)),
            dma,
            dma,
        ],
        compiler_params=pltpu.CompilerParams(
            collective_id=0, has_side_effects=True, vmem_limit_bytes=60 * 1024 * 1024
        ),
    )(bounds, gate, vk, vv, q, tk, tv, wt)


def solution(mesh):
    nx = mesh.shape["head"]
    specs = (
        P("tm", "head"),
        P("tm", "head"),
        P("tm", "head"),
        P("tm", "head"),
        P("tm", "head"),
        P("tm"),
        P("head"),
        P("head", "tm"),
    )
    return jax.shard_map(
        functools.partial(local, (8, mesh.shape["tm"] // 16, nx, 2, 2)),
        mesh=mesh,
        in_specs=specs,
        out_specs=P("tm", "head"),
        check_vma=False,
    )
```
